32 devices in a mesh: clip: 16 (over z, y, core), head: 2 (over x).
Axes of the slice: x: 2, y: 2, z: 4, core: 2. Of those that a mesh axis runs over, the one named last changes fastest.
Arguments:
- tokens: bfloat16 [3, 8192, 768], P(None, 'clip'), may hold values from -6 to 6
- cotangent: bfloat16 [3, 8192, 768], P(None, 'clip'), may hold values from -6 to 6
- clip_len: int32 [3, 8, 4], replicated, may hold values from 1 to 192, 256 in all within a row
- ln_params: float32 [16, 6, 768], P('clip'), as said below
- w_self: bfloat16 [16, 3, 768, 768], P('clip', None, None, 'head'), as said below
- w_self_out: bfloat16 [16, 768, 768], P('clip', 'head'), as said below
- w_offer: bfloat16 [16, 2, 768, 768], P('clip', None, None, 'head'), as said below
- w_query: bfloat16 [16, 768, 768], P('clip', None, 'head'), as said below
- w_cross_out: bfloat16 [16, 768, 768], P('clip', 'head'), as said below
- w_up: bfloat16 [16, 768, 3072], P('clip', None, 'head'), as said below
- w_down: bfloat16 [16, 3072, 768], P('clip', 'head'), as said below
Outputs:
- layer_out: bfloat16 [3, 8192, 768], P(None, 'clip')
- grad_tokens: float32 [3, 8192, 768], P(None, 'clip')
- grad_ln_params: float32 [16, 6, 768], P('clip')
- grad_w_self: float32 [16, 3, 768, 768], P('clip', None, None, 'head')
- grad_w_self_out: float32 [16, 768, 768], P('clip', 'head')
- grad_w_offer: float32 [16, 2, 768, 768], P('clip', None, None, 'head')
- grad_w_query: float32 [16, 768, 768], P('clip', None, 'head')
- grad_w_cross_out: float32 [16, 768, 768], P('clip', 'head')
- grad_w_up: float32 [16, 768, 3072], P('clip', None, 'head')
- grad_w_down: float32 [16, 3072, 768], P('clip', 'head')
The draws below stay inside these ranges and needn't reach their ends.
Inputs may be any that keep to these rules, and one draw needn't show every extreme that they name: `clip_len`: each row (one clip set) sums to half of 512, and its largest entry is 192. `ln_params`: equal on all clip indices of one view range: 0 to 7, the next 4, the last 4. `w_self`: equal on all clip indices of one view range. `w_self_out`: equal on all clip indices of one view range. `w_offer`: equal on all clip indices of one view range. `w_query`: equal on all clip indices of one view range. `w_cross_out`: equal on all clip indices of one view range. `w_up`: equal on all clip indices of one view range. `w_down`: equal on all clip indices of one view range.
All inputs are finite; a program needn't handle non-finite values.
Results may differ from the reference program's by a relative error of at most 0.019.
Values may be sent and summed in bfloat16 or wider, within the bound.
No kernel may reach another device: no remote copies, remote signals or barrier semaphores. Data moves between devices by JAX's collectives and lax.ppermute only.
A program may use at most 256 MiB of HBM per device.

```python
import math
import jax
import jax.numpy as jnp
import numpy as np
from jax import lax

D = 768
HEADS = 12
HEAD_DIM = 64
FF = 3072
TOK_DEV = 512
MICRO = 3
CLIPS = 4
QUARTER = 4
SETS = 8
TOKENS = 8192
MOST = 192
N_CLIP = 16


def device_views():
    places = jnp.arange(4 * QUARTER)
    return jnp.where(places < 2 * QUARTER, 0, jnp.where(places < 3 * QUARTER, 1, 2))


def view_copies(key, shape, spread):
    drawn = jnp.clip(jax.random.normal(key, (3,) + shape, jnp.float32), -4.0, 4.0) * spread
    return drawn[device_views()]


def draw_ln_params(key, part):
    key = jax.random.fold_in(key, 11)
    gain_key, shift_key = jax.random.split(key)
    gains = 1.0 + 0.25 * jnp.clip(jax.random.normal(gain_key, (3, 3, 1, D), jnp.float32), -3.0, 3.0)
    shifts = 0.3 * jnp.clip(jax.random.normal(shift_key, (3, 3, 1, D), jnp.float32), -3.0, 3.0)
    table = jnp.concatenate([gains, shifts], axis=2).reshape(3, 6, D)
    return table[device_views()]


def draw_w_self(key, part):
    key = jax.random.fold_in(key, 12)
    return view_copies(key, (3, D, D), 1.0 / math.sqrt(D)).astype(jnp.bfloat16)


def draw_w_self_out(key, part):
    key = jax.random.fold_in(key, 13)
    return view_copies(key, (D, D), 4.0 / math.sqrt(D)).astype(jnp.bfloat16)


def draw_w_offer(key, part):
    key = jax.random.fold_in(key, 14)
    return view_copies(key, (2, D, D), 1.0 / math.sqrt(D)).astype(jnp.bfloat16)


def draw_w_query(key, part):
    key = jax.random.fold_in(key, 15)
    return view_copies(key, (D, D), 1.0 / math.sqrt(D)).astype(jnp.bfloat16)


def draw_w_cross_out(key, part):
    key = jax.random.fold_in(key, 16)
    return view_copies(key, (D, D), 4.0 / math.sqrt(D)).astype(jnp.bfloat16)


def draw_w_up(key, part):
    key = jax.random.fold_in(key, 17)
    return view_copies(key, (D, FF), 1.0 / math.sqrt(D)).astype(jnp.bfloat16)


def draw_w_down(key, part):
    key = jax.random.fold_in(key, 18)
    return view_copies(key, (FF, D), math.sqrt(2.0 / FF)).astype(jnp.bfloat16)


def shard_levels(key, extent, cuts, least, largest):
    def one(position, parts):
        draws = jax.random.uniform(jax.random.fold_in(jax.random.fold_in(key, 6), position), (parts,), jnp.float32, least / len(cuts), largest / len(cuts))
        return jnp.repeat(jnp.exp(draws), extent[position] // parts).reshape((-1,) + (1,) * (len(extent) - position - 1))

    gain = one(*cuts[0])
    for cut in cuts[1:]:
        gain = gain * one(*cut)
    return gain


def length_profile(number_of, total, most, skew):
    loads = [(1 << 20) // math.isqrt(standing ** skew) + 1 for standing in range(2, number_of + 1)]
    surplus, counts = total - most - (number_of - 1), [1] * (number_of - 1)
    while surplus > 0:
        movable = [i for i in range(number_of - 1) if counts[i] < most]
        mass, budget = sum([loads[i] for i in movable]), surplus
        for i in movable:
            extra = min(most - counts[i], max(1, budget * loads[i] // mass), surplus)
            counts[i] = counts[i] + extra
            surplus = surplus - extra
    return np.array([most] + counts)


def uneven_parts(rng, amount, total, limit, slope):
    if amount == 2:
        one = jax.random.randint(rng, (), max(1, total - limit), min(limit, total - 1) + 1)
        return jnp.stack([one, total - one])
    tallies = jnp.asarray(length_profile(amount, total, limit, slope), jnp.int32)
    pairs = (amount - 1) // 2
    source_of, taker = tallies[1:1 + 2 * pairs:2], tallies[2:2 + 2 * pairs:2]
    margin = jnp.minimum(source_of - 1, limit - taker)
    shifted = jax.random.randint(jax.random.fold_in(rng, 1), (pairs,), 0, 1 << 20) % (margin + 1)
    tallies = tallies.at[1:1 + 2 * pairs:2].set(source_of - shifted).at[2:2 + 2 * pairs:2].set(taker + shifted)
    return tallies[jax.random.permutation(jax.random.fold_in(rng, 2), amount)]


def noise(own_key, extent, deviation, limit, pieces=(), held_as=jnp.bfloat16):
    entries = jax.random.normal(own_key, extent, jnp.float32) * deviation
    if len(pieces) > 0:
        entries = shard_levels(own_key, extent, pieces, -0.22, 0.18) * entries
    return jnp.clip(entries, min=-limit, max=limit).astype(held_as)


def setup_inputs(seed: int = 0) -> dict:
    seeds = jax.random.split(jax.random.key(seed), 12)
    tokens = noise(seeds[0], (MICRO, TOKENS, D), 1.0, 6.0, ((1, 16),))
    cotangent = noise(seeds[1], (MICRO, TOKENS, D), 1.0, 6.0, ((1, 16),))
    clip_len = jax.vmap(lambda own: uneven_parts(own, CLIPS, TOK_DEV // 2, MOST, 1))(jax.random.split(seeds[2], MICRO * SETS)).reshape((MICRO, SETS, CLIPS)).astype(jnp.int32)
    ln_params = draw_ln_params(jax.random.fold_in(seeds[11], 71), 0)
    w_self = draw_w_self(jax.random.fold_in(seeds[11], 71), 0)
    w_self_out = draw_w_self_out(jax.random.fold_in(seeds[11], 71), 0)
    w_offer = draw_w_offer(jax.random.fold_in(seeds[11], 71), 0)
    w_query = draw_w_query(jax.random.fold_in(seeds[11], 71), 0)
    w_cross_out = draw_w_cross_out(jax.random.fold_in(seeds[11], 71), 0)
    w_up = draw_w_up(jax.random.fold_in(seeds[11], 71), 0)
    w_down = draw_w_down(jax.random.fold_in(seeds[11], 71), 0)
    return dict(tokens=tokens, cotangent=cotangent, clip_len=clip_len, ln_params=ln_params, w_self=w_self, w_self_out=w_self_out, w_offer=w_offer, w_query=w_query, w_cross_out=w_cross_out, w_up=w_up, w_down=w_down)


EPSILON = 1e-06
SCORE_SCALE = 0.125
MASKED = -1e+30

@jax.custom_vjp
def low(v):
    return lax.optimization_barrier(v.astype(jnp.bfloat16)).astype(jnp.float32)

@jax.custom_vjp
def low_back(v):
    return v

def low_keep(v):
    return (low(v), None)

def low_pass(kept, grad):
    return (grad,)

def back_keep(v):
    return (v, None)

def back_low(kept, grad):
    return (low(grad),)
low.defvjp(low_keep, low_pass)
low_back.defvjp(back_keep, back_low)

def matmul(left, right):
    return jnp.dot(left, right, precision=lax.Precision.HIGHEST)

def normalize(inputs, norm_gain, norm_shift):
    row_mean = lax.optimization_barrier(jnp.mean(inputs, axis=-1, keepdims=True))
    centered = inputs - row_mean
    variance = lax.optimization_barrier(jnp.mean(centered * centered, axis=-1, keepdims=True))
    return centered * lax.rsqrt(variance + EPSILON) * norm_gain + norm_shift

def clip_ids(lengths, row_count):
    ends = jnp.cumsum(lengths)
    places = jnp.arange(row_count, dtype=jnp.int32)
    return lax.optimization_barrier(jnp.sum((places[:, None] >= ends[None, :]).astype(jnp.int32), axis=1))

def attention(query, key_rows, value_rows, query_ids, key_ids):
    row_count = query.shape[0]
    query_heads = query.reshape(row_count, HEADS, HEAD_DIM)
    key_heads = key_rows.reshape(key_rows.shape[0], HEADS, HEAD_DIM)
    value_heads = value_rows.reshape(value_rows.shape[0], HEADS, HEAD_DIM)
    scores = low_back(jnp.einsum('qhd,khd->hqk', query_heads, key_heads, precision=lax.Precision.HIGHEST) * SCORE_SCALE)
    allowed = (query_ids[:, None] == key_ids[None, :])[None]
    scores = jnp.where(allowed, scores, MASKED)
    row_max = lax.optimization_barrier(jnp.max(scores, axis=-1, keepdims=True))
    exponent = jnp.exp(scores - row_max)
    attn_probs = low(exponent / lax.optimization_barrier(jnp.sum(exponent, axis=-1, keepdims=True)))
    mixture = jnp.einsum('hqk,khd->qhd', attn_probs, value_heads, precision=lax.Precision.HIGHEST)
    return mixture.reshape(row_count, HEADS * HEAD_DIM)

def self_block(rows_in, norm_rows, weights_in, weights_out, clip_of_row):
    normed = low(normalize(rows_in, norm_rows[0], norm_rows[1]))
    projected = low(low_back(jnp.einsum('rd,cde->cre', normed, weights_in, precision=lax.Precision.HIGHEST)))
    mixture = low(low_back(attention(projected[0], projected[1], projected[2], clip_of_row, clip_of_row)))
    return rows_in + low_back(matmul(mixture, weights_out))

def offer(joined, weights_offer):
    return low(low_back(jnp.einsum('rd,cde->cre', joined, weights_offer, precision=lax.Precision.HIGHEST)))

def cross(joined, offered, weights_query, weights_out, query_ids, key_ids):
    query = low(low_back(matmul(joined, weights_query)))
    mixture = low(low_back(attention(query, offered[0], offered[1], query_ids, key_ids)))
    return low_back(matmul(mixture, weights_out))

def finish(second, norm_rows, weights_up, weights_down):
    mlp_in = low(normalize(second, norm_rows[4], norm_rows[5]))
    mlp_pre = low_back(matmul(mlp_in, weights_up))
    activated = low(jax.nn.gelu(mlp_pre, approximate=False))
    return second + low_back(matmul(activated, weights_down))

def group_forward(first_rows, second_rows, third_rows, params, big_ids, small_ids):
    norm_table, self_in, self_out, offer_in, query_in, cross_out, up_in, down_in = params
    hidden_zero = self_block(first_rows, norm_table[0], self_in[0], self_out[0], big_ids)
    hidden_one = self_block(second_rows, norm_table[1], self_in[1], self_out[1], small_ids)
    hidden_two = self_block(third_rows, norm_table[2], self_in[2], self_out[2], small_ids)
    joined_zero = low(normalize(hidden_zero, norm_table[0][2], norm_table[0][3]))
    joined_one = low(normalize(hidden_one, norm_table[1][2], norm_table[1][3]))
    joined_two = low(normalize(hidden_two, norm_table[2][2], norm_table[2][3]))
    offer_zero = offer(joined_zero, offer_in[0])
    offer_one = offer(joined_one, offer_in[1])
    second_one = hidden_one + cross(joined_one, offer_zero, query_in[1], cross_out[1], small_ids, big_ids)
    second_two = hidden_two + cross(joined_two, offer_one, query_in[2], cross_out[2], small_ids, small_ids)
    return (finish(hidden_zero, norm_table[0], up_in[0], down_in[0]), finish(second_one, norm_table[1], up_in[1], down_in[1]), finish(second_two, norm_table[2], up_in[2], down_in[2]))

def reference(tokens, cotangent, clip_len, ln_params, w_self, w_self_out, w_offer, w_query, w_cross_out, w_up, w_down):
    places = jnp.arange(N_CLIP)
    device_view = jnp.where(places < 2 * QUARTER, 0, jnp.where(places < 3 * QUARTER, 1, 2)).astype(jnp.int32)
    firsts = jnp.array([0, 2 * QUARTER, 3 * QUARTER], dtype=jnp.int32)
    weight_views = tuple((weight[firsts].astype(jnp.float32) for weight in (ln_params, w_self, w_self_out, w_offer, w_query, w_cross_out, w_up, w_down)))
    rows_in = tokens.astype(jnp.float32).reshape(MICRO, 4, QUARTER, TOK_DEV, D).transpose(0, 2, 1, 3, 4).reshape(MICRO * QUARTER, 4, TOK_DEV, D)
    cot_in = cotangent.astype(jnp.float32).reshape(MICRO, 4, QUARTER, TOK_DEV, D).transpose(0, 2, 1, 3, 4).reshape(MICRO * QUARTER, 4, TOK_DEV, D)
    set_pairs = clip_len.reshape(MICRO, 2, QUARTER, CLIPS).transpose(0, 2, 1, 3).reshape(MICRO * QUARTER, 2, CLIPS)

    def visit(running, scan_item):
        token_block, cot_block, lengths = scan_item
        big_ids = clip_ids(jnp.concatenate([2 * lengths[0], 2 * lengths[1]]), 2 * TOK_DEV)
        small_ids = clip_ids(jnp.concatenate([lengths[0], lengths[1]]), TOK_DEV)

        def forward(first_rows, second_rows, third_rows, params):
            return group_forward(first_rows, second_rows, third_rows, params, big_ids, small_ids)
        first_rows = jnp.concatenate([token_block[0], token_block[1]])
        group_out, pullback = jax.vjp(forward, first_rows, token_block[2], token_block[3], weight_views)
        cot_first = jnp.concatenate([cot_block[0], cot_block[1]])
        grad_first, grad_second, grad_third, grad_params = pullback((cot_first, cot_block[2], cot_block[3]))
        running = tuple((left + right for left, right in zip(running, grad_params)))
        layer_rows = jnp.stack([group_out[0][:TOK_DEV], group_out[0][TOK_DEV:], group_out[1], group_out[2]]).astype(jnp.bfloat16)
        grad_rows = jnp.stack([grad_first[:TOK_DEV], grad_first[TOK_DEV:], grad_second, grad_third])
        return (running, (layer_rows, grad_rows))
    zero_grads = tuple((jnp.zeros(weight.shape, jnp.float32) for weight in weight_views))
    running, (layer_rows, grad_rows) = lax.scan(visit, zero_grads, (rows_in, cot_in, set_pairs))

    def arrange(stacked):
        return stacked.reshape(MICRO, QUARTER, 4, TOK_DEV, D).transpose(0, 2, 1, 3, 4).reshape(MICRO, 4 * QUARTER * TOK_DEV, D)
    return (arrange(layer_rows), arrange(grad_rows), running[0][device_view], running[1][device_view], running[2][device_view], running[3][device_view], running[4][device_view], running[5][device_view], running[6][device_view], running[7][device_view])
```

```python
import jax
import jax.numpy as jnp
from jax import lax
from jax.experimental import pallas as pl
from jax.experimental.pallas import tpu as pltpu
from jax.sharding import PartitionSpec as P


HEAD_DIM = 64
EPSILON = 1e-06
SCORE_SCALE = 0.125
MASKED = -1e30
BF16 = jnp.bfloat16
F32 = jnp.float32
VMEM_BYTES = 24 * 1024 * 1024


def over_head(value):
    return lax.ppermute(value, "head", [(0, 1), (1, 0)])


def over_bit(value, bit, count=None):
    count = lax.axis_size("clip") if count is None else count
    return lax.ppermute(value, "clip", [(i, i ^ (1 << bit)) for i in range(count)])


def other_core(value):
    return over_bit(value, 0)


def in_core_order(core, mine, theirs, axis):
    first = jnp.where(core == 0, mine, theirs)
    second = jnp.where(core == 0, theirs, mine)
    return jnp.concatenate([first, second], axis=axis)


def core_piece(value, piece, axis):
    size = value.shape[axis] // 2
    return lax.dynamic_slice_in_dim(value, piece * size, size, axis)


def norm_stats(rows):
    mean = jnp.mean(rows, axis=-1, keepdims=True)
    centered = rows - mean
    variance = jnp.mean(centered * centered, axis=-1, keepdims=True)
    inverse = lax.rsqrt(variance + EPSILON)
    return centered * inverse, inverse


def norm_back(grad, normal, inverse, gain):
    scaled = grad * gain
    mean = jnp.mean(scaled, axis=-1, keepdims=True)
    along = jnp.mean(scaled * normal, axis=-1, keepdims=True)
    grad_rows = (scaled - mean - normal * along) * inverse
    return grad_rows, jnp.sum(grad * normal, axis=0), jnp.sum(grad, axis=0)


def attention_blocks(full, query_rows, key_rows):
    half = key_rows // 2
    if full:
        return [
            (slice(r, r + half), slice(0, key_rows), slice(r, r + half), slice(0, key_rows))
            for r in range(0, query_rows, half)
        ]
    blocks = []
    for s in range(2):
        part = slice(s * half, (s + 1) * half)
        if query_rows == key_rows:
            blocks.append((part, part, part, slice(0, half)))
        else:
            blocks.append((part, part, slice(0, half), part))
    return blocks


def dot_nt(left, right):
    return lax.dot_general(left, right, (((1,), (1,)), ((), ())), preferred_element_type=F32)


def dot_tn(left, right):
    return lax.dot_general(left, right, (((0,), (0,)), ((), ())), preferred_element_type=F32)


def dot_nn(left, right):
    return jnp.dot(left, right, preferred_element_type=F32)


def attend_kernel(query_rows, flag_ref, q_ref, k_ref, v_ref, idq_ref, idk_ref, mix_ref, p_ref, bias_ref):
    key_rows = k_ref.shape[0]
    first_head = lax.broadcasted_iota(jnp.int32, (1, 2 * HEAD_DIM), 1) < HEAD_DIM

    def run(full):
        blocks = attention_blocks(full, query_rows, key_rows)

        @pl.when(pl.program_id(0) == 0)
        def _():
            for rows, keys, p_rows, p_cols in blocks:
                same = idq_ref[rows, :] == idk_ref[:, keys]
                bias_ref[p_rows, p_cols] = jnp.where(same, 0.0, MASKED)

        for rows, keys, p_rows, p_cols in blocks:
            query = q_ref[rows, :] * jnp.asarray(SCORE_SCALE, BF16)
            mixes = []
            for h in range(2):
                wanted = first_head if h == 0 else jnp.logical_not(first_head)
                own = jnp.where(wanted, query, jnp.zeros_like(query))
                scores = dot_nt(own, k_ref[keys, :]) + bias_ref[p_rows, p_cols]
                top = jnp.max(scores, axis=-1, keepdims=True)
                exponent = jnp.exp(scores - top)
                total = jnp.sum(exponent, axis=-1, keepdims=True)
                probs = (exponent * (1.0 / total)).astype(BF16)
                p_ref[h, p_rows, p_cols] = probs
                mixes.append(dot_nn(probs, v_ref[keys, :]))
            mix_ref[rows, :] = jnp.where(first_head, mixes[0], mixes[1]).astype(BF16)

    @pl.when(flag_ref[0] != 0)
    def _():
        run(True)
        if query_rows < key_rows:
            mix_ref[query_rows:, :] = jnp.zeros((key_rows - query_rows, 2 * HEAD_DIM), BF16)

    @pl.when(flag_ref[0] == 0)
    def _():
        run(False)


def attend_back_kernel(query_rows, flag_ref, q_ref, k_ref, v_ref, p_ref, grad_ref, dq_ref, dk_ref, dv_ref):
    key_rows = k_ref.shape[0]
    first_head = lax.broadcasted_iota(jnp.int32, (1, 2 * HEAD_DIM), 1) < HEAD_DIM

    def run(full):
        blocks = attention_blocks(full, query_rows, key_rows)
        sums = {}
        for rows, keys, p_rows, p_cols in blocks:
            query = q_ref[rows, :]
            grad = grad_ref[rows, :]
            dq, dk, dv = [], [], []
            for h in range(2):
                wanted = first_head if h == 0 else jnp.logical_not(first_head)
                own = jnp.where(wanted, grad, jnp.zeros_like(grad))
                probs = p_ref[h, p_rows, p_cols]
                wide_probs = probs.astype(F32)
                grad_probs = dot_nt(own, v_ref[keys, :])
                delta = jnp.sum(wide_probs * grad_probs, axis=-1, keepdims=True)
                grad_scores = (wide_probs * (grad_probs - delta)).astype(BF16)
                dq.append(dot_nn(grad_scores, k_ref[keys, :]))
                dk.append(dot_tn(grad_scores, query))
                dv.append(dot_tn(probs, grad))
            dq_ref[rows, :] = (jnp.where(first_head, dq[0], dq[1]) * SCORE_SCALE).astype(BF16)
            both = (jnp.where(first_head, dk[0], dk[1]), jnp.where(first_head, dv[0], dv[1]))
            at = (keys.start, keys.stop)
            sums[at] = (sums[at][0] + both[0], sums[at][1] + both[1]) if at in sums else both
        for (start, stop), (dk, dv) in sums.items():
            dk_ref[start:stop, :] = (dk * SCORE_SCALE).astype(BF16)
            dv_ref[start:stop, :] = dv.astype(BF16)

    @pl.when(flag_ref[0] != 0)
    def _():
        run(True)
        if query_rows < key_rows:
            dq_ref[query_rows:, :] = jnp.zeros((key_rows - query_rows, 2 * HEAD_DIM), BF16)

    @pl.when(flag_ref[0] == 0)
    def _():
        run(False)


def pair_spec(array, rows, lead=None):
    if array.ndim == 3:
        return pl.BlockSpec((None, rows, 2 * HEAD_DIM), lambda j, flag, lead=lead: (lead, 0, j))
    return pl.BlockSpec((rows, 2 * HEAD_DIM), lambda j, flag: (0, j))


def attention_cost(heads, query_rows, key_rows, matmuls):
    return pl.CostEstimate(
        flops=2 * heads * query_rows * key_rows * 256 * matmuls,
        bytes_accessed=2 * heads * query_rows * key_rows + 8 * heads * key_rows * HEAD_DIM,
        transcendentals=heads * query_rows * key_rows,
    )


def attend(full, query, keys, values, ids, query_rows, heads):
    rows = 512
    id_query, id_keys = ids
    pairs = heads // 2
    return pl.pallas_call(
        lambda *refs: attend_kernel(query_rows, *refs),
        grid_spec=pltpu.PrefetchScalarGridSpec(
            num_scalar_prefetch=1,
            grid=(pairs,),
            in_specs=[pair_spec(a, rows, lead) for a, lead in (query, keys, values)]
            + [
                pl.BlockSpec((rows, 1), lambda j, flag: (0, 0)),
                pl.BlockSpec((1, rows), lambda j, flag: (0, 0)),
            ],
            out_specs=[
                pl.BlockSpec((rows, 2 * HEAD_DIM), lambda j, flag: (0, j)),
                pl.BlockSpec((2, query_rows, rows), lambda j, flag: (j, 0, 0)),
            ],
            scratch_shapes=[pltpu.VMEM((query_rows, rows), F32)],
        ),
        out_shape=[
            jax.ShapeDtypeStruct((rows, heads * HEAD_DIM), BF16),
            jax.ShapeDtypeStruct((heads, query_rows, rows), BF16),
        ],
        compiler_params=pltpu.CompilerParams(vmem_limit_bytes=VMEM_BYTES),
        cost_estimate=attention_cost(heads, query_rows, rows, 2),
        name="attend",
    )(full, query[0], keys[0], values[0], id_query, id_keys)


def attend_back(full, query, keys, values, probs, grad, query_rows, heads):
    rows = 512
    pairs = heads // 2
    out = jax.ShapeDtypeStruct((rows, heads * HEAD_DIM), BF16)
    out_spec = pl.BlockSpec((rows, 2 * HEAD_DIM), lambda j, flag: (0, j))
    return pl.pallas_call(
        lambda *refs: attend_back_kernel(query_rows, *refs),
        grid_spec=pltpu.PrefetchScalarGridSpec(
            num_scalar_prefetch=1,
            grid=(pairs,),
            in_specs=[pair_spec(a, rows, lead) for a, lead in (query, keys, values)]
            + [
                pl.BlockSpec((2, query_rows, rows), lambda j, flag: (j, 0, 0)),
                pair_spec(grad, rows),
            ],
            out_specs=[out_spec] * 3,
        ),
        out_shape=[out] * 3,
        compiler_params=pltpu.CompilerParams(vmem_limit_bytes=VMEM_BYTES),
        cost_estimate=attention_cost(heads, query_rows, rows, 4),
        name="attend_back",
    )(full, query[0], keys[0], values[0], probs, grad)


def to_slots(rows, exchange, core):
    received = other_core(core_piece(rows, 1 - core, 2))
    width = rows.shape[2] // 2
    left, right = rows[..., :width], rows[..., width:]
    first = jnp.where(jnp.logical_and(exchange, core == 1), received, left)
    second = jnp.where(jnp.logical_and(exchange, core == 0), received, right)
    return jnp.concatenate([first, second], axis=1)


def from_slots(slots, exchange, core):
    received = other_core(core_piece(slots, 1 - core, 1))
    height = slots.shape[1] // 2
    top, bottom = slots[:, :height], slots[:, height:]
    first = jnp.where(jnp.logical_and(exchange, core == 1), received, top)
    second = jnp.where(jnp.logical_and(exchange, core == 0), received, bottom)
    return jnp.concatenate([first, second], axis=2)


def clip_ids(lengths, row_count):
    ends = jnp.cumsum(lengths)
    places = jnp.arange(row_count, dtype=jnp.int32)
    return jnp.sum((places[:, None] >= ends[None, :]).astype(jnp.int32), axis=1)


def row_of(table, index):
    return lax.dynamic_index_in_dim(table, index, 0, keepdims=False)


def local(
    tokens,
    cotangent,
    clip_len,
    ln_params,
    w_self,
    w_self_out,
    w_offer,
    w_query,
    w_cross_out,
    w_up,
    w_down,
):
    index = lax.axis_index("clip")
    across = lax.axis_index("head")
    count = lax.axis_size("clip")
    quarter = count // 4
    view = jnp.where(index < 2 * quarter, 0, jnp.where(index < 3 * quarter, 1, 2))
    member = index % quarter
    core = index % 2
    own_micro2 = core == across
    is_big = view == 0
    is_mid = view == 1
    gains = ln_params[0]
    row_count = tokens.shape[1]
    half_rows = row_count // 2
    part_a = row_count

    def my_rows(array):
        first = row_of(array, across)
        kept = core_piece(array[2], core, 0)
        received = other_core(core_piece(array[2], 1 - core, 0))
        return jnp.concatenate([first, jnp.where(own_micro2, kept, received)], axis=0)

    def fetch(pieces):
        mine = over_head(pieces)
        return mine, other_core(mine)

    def assemble(mine, theirs, axis):
        return in_core_order(core, mine, theirs, axis)

    self_mine, self_theirs = fetch(core_piece(w_self[0], core, 1))
    bundle = [
        core_piece(w_self_out[0], core, 1),
        core_piece(w_query[0], core, 0),
        core_piece(w_offer[0, 0], core, 0),
        core_piece(w_offer[0, 1], core, 0),
        core_piece(w_cross_out[0], core, 1),
    ]
    mid_mine, mid_theirs = fetch(jnp.stack(bundle))
    up_mine, up_theirs = fetch(core_piece(w_up[0], core, 0))
    down_mine, down_theirs = fetch(core_piece(w_down[0], core, 0))

    full_self = jnp.concatenate([w_self[0], assemble(self_mine, self_theirs, 1)], axis=2)
    full_self_out = jnp.concatenate([w_self_out[0], assemble(mid_mine[0], mid_theirs[0], 1)], axis=0)
    full_query = jnp.concatenate([w_query[0], assemble(mid_mine[1], mid_theirs[1], 0)], axis=1)
    full_offer = jnp.concatenate([w_offer[0], assemble(mid_mine[2:4], mid_theirs[2:4], 1)], axis=2)
    full_cross_out = jnp.concatenate([w_cross_out[0], assemble(mid_mine[4], mid_theirs[4], 1)], axis=0)
    full_up = jnp.concatenate([w_up[0], assemble(up_mine, up_theirs, 0)], axis=1)
    full_down = jnp.concatenate([w_down[0], assemble(down_mine, down_theirs, 0)], axis=0)

    even_index = index - core + across
    even_member = even_index % quarter
    lens_a, lens_b = row_of(clip_len, across), clip_len[2]
    big_a = row_of(lens_a, jnp.minimum(index, 2 * quarter - 1))
    big_b = row_of(lens_b, jnp.minimum(even_index, 2 * quarter - 1))
    set_a = [clip_ids(row_of(lens_a, member + s * quarter), half_rows) for s in range(2)]
    set_b = clip_ids(row_of(lens_b, even_member + core * quarter), half_rows)
    keys_a = jnp.where(is_big, clip_ids(2 * big_a, row_count), jnp.concatenate(set_a))
    keys_b = jnp.where(is_big, clip_ids(2 * big_b, row_count), jnp.concatenate([set_b, set_b]))
    asks_a = jnp.where(is_big, jnp.concatenate([clip_ids(big_a, half_rows)] * 2), keys_a)
    asks_b = jnp.where(is_big, jnp.concatenate([clip_ids(big_b, half_rows)] * 2), keys_b)
    self_ids_a = (keys_a[:, None], keys_a[None, :])
    self_ids_b = (keys_b[:, None], keys_b[None, :])
    cross_ids_a = (asks_a[:, None], keys_a[None, :])
    cross_ids_b = (asks_b[:, None], keys_b[None, :])
    full_flag = is_big.astype(jnp.int32)[None]

    near = [(i, i - quarter) for i in range(2 * quarter, count)]
    far = [(i, i - 2 * quarter) for i in range(2 * quarter, 3 * quarter)]
    far += [(i, i - quarter) for i in range(3 * quarter, count)]

    def to_server(rows_a, slots_b):
        whole = jnp.concatenate([rows_a, slots_b], axis=1)
        second = lax.ppermute(whole[half_rows:], "clip", near)
        first = lax.ppermute(whole[:half_rows], "clip", far)
        second_plane = jnp.logical_and(is_big, index >= quarter)
        return jnp.concatenate([jnp.where(second_plane, second, first), second], axis=0)

    def to_reader(rows_a, slots_b):
        whole = jnp.concatenate([rows_a, slots_b], axis=1)
        top = whole[:half_rows]
        second = lax.ppermute(
            jnp.where(is_big, top, whole[half_rows:]), "clip", [(b, a) for a, b in near]
        )
        first = lax.ppermute(top, "clip", [(b, a) for a, b in far])
        both = jnp.concatenate([first, second], axis=0)
        width = rows_a.shape[1]
        return both[:, :width], both[:, width:]

    inputs = my_rows(tokens).astype(F32)
    grad_out_b = my_rows(cotangent)
    normal1, inverse1 = norm_stats(inputs)
    a1 = (normal1 * gains[0] + gains[1]).astype(BF16)
    qkv = jnp.einsum("rd,cde->cre", a1, full_self, preferred_element_type=F32).astype(BF16)
    qkv_b = to_slots(qkv[:, part_a:], is_big, core)
    self_a = [(qkv, 0), (qkv, 1), (qkv, 2)]
    self_b = [(qkv_b, 0), (qkv_b, 1), (qkv_b, 2)]
    heads = qkv.shape[2] // HEAD_DIM
    self_mix_a, self_p_a = attend(full_flag, *self_a, self_ids_a, row_count, heads)
    self_mix_b, self_p_b = attend(full_flag, *self_b, self_ids_b, row_count, heads // 2)
    self_mix = jnp.concatenate([self_mix_a, from_slots(self_mix_b[None], is_big, core)[0]], axis=0)
    hidden = inputs + dot_nn(self_mix, full_self_out)
    normal2, inverse2 = norm_stats(hidden)
    joined = (normal2 * gains[2] + gains[3]).astype(BF16)

    cross_q = dot_nn(joined, full_query).astype(BF16)
    cross_q_b = to_slots(cross_q[None, part_a:], is_mid, core)[0]
    asked = to_server(cross_q[:part_a], cross_q_b)
    offer_kv = jnp.einsum("rd,cde->cre", joined, full_offer, preferred_element_type=F32).astype(BF16)
    offer_b = to_slots(offer_kv[:, part_a:], is_big, core)
    wide = heads * HEAD_DIM
    asked_a, asked_b = asked[:, :wide], asked[:, wide:]
    cross_a = [(asked_a, None), (offer_kv, 0), (offer_kv, 1)]
    cross_b = [(asked_b, None), (offer_b, 0), (offer_b, 1)]
    served_a, cross_p_a = attend(full_flag, *cross_a, cross_ids_a, half_rows, heads)
    served_b, cross_p_b = attend(full_flag, *cross_b, cross_ids_b, half_rows, heads // 2)
    cross_mix_a, cross_mix_b = to_reader(served_a, served_b)
    cross_mix = jnp.concatenate([cross_mix_a, from_slots(cross_mix_b[None], is_mid, core)[0]], axis=0)
    second = hidden + dot_nn(cross_mix, full_cross_out)

    normal3, inverse3 = norm_stats(second)
    mlp_in = (normal3 * gains[4] + gains[5]).astype(BF16)
    mlp_pre = dot_nn(mlp_in, full_up)
    spread = lax.erf(mlp_pre * 0.7071067811865476) * 0.5 + 0.5
    density = jnp.exp(mlp_pre * mlp_pre * -0.5) * 0.3989422804014327
    activated = (mlp_pre * spread).astype(BF16)
    slope = spread + mlp_pre * density
    result = (second + dot_nn(activated, full_down)).astype(BF16)
    grad_up = (dot_nt(grad_out_b, full_down) * slope).astype(BF16)
    grad_mlp_in = dot_nt(grad_up, full_up)
    back3, gain3, shift3 = norm_back(grad_mlp_in, normal3, inverse3, gains[4])
    grad_second = grad_out_b.astype(F32) + back3
    grad_second_b = grad_second.astype(BF16)

    grad_cross_mix = dot_nt(grad_second_b, full_cross_out).astype(BF16)
    grad_cross_b = to_slots(grad_cross_mix[None, part_a:], is_mid, core)[0]
    grad_asked = to_server(grad_cross_mix[:part_a], grad_cross_b)
    g_down = dot_tn(activated, grad_out_b).astype(BF16)
    g_up = dot_tn(mlp_in, grad_up).astype(BF16)
    g_cross_out = dot_tn(cross_mix, grad_second_b).astype(BF16)
    dq_a, dk_a, dv_a = attend_back(
        full_flag, *cross_a, cross_p_a, grad_asked[:, :wide], half_rows, heads
    )
    dq_b, dk_b, dv_b = attend_back(
        full_flag, *cross_b, cross_p_b, grad_asked[:, wide:], half_rows, heads // 2
    )
    grad_q_a, grad_q_b = to_reader(dq_a, dq_b)
    grad_offer_b = from_slots(jnp.stack([dk_b, dv_b]), is_big, core)
    grad_offer = jnp.concatenate([jnp.stack([dk_a, dv_a]), grad_offer_b], axis=1)
    grad_q = jnp.concatenate([grad_q_a, from_slots(grad_q_b[None], is_mid, core)[0]], axis=0)
    g_offer = jnp.einsum("rd,cre->cde", joined, grad_offer, preferred_element_type=F32).astype(BF16)
    g_query = dot_tn(joined, grad_q).astype(BF16)
    grad_joined = dot_nt(grad_q, full_query) + jnp.einsum(
        "cre,cde->rd", grad_offer, full_offer, preferred_element_type=F32
    )
    back2, gain2, shift2 = norm_back(grad_joined, normal2, inverse2, gains[2])
    grad_hidden = grad_second + back2
    grad_hidden_b = grad_hidden.astype(BF16)

    grad_self_mix = dot_nt(grad_hidden_b, full_self_out).astype(BF16)
    g_self_out = dot_tn(self_mix, grad_hidden_b).astype(BF16)
    grad_mix_b = to_slots(grad_self_mix[None, part_a:], is_big, core)[0]
    dqkv_a = attend_back(
        full_flag, *self_a, self_p_a, grad_self_mix[:part_a], row_count, heads
    )
    dqkv_b = attend_back(full_flag, *self_b, self_p_b, grad_mix_b, row_count, heads // 2)
    grad_qkv_b = from_slots(jnp.stack(dqkv_b), is_big, core)
    grad_qkv = jnp.concatenate([jnp.stack(dqkv_a), grad_qkv_b], axis=1)
    g_self = jnp.einsum("rd,cre->cde", a1, grad_qkv, preferred_element_type=F32).astype(BF16)
    grad_a1 = jnp.einsum("cre,cde->rd", grad_qkv, full_self, preferred_element_type=F32)
    back1, gain1, shift1 = norm_back(grad_a1, normal1, inverse1, gains[0])
    grad_rows = (grad_hidden + back1).astype(BF16)

    def all_rows(mine):
        theirs = over_head(mine)
        a_mine, b_mine = mine[:part_a], mine[part_a:]
        a_theirs, b_theirs = theirs[:part_a], theirs[part_a:]
        kept = jnp.where(own_micro2, b_mine, b_theirs)
        received = other_core(jnp.where(own_micro2, b_theirs, b_mine))
        micro2 = in_core_order(core, kept, received, 0)
        micro0 = jnp.where(across == 0, a_mine, a_theirs)
        micro1 = jnp.where(across == 0, a_theirs, a_mine)
        return jnp.stack([micro0, micro1, micro2])

    levels = (2 * quarter).bit_length() - 1

    def view_sum(part):
        for bit in range(1, levels):
            members = 2 * quarter if bit == levels - 1 else None
            part = part + over_bit(part.astype(BF16), bit, members).astype(F32)
        return part

    def by_core(grad, axis):
        return core_piece(grad, core, axis).astype(F32) + other_core(
            core_piece(grad, 1 - core, axis)
        ).astype(F32)

    def reduce_pieces(mine, other):
        total = view_sum(mine + over_head(other.astype(BF16)).astype(F32))
        return total, other_core(total.astype(BF16)).astype(F32)

    width = w_query.shape[2]
    hidden_width = w_up.shape[2]
    down = by_core(g_down.reshape(2, hidden_width, -1), 1)
    down_sum = reduce_pieces(down[0], down[1])
    up = by_core(g_up, 0)
    up_sum = reduce_pieces(up[:, :hidden_width], up[:, hidden_width:])
    cross_out = by_core(g_cross_out, 1)
    query = by_core(g_query, 0)
    offer = by_core(g_offer, 1)
    cross_sum = reduce_pieces(
        jnp.concatenate([cross_out[None, :width], query[None, :, :width], offer[..., :width]]),
        jnp.concatenate([cross_out[None, width:], query[None, :, width:], offer[..., width:]]),
    )
    self_out = by_core(g_self_out, 1)
    self_in = by_core(g_self, 1)
    self_sum = reduce_pieces(
        jnp.concatenate([self_out[None, :width], self_in[..., :width]]),
        jnp.concatenate([self_out[None, width:], self_in[..., width:]]),
    )

    norms = jnp.stack([gain1, shift1, gain2, shift2, gain3, shift3])
    norms = norms + other_core(norms)
    for bit in range(1, levels):
        norms = norms + over_bit(norms, bit, 2 * quarter if bit == levels - 1 else None)
    norms = norms + over_head(norms)

    def whole(sums, axis, pick=slice(None)):
        return in_core_order(core, sums[0][pick], sums[1][pick], axis)

    return (
        all_rows(result),
        all_rows(grad_rows).astype(F32),
        norms[None],
        whole(self_sum, 1, slice(1, 4))[None],
        whole(self_sum, 1, 0)[None],
        whole(cross_sum, 1, slice(2, 4))[None],
        whole(cross_sum, 0, 1)[None],
        whole(cross_sum, 1, 0)[None],
        whole(up_sum, 0)[None],
        whole(down_sum, 0)[None],
    )


def solution(mesh):
    return jax.shard_map(
        local,
        mesh=mesh,
        in_specs=(
            P(None, "clip", None),
            P(None, "clip", None),
            P(),
            P("clip", None, None),
            P("clip", None, None, "head"),
            P("clip", "head", None),
            P("clip", None, None, "head"),
            P("clip", None, "head"),
            P("clip", "head", None),
            P("clip", None, "head"),
            P("clip", "head", None),
        ),
        out_specs=(
            P(None, "clip", None),
            P(None, "clip", None),
            P("clip", None, None),
            P("clip", None, None, "head"),
            P("clip", "head", None),
            P("clip", None, None, "head"),
            P("clip", None, "head"),
            P("clip", "head", None),
            P("clip", None, "head"),
            P("clip", "head", None),
        ),
        check_vma=False,
    )
```

```python
import functools

import jax
import jax.numpy as jnp
from jax import lax
from jax.experimental import pallas as pl
from jax.experimental.pallas import tpu as pltpu
from jax.sharding import PartitionSpec as P


HEAD_DIM = 64
EPSILON = 1e-06
SCORE_SCALE = 0.125
MASKED = -1e30
BF16 = jnp.bfloat16
F32 = jnp.float32
COST_BYTES = 1

FULL, CORE, ACROSS, SECOND_PLANE, TOP_BIG, BOTTOM_BIG, TOP_MID, BOTTOM_MID, ENDS = range(9)
SELF_A, SELF_B, CROSS_A, CROSS_B = range(4)


def over_head(value):
    return lax.ppermute(value, "head", [(0, 1), (1, 0)])


def over_bit(value, bit, count=None):
    count = lax.axis_size("clip") if count is None else count
    return lax.ppermute(value, "clip", [(i, i ^ (1 << bit)) for i in range(count)])


def other_core(value):
    return over_bit(value, 0)


def fence(*values):
    return lax.optimization_barrier(values)


def after(value, *others):
    return lax.optimization_barrier((value,) + others)[0]


def in_core_order(core, mine, theirs, axis):
    first = jnp.where(core == 0, mine, theirs)
    second = jnp.where(core == 0, theirs, mine)
    return jnp.concatenate([first, second], axis=axis)


def core_piece(value, piece, axis):
    size = value.shape[axis] // 2
    return lax.dynamic_slice_in_dim(value, piece * size, size, axis)


def dot_nt(left, right):
    return lax.dot_general(left, right, (((1,), (1,)), ((), ())), preferred_element_type=F32)


def dot_tn(left, right):
    return lax.dot_general(left, right, (((0,), (0,)), ((), ())), preferred_element_type=F32)


def dot_nn(left, right):
    return jnp.dot(left, right, preferred_element_type=F32)


def norm_stats(rows):
    mean = jnp.mean(rows, axis=-1, keepdims=True)
    centered = rows - mean
    variance = jnp.mean(centered * centered, axis=-1, keepdims=True)
    inverse = lax.rsqrt(variance + EPSILON)
    return centered * inverse, inverse


def norm_back(grad, normal, inverse, gain):
    scaled = grad * gain
    mean = jnp.mean(scaled, axis=-1, keepdims=True)
    along = jnp.mean(scaled * normal, axis=-1, keepdims=True)
    grad_rows = (scaled - mean - normal * along) * inverse
    gain_grad = jnp.sum(grad * normal, axis=0, keepdims=True)
    return grad_rows, gain_grad, jnp.sum(grad, axis=0, keepdims=True)


def pick(info, flag, yes, no):
    return jnp.where(info[flag] != 0, yes, no)


def core_order(info, mine, theirs):
    return pick(info, CORE, theirs, mine), pick(info, CORE, mine, theirs)


def joined_pieces(info, mine, theirs, axis):
    return jnp.concatenate(core_order(info, mine, theirs), axis=axis)


def exchanged(info, top_flag, first, second, received):
    return pick(info, top_flag, received, first), pick(info, top_flag + 1, received, second)


def to_send(info, first, second):
    return pick(info, CORE, first, second)


def put_pieces(info, keep_ref, send_ref, at, value, axis):
    size = value.shape[axis] // 2
    low, high = (value[:size], value[size:]) if axis == 0 else (value[:, :size], value[:, size:])
    mine, theirs = core_order(info, low.astype(BF16), high.astype(BF16))
    keep_ref[at] = mine
    send_ref[at] = theirs


def resident(shape, index=None):
    index = (lambda j, info: (0,) * len(shape)) if index is None else index
    return pl.BlockSpec(shape, index, pipeline_mode=pl.Buffered(1))


def whole_in(array):
    return (array, resident(array.shape))


def whole_out(*shape, kind=BF16):
    return (shape, kind, resident(shape))


def lead_spec(*shape):
    return pl.BlockSpec((None,) + shape, lambda j, info: (j,) + (0,) * len(shape))


def out_type(shape, kind, spec, in_hbm=False):
    return pltpu.HBM(shape, kind) if in_hbm else jax.ShapeDtypeStruct(shape, kind)


def call(kernel, info, steps, ins, outs, scratch, name, mebibytes, cost):
    return pl.pallas_call(
        kernel,
        grid_spec=pltpu.PrefetchScalarGridSpec(
            num_scalar_prefetch=1,
            grid=(steps,),
            in_specs=[spec for _, spec in ins],
            out_specs=[out[2] for out in outs],
            scratch_shapes=scratch,
        ),
        out_shape=[out_type(*out) for out in outs],
        compiler_params=pltpu.CompilerParams(vmem_limit_bytes=mebibytes * 1024 * 1024),
        cost_estimate=pl.CostEstimate(flops=0, bytes_accessed=cost * COST_BYTES, transcendentals=0),
        name=name,
    )(info, *[array for array, _ in ins])


def part_rows(array):
    _, count, width = array.shape
    return [
        (array, resident((None, count, width), lambda j, info: (info[ACROSS], 0, 0))),
        (array, resident((None, count // 2, width), lambda j, info: (2, info[CORE], 0))),
    ]


def joined_rows(info, a_ref, kept_ref, received_ref):
    own = info[CORE] == info[ACROSS]
    return jnp.concatenate([a_ref[...], jnp.where(own, kept_ref[...], received_ref[...])], axis=0)


def clip_bias(info, group, rows, cols, row_kind, col_kind):
    def clips(kind, places, shape, axis):
        base = ENDS + 16 * group + 4 * kind
        place = lax.broadcasted_iota(jnp.int32, shape, axis) + places.start
        return sum((place >= info[base + k]).astype(jnp.int32) for k in range(4))

    of_rows = clips(row_kind, rows, (rows.stop - rows.start, 128), 0)[:, :1]
    of_cols = clips(col_kind, cols, (8, cols.stop - cols.start), 1)[:1, :]
    return jnp.where(of_rows == of_cols, 0.0, MASKED)


def attention_blocks(full, cross, half):
    if full and cross:
        return [(None, (0, 1), slice(0, half), slice(0, 2 * half))]
    if full:
        return [(s, (0, 1), slice(s * half, (s + 1) * half), slice(0, 2 * half)) for s in range(2)]
    if cross:
        return [(s, (s,), slice(0, half), slice(s * half, (s + 1) * half)) for s in range(2)]
    return [(s, (s,), slice(s * half, (s + 1) * half), slice(0, half)) for s in range(2)]


def load_halves(info, refs, exchange):
    first, second = refs[0][...], refs[1][...]
    if exchange:
        first, second = exchanged(info, TOP_BIG, first, second, refs[2][...])
    return first, second


def query_half(info, halves, s):
    return pick(info, SECOND_PLANE, halves[1], halves[0]) if s is None else halves[s]


def head_lanes(h):
    first = lax.broadcasted_iota(jnp.int32, (1, 2 * HEAD_DIM), 1) < HEAD_DIM
    return first if h == 0 else jnp.logical_not(first)


def attend_kernel(group, counts, info, *refs):
    cross = group in (CROSS_A, CROSS_B)
    part_b = group in (SELF_B, CROSS_B)
    operands, at = [], 0
    for n in counts:
        operands.append(refs[at : at + n])
        at += n
    outs = refs[at:]
    bias_ref = outs[-1]
    p_ref = outs[-2]
    q, k, v = (load_halves(info, refs, len(refs) == 3) for refs in operands)
    half = q[0].shape[0]

    def run(full):
        blocks = attention_blocks(full, cross, half)

        @pl.when(pl.program_id(0) == 0)
        def _():
            for s, keys, rows, cols in blocks:
                at = rows if full else slice(0, half)
                kinds = (0, 1) if full else (2 + s, 2 + s)
                bias_ref[rows, cols] = clip_bias(info, group, at, slice(0, half * len(keys)), *kinds)

        mixes = []
        for s, keys, rows, cols in blocks:
            query = query_half(info, q, s) * jnp.asarray(SCORE_SCALE, BF16)
            key = jnp.concatenate([k[t] for t in keys], axis=0)
            value = jnp.concatenate([v[t] for t in keys], axis=0)
            pair = []
            for h in range(2):
                own = jnp.where(head_lanes(h), query, jnp.zeros_like(query))
                scores = dot_nt(own, key) + bias_ref[rows, cols]
                top = jnp.max(scores, axis=-1, keepdims=True)
                exponent = jnp.exp(scores - top)
                total = jnp.sum(exponent, axis=-1, keepdims=True)
                probs = (exponent * (1.0 / total)).astype(BF16)
                p_ref[h, rows, cols] = probs
                pair.append(dot_nn(probs, value))
            mixes.append(jnp.where(head_lanes(0), pair[0], pair[1]).astype(BF16))
        top, bottom = mixes[0], mixes[-1]
        if cross:
            outs[0][...] = top
            outs[1][...] = bottom
        else:
            outs[0][:half, :] = top
            outs[0][half:, :] = bottom
            if part_b:
                outs[1][...] = to_send(info, top, bottom)

    pl.when(info[FULL] != 0)(lambda: run(True))
    pl.when(info[FULL] == 0)(lambda: run(False))


def attend_back_kernel(group, counts, info, *refs):
    cross = group in (CROSS_A, CROSS_B)
    part_b = group in (SELF_B, CROSS_B)
    operands, at = [], 0
    for n in counts:
        operands.append(refs[at : at + n])
        at += n
    p_ref, outs = refs[at], refs[at + 1 :]
    q, k, v, g = (load_halves(info, refs, len(refs) == 3) for refs in operands)
    half = q[0].shape[0]

    def run(full):
        blocks = attention_blocks(full, cross, half)
        queries, sums = [], {}
        for s, keys, rows, cols in blocks:
            query = query_half(info, q, s)
            grad = query_half(info, g, s)
            key = jnp.concatenate([k[t] for t in keys], axis=0)
            value = jnp.concatenate([v[t] for t in keys], axis=0)
            dq, dk, dv = [], [], []
            for h in range(2):
                own = jnp.where(head_lanes(h), grad, jnp.zeros_like(grad))
                probs = p_ref[h, rows, cols]
                wide_probs = probs.astype(F32)
                grad_probs = dot_nt(own, value)
                delta = jnp.sum(wide_probs * grad_probs, axis=-1, keepdims=True)
                grad_scores = (wide_probs * (grad_probs - delta)).astype(BF16)
                dq.append(dot_nn(grad_scores, key))
                dk.append(dot_tn(grad_scores, query))
                dv.append(dot_tn(probs, grad))
            queries.append((jnp.where(head_lanes(0), dq[0], dq[1]) * SCORE_SCALE).astype(BF16))
            both = (jnp.where(head_lanes(0), dk[0], dk[1]), jnp.where(head_lanes(0), dv[0], dv[1]))
            sums[keys] = (sums[keys][0] + both[0], sums[keys][1] + both[1]) if keys in sums else both
        grads = []
        for t in range(2):
            dk, dv = (sums[(0, 1)] if full else sums[(t,)])
            rows = slice(t * half, (t + 1) * half) if full else slice(0, half)
            grads.append(((dk[rows] * SCORE_SCALE).astype(BF16), dv[rows].astype(BF16)))
        top, bottom = queries[0], queries[-1]
        if cross:
            outs[0][...] = top
            outs[1][...] = bottom
        parts = [(g0, g1) for g0, g1 in zip(*grads)]
        if not cross:
            parts = [(top, bottom)] + parts
        out_ref = outs[2] if cross else outs[0]
        for n, (first, second) in enumerate(parts):
            out_ref[n, :half, :] = first
            out_ref[n, half:, :] = second
            if part_b:
                outs[3 if cross else 1][n] = to_send(info, first, second)

    pl.when(info[FULL] != 0)(lambda: run(True))
    pl.when(info[FULL] == 0)(lambda: run(False))


def column_block(array, lead=None, row=0, column=0, rows=256):
    lanes = 2 * HEAD_DIM
    if array.ndim == 3:
        return (array, pl.BlockSpec((None, rows, lanes), lambda j, info: (lead, row, j + column)))
    return (array, pl.BlockSpec((rows, lanes), lambda j, info: (row, j + column)))


def halves_of(array, lead=None):
    return [column_block(array, lead, 0), column_block(array, lead, 1)]


def attend(info, group, operands, columns, rows=256):
    cross = group in (CROSS_A, CROSS_B)
    lanes = 2 * HEAD_DIM
    heads = columns // HEAD_DIM
    p_rows = rows if cross else 2 * rows
    half_out = ((rows, columns), BF16, pl.BlockSpec((rows, lanes), lambda j, info: (0, j)))
    mix_out = ((2 * rows, columns), BF16, pl.BlockSpec((2 * rows, lanes), lambda j, info: (0, j)))
    outs = [half_out, half_out] if cross else [mix_out] + ([half_out] if group == SELF_B else [])
    p_block = pl.BlockSpec((2, p_rows, 2 * rows), lambda j, info: (j, 0, 0))
    p_out = ((heads, p_rows, 2 * rows), BF16, p_block, True)
    return call(
        functools.partial(attend_kernel, group, [len(o) for o in operands]),
        info,
        heads // 2,
        sum(operands, []),
        outs + [p_out],
        [pltpu.VMEM((p_rows, 2 * rows), F32)],
        "attend",
        14,
        heads * 2 // 3,
    )


def attend_back(info, group, operands, probs, columns, rows=256):
    cross = group in (CROSS_A, CROSS_B)
    part_b = group in (SELF_B, CROSS_B)
    lanes = 2 * HEAD_DIM
    half_out = ((rows, columns), BF16, pl.BlockSpec((rows, lanes), lambda j, info: (0, j)))
    count = 2 if cross else 3

    def stacked(height):
        return ((count, height, columns), BF16, pl.BlockSpec((count, height, lanes), lambda j, info: (0, 0, j)))

    outs = [half_out, half_out] if cross else []
    outs = outs + [stacked(2 * rows)] + ([stacked(rows)] if part_b else [])
    p_block = pl.BlockSpec((2,) + probs.shape[1:], lambda j, info: (j, 0, 0))
    return call(
        functools.partial(attend_back_kernel, group, [len(o) for o in operands]),
        info,
        probs.shape[0] // 2,
        sum(operands, []) + [(probs, p_block)],
        outs,
        [],
        "attend_back",
        14,
        probs.shape[0],
    )


def first_project_kernel(info, a_ref, kept_ref, received_ref, norms_ref, w_ref, rows_ref, normed_ref, out_ref):
    @pl.when(pl.program_id(0) == 0)
    def _():
        rows = joined_rows(info, a_ref, kept_ref, received_ref)
        rows_ref[...] = rows
        normal, _ = norm_stats(rows.astype(F32))
        normed_ref[...] = (normal * norms_ref[0:1, :] + norms_ref[1:2, :]).astype(BF16)

    out_ref[...] = dot_nn(normed_ref[...], w_ref[...]).astype(BF16)


def first_project(info, tokens, received, norms, w_self):
    count, width, cols = w_self.shape
    rows = tokens.shape[1] + received.shape[0]
    return call(
        first_project_kernel,
        info,
        count,
        part_rows(tokens) + [whole_in(received), whole_in(norms), (w_self, lead_spec(width, cols))],
        [whole_out(rows, width), whole_out(rows, width), ((count, rows, cols), BF16, lead_spec(rows, cols))],
        [],
        "first_project",
        16,
        4,
    )


def other_project_kernel(info, normed_ref, own_b_ref, mine_ref, theirs_ref, out_ref, send_ref):
    weights = joined_pieces(info, mine_ref[...], theirs_ref[...], 0)
    out = dot_nn(normed_ref[...], weights).astype(BF16)
    out_ref[...] = out
    part_b = out.shape[0] - own_b_ref.shape[0]
    send_ref[...] = to_send(info, own_b_ref[...], out[part_b:])


def other_project(info, normed, qkv_own, mine, theirs, part_b):
    count, half, cols = mine.shape
    rows = normed.shape[0]
    own_b = pl.BlockSpec((None, part_b, cols), lambda j, info: (j, rows // part_b - 1, 0))
    return call(
        other_project_kernel,
        info,
        count,
        [whole_in(normed), (qkv_own, own_b), (mine, lead_spec(half, cols)), (theirs, lead_spec(half, cols))],
        [
            ((count, rows, cols), BF16, lead_spec(rows, cols)),
            ((count, part_b, cols), BF16, lead_spec(part_b, cols)),
        ],
        [],
        "other_project",
        12,
        3,
    )


def put_query_parts(info, value, far_ref, near_ref, left_ref, right_ref, send_ref):
    rows = left_ref.shape[0]
    cols = left_ref.shape[1]
    for h in range(2):
        at = slice(h * cols, (h + 1) * cols)
        far_ref[:, at] = value[h][:rows]
        near_ref[:, at] = value[h][rows : 2 * rows]
    left, right = value[0][2 * rows :], value[1][2 * rows :]
    left_ref[...] = left
    right_ref[...] = right
    send_ref[...] = to_send(info, left, right)


def query_outs(rows, width):
    whole, half = whole_out(rows, width), whole_out(rows, width // 2)
    return [whole, whole, half, half, half]


def self_mixes(info, mix0_ref, mix1_ref, slots_ref, received_ref):
    rows = received_ref.shape[0]
    parts = exchanged(info, TOP_BIG, slots_ref[:rows, :], slots_ref[rows:, :], received_ref[...])
    return [
        jnp.concatenate([ref[...], part], axis=0) for ref, part in zip((mix0_ref, mix1_ref), parts)
    ]


def second_project_kernel(
    info, rows_ref, norms_ref, mix0_ref, mix1_ref, slots_ref, received_ref, out_ref, query_ref, mine_ref, theirs_ref,
    hidden_ref, joined_ref, *query_refs,
):
    mixes = self_mixes(info, mix0_ref, mix1_ref, slots_ref, received_ref)
    other_out = joined_pieces(info, mine_ref[0], theirs_ref[0], 1)
    hidden = rows_ref[...].astype(F32) + dot_nn(mixes[0], out_ref[...]) + dot_nn(mixes[1], other_out)
    hidden_ref[...] = hidden
    normal, _ = norm_stats(hidden)
    joined = (normal * norms_ref[2:3, :] + norms_ref[3:4, :]).astype(BF16)
    joined_ref[...] = joined
    other_query = joined_pieces(info, mine_ref[1], theirs_ref[1], 0)
    queries = [dot_nn(joined, w).astype(BF16) for w in (query_ref[...], other_query)]
    put_query_parts(info, queries, *query_refs)


def second_project(info, rows, norms, mixes, w_self_out, w_query, mine, theirs, part_b):
    shape = rows.shape
    return call(
        second_project_kernel,
        info,
        1,
        [whole_in(a) for a in (rows, norms, *mixes, w_self_out, w_query, mine, theirs)],
        [whole_out(*shape, kind=F32), whole_out(*shape)] + query_outs(part_b, shape[1]),
        [],
        "second_project",
        20,
        5,
    )


def offer_project_kernel(info, rows_ref, own_ref, mine_ref, theirs_ref, out_ref, send_ref):
    cols = own_ref.shape[1]
    rows = send_ref.shape[0]
    other = joined_pieces(info, mine_ref[...], theirs_ref[...], 0)
    parts = [dot_nn(rows_ref[...], w).astype(BF16) for w in (own_ref[...], other)]
    for h in range(2):
        out_ref[:, h * cols : (h + 1) * cols] = parts[h]
    send_ref[...] = to_send(info, parts[0][-rows:], parts[1][-rows:])


def offer_project(info, joined, w_offer, mine, theirs, part_b):
    count, width, cols = w_offer.shape
    rows = joined.shape[0]
    piece = lead_spec(cols, cols)
    return call(
        offer_project_kernel,
        info,
        count,
        [whole_in(joined), (w_offer, lead_spec(width, cols)), (mine, piece), (theirs, piece)],
        [
            ((count, rows, 2 * cols), BF16, lead_spec(rows, 2 * cols)),
            ((count, part_b, cols), BF16, lead_spec(part_b, cols)),
        ],
        [],
        "offer_project",
        12,
        4,
    )


def reader_rows(info, far_ref, near_ref, far_b_ref, near_b_ref, received_ref):
    half = far_b_ref.shape[1]
    parts = exchanged(info, TOP_MID, far_b_ref[...], near_b_ref[...], received_ref[...])
    return [
        jnp.concatenate([ref[:, h * half : (h + 1) * half] for ref in (far_ref, near_ref)] + [parts[h]], axis=0)
        for h in range(2)
    ]


def mlp_kernel(
    info, hidden_ref, norms_ref, far_ref, near_ref, far_b_ref, near_b_ref, received_ref, w_cross_ref, mine_ref,
    theirs_ref, grad_a_ref, grad_kept_ref, grad_received_ref, up_ref, down_ref, result_ref, grad_second_ref, gm_far_ref, gm_near_ref, gm_left_ref, gm_right_ref,
    gm_send_ref, up_keep_ref, up_send_ref, down_keep_ref, down_send_ref, keep_ref, send_ref, g_norms_ref, second_ref,
    rows_ref, grad_ref, sum_ref, back_ref,
):
    step = pl.program_id(0)

    def mixes():
        return reader_rows(info, far_ref, near_ref, far_b_ref, near_b_ref, received_ref)

    def cross_weights():
        return w_cross_ref[...], joined_pieces(info, mine_ref[...], theirs_ref[...], 1)

    @pl.when(step == 0)
    def _():
        grad_ref[...] = joined_rows(info, grad_a_ref, grad_kept_ref, grad_received_ref)
        second = hidden_ref[...]
        for mix, weight in zip(mixes(), cross_weights()):
            second = second + dot_nn(mix, weight)
        second_ref[...] = second
        normal, _ = norm_stats(second)
        rows_ref[...] = (normal * norms_ref[4:5, :] + norms_ref[5:6, :]).astype(BF16)
        sum_ref[...] = second
        back_ref[...] = jnp.zeros_like(back_ref)

    rows, grad, up, down = rows_ref[...], grad_ref[...], up_ref[...], down_ref[...]
    pre = dot_nn(rows, up)
    spread = lax.erf(pre * 0.7071067811865476) * 0.5 + 0.5
    slope = spread + pre * (jnp.exp(pre * pre * -0.5) * 0.3989422804014327)
    activated = (pre * spread).astype(BF16)
    grad_up = (dot_nt(grad, down) * slope).astype(BF16)
    sum_ref[...] += dot_nn(activated, down)
    back_ref[...] += dot_nt(grad_up, up)
    g_up = dot_tn(rows, grad_up).astype(BF16)
    g_down = dot_tn(activated, grad).astype(BF16)

    @pl.when(step < 2)
    def _():
        up_keep_ref[...] = g_up
        down_keep_ref[...] = g_down

    @pl.when(step >= 2)
    def _():
        up_send_ref[...] = g_up
        down_send_ref[...] = g_down

    @pl.when(step == 3)
    def _():
        result_ref[...] = sum_ref[...].astype(BF16)
        normal, inverse = norm_stats(second_ref[...])
        back, gain, shift = norm_back(back_ref[...], normal, inverse, norms_ref[4:5, :])
        g_norms_ref[0:1, :] = gain
        g_norms_ref[1:2, :] = shift
        grad_second = grad_ref[...].astype(F32) + back
        grad_second_ref[...] = grad_second
        rounded = grad_second.astype(BF16)
        parts = []
        for h, (mix, weight) in enumerate(zip(mixes(), cross_weights())):
            parts.append(dot_nt(rounded, weight).astype(BF16))
            put_pieces(info, keep_ref, send_ref, h, dot_tn(mix, rounded), 1)
        put_query_parts(info, parts, gm_far_ref, gm_near_ref, gm_left_ref, gm_right_ref, gm_send_ref)


def mlp(info, hidden, norms, mixes, w_cross, mine, theirs, cotangent, received, up, down):
    rows, width = hidden.shape
    half = width // 2
    part_b = received.shape[0]

    def pieces(index):
        return ((2, width, width), BF16, pl.BlockSpec((None, width, width), lambda j, info: (index(j), 0, 0)))

    keep, send = pieces(lambda j: jnp.minimum(j, 1)), pieces(lambda j: jnp.maximum(j - 2, 0))
    wide = pltpu.VMEM((rows, width), F32)
    narrow = pltpu.VMEM((rows, width), BF16)
    return call(
        mlp_kernel,
        info,
        4,
        [whole_in(a) for a in (hidden, norms, *mixes, w_cross)]
        + [whole_in(mine), whole_in(theirs)]
        + part_rows(cotangent)
        + [whole_in(received), (up, lead_spec(width, width)), (down, lead_spec(width, width))],
        [whole_out(rows, width), whole_out(rows, width, kind=F32)]
        + query_outs(part_b, width)
        + [keep, send, keep, send, whole_out(2, half, half), whole_out(2, half, half)]
        + [whole_out(2, width, kind=F32)],
        [wide, narrow, narrow, wide, wide],
        "mlp",
        46,
        34,
    )


def second_back_kernel(
    info, far_ref, near_ref, far_b_ref, near_b_ref, received_ref, dkv_ref, slots_ref, slots_received_ref, joined_ref,
    hidden_ref, grad_second_ref, norms_ref, offer_ref, offer_mine_ref, offer_theirs_ref, query_ref, out_ref, mine_ref,
    theirs_ref, mix0_ref, mix1_ref, mix_slots_ref, mix_received_ref, cross_keep_ref, cross_send_ref, grad_hidden_ref,
    grad_mix_ref, mix_send_ref, keep_ref, send_ref, g_norms_ref, back_ref,
):
    step = pl.program_id(0)
    half = query_ref.shape[1]
    rows = received_ref.shape[0]

    def add(at, grads, weights, first):
        joined = joined_ref[...]
        total = dot_nt(grads[0], weights[0]) + dot_nt(grads[1], weights[1])
        back_ref[...] = total if first else back_ref[...] + total
        for h in range(2):
            put_pieces(info, keep_ref, send_ref, (h, at), dot_tn(joined, grads[h]), 0)

    def add_offer(at):
        parts = exchanged(info, TOP_BIG, slots_ref[:rows, :], slots_ref[rows:, :], slots_received_ref[...])
        grads = [
            jnp.concatenate([dkv_ref[:, h * half : (h + 1) * half], parts[h]], axis=0) for h in range(2)
        ]
        other = joined_pieces(info, offer_mine_ref[...], offer_theirs_ref[...], 0)
        add(at, grads, (offer_ref[...], other), at == 0)

    pl.when(step == 0)(lambda: add_offer(0))
    pl.when(step == 1)(lambda: add_offer(1))

    @pl.when(step == 2)
    def _():
        for h in range(2):
            keep_ref[h, 4] = cross_keep_ref[h]
            send_ref[h, 4] = cross_send_ref[h]
        grads = reader_rows(info, far_ref, near_ref, far_b_ref, near_b_ref, received_ref)
        add(2, grads, (query_ref[...], joined_pieces(info, mine_ref[1], theirs_ref[1], 0)), False)
        normal, inverse = norm_stats(hidden_ref[...])
        back, gain, shift = norm_back(back_ref[...], normal, inverse, norms_ref[2:3, :])
        g_norms_ref[0:1, :] = gain
        g_norms_ref[1:2, :] = shift
        grad_hidden = grad_second_ref[...] + back
        grad_hidden_ref[...] = grad_hidden
        rounded = grad_hidden.astype(BF16)
        mixes = self_mixes(info, mix0_ref, mix1_ref, mix_slots_ref, mix_received_ref)
        parts = []
        for h, weight in enumerate((out_ref[...], joined_pieces(info, mine_ref[0], theirs_ref[0], 1))):
            part = dot_nt(rounded, weight).astype(BF16)
            grad_mix_ref[h] = part
            parts.append(part[-rows:])
            put_pieces(info, keep_ref, send_ref, (h, 3), dot_tn(mixes[h], rounded), 1)
        mix_send_ref[...] = to_send(info, *parts)


def second_back(
    info, grad_q, dkv, slots, slots_received, joined, hidden, grad_second, norms, w_offer, offer_mine, offer_theirs,
    w_query, w_self_out, mine, theirs, mixes, cross_keep, cross_send,
):
    rows, width = hidden.shape
    half = width // 2
    part_b = slots_received.shape[1]

    def offered(array, *shape):
        return (array, pl.BlockSpec((None,) + shape, lambda j, info: (jnp.minimum(j, 1), 0, 0)))

    return call(
        second_back_kernel,
        info,
        3,
        [whole_in(a) for a in grad_q]
        + [offered(dkv, *dkv.shape[1:]), offered(slots, *slots.shape[1:])]
        + [offered(slots_received, *slots_received.shape[1:])]
        + [whole_in(a) for a in (joined, hidden, grad_second, norms)]
        + [offered(w_offer, width, half), offered(offer_mine, half, half), offered(offer_theirs, half, half)]
        + [whole_in(a) for a in (w_query, w_self_out, mine, theirs, *mixes, cross_keep, cross_send)],
        [whole_out(rows, width, kind=F32), whole_out(2, rows, half), whole_out(part_b, half)]
        + [whole_out(2, 5, half, half), whole_out(2, 5, half, half), whole_out(2, width, kind=F32)],
        [pltpu.VMEM((rows, width), F32)],
        "second_back",
        40,
        12,
    )


def first_back_kernel(
    info, own_ref, other_ref, slots_ref, received_ref, rows_ref, normed_ref, grad_hidden_ref, norms_ref, w_own_ref,
    mine_ref, theirs_ref, grad_rows_ref, keep_ref, send_ref, g_norms_ref, back_ref,
):
    step = pl.program_id(0)
    rows = received_ref.shape[0]
    parts = exchanged(info, TOP_BIG, slots_ref[:rows, :], slots_ref[rows:, :], received_ref[...])
    grads = [jnp.concatenate([ref[...], part], axis=0) for ref, part in zip((own_ref, other_ref), parts)]
    normed = normed_ref[...]
    for h in range(2):
        put_pieces(info, keep_ref, send_ref, (h, step), dot_tn(normed, grads[h]), 0)
    other = joined_pieces(info, mine_ref[...], theirs_ref[...], 0)
    total = dot_nt(grads[0], w_own_ref[...]) + dot_nt(grads[1], other)

    @pl.when(step == 0)
    def _():
        back_ref[...] = total

    @pl.when(step > 0)
    def _():
        back_ref[...] += total

    @pl.when(step == pl.num_programs(0) - 1)
    def _():
        normal, inverse = norm_stats(rows_ref[...].astype(F32))
        back, gain, shift = norm_back(back_ref[...], normal, inverse, norms_ref[0:1, :])
        g_norms_ref[0:1, :] = gain
        g_norms_ref[1:2, :] = shift
        grad_rows_ref[...] = (grad_hidden_ref[...] + back).astype(BF16)


def first_back(info, own, other, slots, received, rows, normed, grad_hidden, norms, w_self, mine, theirs):
    count, half = own.shape[0], own.shape[2]
    width = rows.shape[1]
    ins = [(a, lead_spec(*a.shape[1:])) for a in (own, other, slots, received)]
    ins += [whole_in(a) for a in (rows, normed, grad_hidden, norms)]
    ins += [(a, lead_spec(*a.shape[1:])) for a in (w_self, mine, theirs)]
    pieces = whole_out(2, count, half, half)
    return call(
        first_back_kernel,
        info,
        count,
        ins,
        [whole_out(*rows.shape), pieces, pieces, whole_out(2, width, kind=F32)],
        [pltpu.VMEM(rows.shape, F32)],
        "first_back",
        32,
        11,
    )


def row_of(table, index):
    return lax.dynamic_index_in_dim(table, index, 0, keepdims=False)


def scalars(clip_len, index, across, quarter):
    core = index % 2
    is_big = index < 2 * quarter
    is_mid = jnp.logical_and(index >= 2 * quarter, index < 3 * quarter)
    first, last = core == 0, core == 1
    flags = [
        is_big,
        core,
        across,
        jnp.logical_and(is_big, index >= quarter),
        jnp.logical_and(is_big, last),
        jnp.logical_and(is_big, first),
        jnp.logical_and(is_mid, last),
        jnp.logical_and(is_mid, first),
    ]
    shared = index - core + across
    lens_a, lens_b = row_of(clip_len, across), clip_len[2]
    big_a = row_of(lens_a, jnp.minimum(index, 2 * quarter - 1))
    big_b = row_of(lens_b, jnp.minimum(shared, 2 * quarter - 1))
    sets_a = [row_of(lens_a, index % quarter + s * quarter) for s in range(2)]
    sets_b = [row_of(lens_b, shared % quarter + core * quarter)] * 2
    table = jnp.stack(
        [2 * big_a, 2 * big_a, *sets_a, 2 * big_b, 2 * big_b, *sets_b]
        + [big_a, 2 * big_a, *sets_a, big_b, 2 * big_b, *sets_b]
    )
    ends = [table[:, 0]]
    for k in range(1, 4):
        ends.append(ends[-1] + table[:, k])
    flags = jnp.stack([flag.astype(jnp.int32) for flag in flags])
    return jnp.concatenate([flags, jnp.stack(ends, axis=1).reshape(-1)])


def local(
    tokens,
    cotangent,
    clip_len,
    ln_params,
    w_self,
    w_self_out,
    w_offer,
    w_query,
    w_cross_out,
    w_up,
    w_down,
):
    index = lax.axis_index("clip")
    across = lax.axis_index("head")
    count = lax.axis_size("clip")
    quarter = count // 4
    levels = (2 * quarter).bit_length() - 1
    core = index % 2
    is_big = index < 2 * quarter
    is_mid = jnp.logical_and(index >= 2 * quarter, index < 3 * quarter)
    own_micro2 = core == across
    norms = ln_params[0]
    w_self, w_self_out, w_offer, w_query = w_self[0], w_self_out[0], w_offer[0], w_query[0]
    w_cross_out, w_up, w_down = w_cross_out[0], w_up[0], w_down[0]
    half = w_query.shape[1]
    part_a = tokens.shape[1]
    part_b = part_a // 2
    wide = 2 * half

    near = [(i, i - quarter) for i in range(2 * quarter, count)]
    far = [(i, i - 2 * quarter) for i in range(2 * quarter, 3 * quarter)]
    far += [(i, i - quarter) for i in range(3 * quarter, count)]

    def to_server(far_rows, near_rows):
        second = lax.ppermute(near_rows, "clip", near)
        return lax.ppermute(far_rows, "clip", far), second

    def to_reader(far_rows, near_rows):
        second = lax.ppermute(near_rows, "clip", [(b, a) for a, b in near])
        return lax.ppermute(far_rows, "clip", [(b, a) for a, b in far]), second

    def reader_slots(left, right, received):
        top = jnp.where(jnp.logical_and(is_mid, core == 1), received, left)
        return top, jnp.where(jnp.logical_and(is_mid, core == 0), received, right)

    def from_server(top, bottom):
        return top, bottom, other_core(jnp.where(core == 0, bottom, top))

    def over_level(part, bit):
        return over_bit(part, bit, 2 * quarter if bit == levels - 1 else None)

    def add(left, right):
        return (left.astype(F32) + right.astype(F32)).astype(BF16)

    def view_sum(total, received):
        total = add(total, received)
        for bit in range(2, levels):
            total = add(total, over_level(total, bit))
        return total

    def all_rows(mine, theirs):
        a_mine, b_mine = mine[:part_a], mine[part_a:]
        a_theirs, b_theirs = theirs[:part_a], theirs[part_a:]
        kept = jnp.where(own_micro2, b_mine, b_theirs)
        received = other_core(jnp.where(own_micro2, b_theirs, b_mine))
        micro2 = in_core_order(core, kept, received, 0)
        micro0 = jnp.where(across == 0, a_mine, a_theirs)
        micro1 = jnp.where(across == 0, a_theirs, a_mine)
        return jnp.stack([micro0, micro1, micro2])


    def over_head_rows(array, start, stop, *others):
        return over_head(after(array[start:stop], *others) if others else array[start:stop])

    self_mine = over_head(core_piece(w_self, core, 1))
    tokens_received = other_core(core_piece(tokens[2], 1 - core, 0))
    info = scalars(clip_len, index, across, quarter)
    rows, normed, qkv_own = first_project(info, tokens, tokens_received, norms, w_self)
    self_0 = [halves_of(qkv_own, n) for n in range(3)]
    mix_0, p_0 = attend(info, SELF_A, self_0, half)
    first_piece = jnp.stack([core_piece(w_self_out, core, 1), core_piece(w_query, core, 0)])
    offer_piece, up_piece, down_piece = core_piece(w_offer, core, 1), core_piece(w_up, core, 1), core_piece(w_down, core, 0)
    cross_piece = core_piece(w_cross_out, core, 1)
    (self_mine, mix_0, first_piece) = fence(self_mine, mix_0, first_piece)

    first_mine = over_head(first_piece)
    self_theirs = other_core(self_mine)
    qkv_other, qkv_send = other_project(info, normed, qkv_own, self_mine, self_theirs, part_b)
    self_1 = [halves_of(qkv_other, n) for n in range(3)]
    mix_1, p_1 = attend(info, SELF_A, self_1, half)
    qkv_received, first_mine, mix_1, offer_piece = fence(other_core(qkv_send), first_mine, mix_1, offer_piece)

    offer_mine = over_head(offer_piece)
    self_b = [
        [column_block(qkv_own, n, 2), column_block(qkv_other, n, 2), column_block(qkv_received, n)] for n in range(3)
    ]
    mix_s, mix_send, p_s = attend(info, SELF_B, self_b, half)
    first_theirs = other_core(first_mine)
    mixes = (mix_0, mix_1, mix_s, other_core(mix_send))
    hidden, joined, q_far, q_near, q_left, q_right, q_send = second_project(
        info, rows, norms, mixes, w_self_out, w_query, first_mine, first_theirs, part_b
    )
    q_far, q_near, q_top, q_bottom, joined, offer_mine, cross_piece, up_piece, down_piece, cotangent = fence(
        q_far, q_near, *reader_slots(q_left, q_right, other_core(q_send)), joined, offer_mine, cross_piece, up_piece,
        down_piece, cotangent,
    )

    up_mine = over_head(up_piece)
    asked_a = to_server(q_far, q_near)
    asked_b = to_server(q_top, q_bottom)
    offer_theirs = other_core(offer_mine)
    offer, offer_send = offer_project(info, joined, w_offer, offer_mine, offer_theirs, part_b)
    cotangent_received = other_core(core_piece(cotangent[2], 1 - core, 0))
    offer_received = other_core(offer_send)
    *asked_a, asked_b_far, asked_b_near, offer_received, cotangent_received, up_mine, down_piece, cross_piece = fence(
        *asked_a, *asked_b, offer_received, cotangent_received, up_mine, down_piece, cross_piece
    )

    down_mine = [over_head(down_piece[:320])]
    cross_a = [[column_block(asked_a[0]), column_block(asked_a[1])]] + [halves_of(offer, n) for n in range(2)]
    far_a, near_a, cross_p_a = attend(info, CROSS_A, cross_a, wide)
    far_a, near_a, asked_b_far, asked_b_near, up_mine, down_mine[0], down_piece, cross_piece = fence(
        far_a, near_a, asked_b_far, asked_b_near, up_mine, down_mine[0], down_piece, cross_piece
    )

    back_a = to_reader(far_a, near_a)
    down_mine.append(over_head(down_piece[320:]))
    cross_mine = over_head(cross_piece)
    cross_b = [[column_block(asked_b_far), column_block(asked_b_near)]] + [
        [
            column_block(offer, n, 2),
            column_block(offer, n, 2, half // (2 * HEAD_DIM)),
            column_block(offer_received, n),
        ]
        for n in range(2)
    ]
    far_b, near_b, cross_p_b = attend(info, CROSS_B, cross_b, half)
    up_theirs = other_core(up_mine)
    *back_a, far_b, near_b, cross_mine, up_mine, up_theirs, down_mine[1] = fence(
        *back_a, far_b, near_b, cross_mine, up_mine, up_theirs, down_mine[1]
    )

    back_b = from_server(*to_reader(far_b, near_b))
    down_mine = jnp.concatenate(down_mine)
    down_theirs = other_core(down_mine)
    cross_theirs = other_core(cross_mine)
    up_pieces = jnp.stack([core_piece(w_up, core, 1), up_mine, core_piece(w_up, 1 - core, 1), up_theirs])
    down_pieces = jnp.stack([core_piece(w_down, core, 0), down_mine, core_piece(w_down, 1 - core, 0), down_theirs])

    (
        result, grad_second, gm_far, gm_near, gm_left, gm_right, gm_send,
        up_keep, up_send, down_keep, down_send, cross_keep, cross_send, norms_3,
    ) = mlp(
        info, hidden, norms, (*back_a, *back_b), w_cross_out, cross_mine, cross_theirs, cotangent, cotangent_received,
        up_pieces, down_pieces,
    )

    gm_far, gm_near, gm_top, gm_bottom, result, down_send, up_send = fence(
        gm_far, gm_near, *reader_slots(gm_left, gm_right, other_core(gm_send)), result, down_send, up_send
    )

    grad_a = to_server(gm_far, gm_near)
    grad_b = to_server(gm_top, gm_bottom)
    layer_x = over_head(result)
    down = add(down_keep, other_core(down_send))
    up = add(up_keep, other_core(up_send))
    *grad_a, grad_b_far, grad_b_near, layer_x, down, up = fence(*grad_a, *grad_b, layer_x, down, up)

    down_x = [over_head(down[1, :384])]
    grad_in = [column_block(grad_a[0]), column_block(grad_a[1])]
    dq_far, dq_near, dkv_a = attend_back(info, CROSS_A, cross_a + [grad_in], cross_p_a, wide)
    dq_far, dq_near, grad_b_far, grad_b_near, down_x[0], down, up = fence(
        dq_far, dq_near, grad_b_far, grad_b_near, down_x[0], down, up
    )

    dq_a = to_reader(dq_far, dq_near)
    down_x.append(over_head(down[1, 384:]))
    up_x = [over_head(up[1, :128])]
    grad_in = [column_block(grad_b_far), column_block(grad_b_near)]
    dq_b_far, dq_b_near, dkv_b, dkv_send = attend_back(info, CROSS_B, cross_b + [grad_in], cross_p_b, half)
    *dq_a, dq_b_far, dq_b_near, down_x[1], up_x[0], up = fence(*dq_a, dq_b_far, dq_b_near, down_x[1], up_x[0], up)

    dq_b = from_server(*to_reader(dq_b_far, dq_b_near))
    dkv_received = other_core(dkv_send)
    up_x.append(over_head(up[1, 128:448]))
    down_total = add(down[0], jnp.concatenate(down_x))
    *dq_b, dkv_received, up_x[1], down_total, up = fence(*dq_b, dkv_received, up_x[1], down_total, up)

    up_x.append(over_head(up[1, 448:]))
    down_y = over_level(down_total, 1)
    grad_hidden, grad_mix, grad_send, mid_keep, mid_send, norms_2 = second_back(
        info, (*dq_a, *dq_b), dkv_a, dkv_b, dkv_received, joined, hidden, grad_second, norms, w_offer,
        offer_mine, offer_theirs, w_query, w_self_out, first_mine, first_theirs, mixes, cross_keep, cross_send,
    )
    grad_hidden, grad_mix, grad_send, mid_keep, mid_send, up_x[2], down_y = fence(
        grad_hidden, grad_mix, grad_send, mid_keep, mid_send, up_x[2], down_y
    )

    mid = add(mid_keep, other_core(mid_send))
    grad_in = [column_block(grad_mix, 0, 2), column_block(grad_mix, 1, 2), column_block(other_core(grad_send))]
    (back_0,) = attend_back(info, SELF_A, self_0 + [halves_of(grad_mix, 0)], p_0, half)
    back_s, back_send = attend_back(info, SELF_B, self_b + [grad_in], p_s, half)
    up_total = add(up[0], jnp.concatenate(up_x))
    back_0, back_s, back_send, mid, up_total, grad_mix, down_total, down_y = fence(
        back_0, back_s, back_send, mid, up_total, grad_mix, down_total, down_y
    )

    mid_x = [over_head(mid[1, :1])]
    up_y = [over_level(up_total[:256], 1)]
    back_received = other_core(back_send)
    (back_1,) = attend_back(info, SELF_A, self_1 + [halves_of(grad_mix, 1)], p_1, half)
    back_1, back_received, mid_x[0], mid, up_y[0], up_total = fence(
        back_1, back_received, mid_x[0], mid, up_y[0], up_total
    )

    mid_x.append(over_head(mid[1, 1:3]))
    up_y.append(over_level(up_total[256:], 1))
    grad_rows, self_keep, self_send, norms_1 = first_back(
        info, back_0, back_1, back_s, back_received, rows, normed, grad_hidden, norms, w_self, self_mine, self_theirs
    )
    grad_rows, self_keep, self_send, mid_x[1], up_y[1], mid = fence(
        grad_rows, self_keep, self_send, mid_x[1], up_y[1], mid
    )
    mid_x.append(over_head(mid[1, 3:]))
    mid_total = [add(mid[0, :3], jnp.concatenate(mid_x[:2]))]
    mid_y = [over_level(mid_total[0], 1)]
    layer_out = all_rows(result, after(layer_x, grad_rows))
    norm_grads = jnp.concatenate([norms_1, norms_2, norms_3, jnp.zeros((2, wide), F32)], axis=0)
    norm_grads = norm_grads.reshape(-1, half).astype(BF16)
    norm_grads = add(norm_grads, other_core(norm_grads))
    last = add(self_keep, other_core(self_send))
    last, norm_grads, mid_x[2], mid, grad_rows = fence(last, norm_grads, mid_x[2], mid, grad_rows)

    end = jnp.concatenate([last[:, 2], jnp.stack([norm_grads, norm_grads])], axis=1)
    last_x = over_head(last[1, :2])
    mid_total.append(add(mid[0, 3:], mid_x[2]))
    mid_y.append(over_level(mid_total[1], 1))
    last_x, last, end, grad_rows = fence(last_x, last, end, grad_rows)

    end_x = over_head(end[1])
    rows_x = over_head(grad_rows)
    last_total = add(last[0, :2], last_x)
    last_y = over_level(last_total, 1)
    last_total, last_y, end_x = fence(last_total, last_y, end_x)

    end_total = add(end[0], end_x)
    end_total = view_sum(end_total, over_level(end_total, 1))
    last_total = view_sum(last_total, last_y)
    down_total = view_sum(down_total, down_y)
    up_total = view_sum(up_total, jnp.concatenate(up_y))
    mid_total = [n for total, received in zip(mid_total, mid_y) for n in view_sum(total, received)]
    norms_total = end_total[half:].reshape(-1, wide)[:6]

    def whole(mine, axis):
        return in_core_order(core, mine, other_core(mine), axis).astype(F32)[None]

    return (
        layer_out,
        all_rows(grad_rows, rows_x).astype(F32),
        norms_total.astype(F32)[None],
        whole(jnp.concatenate([last_total, end_total[None, :half]]), 1),
        whole(mid_total[3], 1),
        whole(jnp.stack(mid_total[:2]), 1),
        whole(mid_total[2], 0),
        whole(mid_total[4], 1),
        whole(up_total, 1),
        whole(down_total, 0),
    )


def solution(mesh):
    return jax.shard_map(
        local,
        mesh=mesh,
        in_specs=(
            P(None, "clip", None),
            P(None, "clip", None),
            P(),
            P("clip", None, None),
            P("clip", None, None, "head"),
            P("clip", "head", None),
            P("clip", None, None, "head"),
            P("clip", None, "head"),
            P("clip", "head", None),
            P("clip", None, "head"),
            P("clip", "head", None),
        ),
        out_specs=(
            P(None, "clip", None),
            P(None, "clip", None),
            P("clip", None, None),
            P("clip", None, None, "head"),
            P("clip", "head", None),
            P("clip", None, None, "head"),
            P("clip", None, "head"),
            P("clip", "head", None),
            P("clip", None, "head"),
            P("clip", "head", None),
        ),
        check_vma=False,
    )
```

```python
import functools

import jax
import jax.numpy as jnp
from jax import lax
from jax.experimental import pallas as pl
from jax.experimental.pallas import tpu as pltpu
from jax.sharding import PartitionSpec as P


HEAD_DIM = 64
EPSILON = 1e-06
SCORE_SCALE = 0.125
MASKED = -1e30
BF16 = jnp.bfloat16
F32 = jnp.float32
COST_BYTES = 1

FULL, CORE, ACROSS, SECOND_PLANE, TOP_BIG, BOTTOM_BIG, TOP_MID, BOTTOM_MID, ENDS = range(9)
SELF_A, SELF_B, CROSS_A, CROSS_B = range(4)


def over_head(value):
    return lax.ppermute(value, "head", [(0, 1), (1, 0)])


def over_bit(value, bit, count=None):
    count = lax.axis_size("clip") if count is None else count
    return lax.ppermute(value, "clip", [(i, i ^ (1 << bit)) for i in range(count)])


def other_core(value):
    return over_bit(value, 0)


def fence(*values):
    return lax.optimization_barrier(values)


def after(value, *others):
    return lax.optimization_barrier((value,) + others)[0]


def in_core_order(core, mine, theirs, axis):
    first = jnp.where(core == 0, mine, theirs)
    second = jnp.where(core == 0, theirs, mine)
    return jnp.concatenate([first, second], axis=axis)


def core_piece(value, piece, axis):
    size = value.shape[axis] // 2
    return lax.dynamic_slice_in_dim(value, piece * size, size, axis)


def dot_nt(left, right):
    return lax.dot_general(left, right, (((1,), (1,)), ((), ())), preferred_element_type=F32)


def dot_tn(left, right):
    return lax.dot_general(left, right, (((0,), (0,)), ((), ())), preferred_element_type=F32)


def dot_nn(left, right):
    return jnp.dot(left, right, preferred_element_type=F32)


def norm_stats(rows):
    mean = jnp.mean(rows, axis=-1, keepdims=True)
    centered = rows - mean
    variance = jnp.mean(centered * centered, axis=-1, keepdims=True)
    inverse = lax.rsqrt(variance + EPSILON)
    return centered * inverse, inverse


def norm_back(grad, normal, inverse, gain):
    scaled = grad * gain
    mean = jnp.mean(scaled, axis=-1, keepdims=True)
    along = jnp.mean(scaled * normal, axis=-1, keepdims=True)
    grad_rows = (scaled - mean - normal * along) * inverse
    gain_grad = jnp.sum(grad * normal, axis=0, keepdims=True)
    return grad_rows, gain_grad, jnp.sum(grad, axis=0, keepdims=True)


def pick(info, flag, yes, no):
    return jnp.where(info[flag] != 0, yes, no)


def core_order(info, mine, theirs):
    return pick(info, CORE, theirs, mine), pick(info, CORE, mine, theirs)


def joined_pieces(info, mine, theirs, axis):
    return jnp.concatenate(core_order(info, mine, theirs), axis=axis)


def exchanged(info, top_flag, first, second, received):
    return pick(info, top_flag, received, first), pick(info, top_flag + 1, received, second)


def to_send(info, first, second):
    return pick(info, CORE, first, second)


def put_pieces(info, keep_ref, send_ref, at, value, axis):
    size = value.shape[axis] // 2
    low, high = (value[:size], value[size:]) if axis == 0 else (value[:, :size], value[:, size:])
    mine, theirs = core_order(info, low.astype(BF16), high.astype(BF16))
    keep_ref[at] = mine
    send_ref[at] = theirs


def resident(shape, index=None):
    index = (lambda j, info: (0,) * len(shape)) if index is None else index
    return pl.BlockSpec(shape, index, pipeline_mode=pl.Buffered(1))


def whole_in(array):
    return (array, resident(array.shape))


def whole_out(*shape, kind=BF16):
    return (shape, kind, resident(shape))


def lead_spec(*shape):
    return pl.BlockSpec((None,) + shape, lambda j, info: (j,) + (0,) * len(shape))


def out_type(shape, kind, spec, in_hbm=False):
    return pltpu.HBM(shape, kind) if in_hbm else jax.ShapeDtypeStruct(shape, kind)


def call(kernel, info, steps, ins, outs, scratch, name, mebibytes, cost):
    return pl.pallas_call(
        kernel,
        grid_spec=pltpu.PrefetchScalarGridSpec(
            num_scalar_prefetch=1,
            grid=(steps,),
            in_specs=[spec for _, spec in ins],
            out_specs=[out[2] for out in outs],
            scratch_shapes=scratch,
        ),
        out_shape=[out_type(*out) for out in outs],
        compiler_params=pltpu.CompilerParams(vmem_limit_bytes=mebibytes * 1024 * 1024),
        cost_estimate=pl.CostEstimate(flops=0, bytes_accessed=cost * COST_BYTES, transcendentals=0),
        name=name,
    )(info, *[array for array, _ in ins])


def part_rows(array):
    _, count, width = array.shape
    return [
        (array, resident((None, count, width), lambda j, info: (info[ACROSS], 0, 0))),
        (array, resident((None, count // 2, width), lambda j, info: (2, info[CORE], 0))),
    ]


def joined_rows(info, a_ref, kept_ref, received_ref):
    own = info[CORE] == info[ACROSS]
    return jnp.concatenate([a_ref[...], jnp.where(own, kept_ref[...], received_ref[...])], axis=0)


def clip_bias(info, group, rows, cols, row_kind, col_kind):
    def clips(kind, places, shape, axis):
        base = ENDS + 16 * group + 4 * kind
        place = lax.broadcasted_iota(jnp.int32, shape, axis) + places.start
        return sum((place >= info[base + k]).astype(jnp.int32) for k in range(4))

    of_rows = clips(row_kind, rows, (rows.stop - rows.start, 128), 0)[:, :1]
    of_cols = clips(col_kind, cols, (8, cols.stop - cols.start), 1)[:1, :]
    return jnp.where(of_rows == of_cols, 0.0, MASKED)


def attention_blocks(full, cross, half):
    if full and cross:
        return [(None, (0, 1), slice(0, half), slice(0, 2 * half))]
    if full:
        return [(s, (0, 1), slice(s * half, (s + 1) * half), slice(0, 2 * half)) for s in range(2)]
    if cross:
        return [(s, (s,), slice(0, half), slice(s * half, (s + 1) * half)) for s in range(2)]
    return [(s, (s,), slice(s * half, (s + 1) * half), slice(0, half)) for s in range(2)]


def load_halves(info, refs, exchange):
    first, second = refs[0][...], refs[1][...]
    if exchange:
        first, second = exchanged(info, TOP_BIG, first, second, refs[2][...])
    return first, second


def query_half(info, halves, s):
    return pick(info, SECOND_PLANE, halves[1], halves[0]) if s is None else halves[s]


def head_lanes(h):
    first = lax.broadcasted_iota(jnp.int32, (1, 2 * HEAD_DIM), 1) < HEAD_DIM
    return first if h == 0 else jnp.logical_not(first)


def attend_kernel(group, counts, info, *refs):
    cross = group in (CROSS_A, CROSS_B)
    part_b = group in (SELF_B, CROSS_B)
    operands, at = [], 0
    for n in counts:
        operands.append(refs[at : at + n])
        at += n
    outs = refs[at:]
    bias_ref = outs[-1]
    p_ref = outs[-2]
    q, k, v = (load_halves(info, refs, len(refs) == 3) for refs in operands)
    half = q[0].shape[0]

    def run(full):
        blocks = attention_blocks(full, cross, half)

        @pl.when(pl.program_id(0) == 0)
        def _():
            for s, keys, rows, cols in blocks:
                at = rows if full else slice(0, half)
                kinds = (0, 1) if full else (2 + s, 2 + s)
                bias_ref[rows, cols] = clip_bias(info, group, at, slice(0, half * len(keys)), *kinds)

        mixes = []
        for s, keys, rows, cols in blocks:
            query = query_half(info, q, s) * jnp.asarray(SCORE_SCALE, BF16)
            key = jnp.concatenate([k[t] for t in keys], axis=0)
            value = jnp.concatenate([v[t] for t in keys], axis=0)
            pair = []
            for h in range(2):
                own = jnp.where(head_lanes(h), query, jnp.zeros_like(query))
                scores = dot_nt(own, key) + bias_ref[rows, cols]
                top = jnp.max(scores, axis=-1, keepdims=True)
                exponent = jnp.exp(scores - top)
                total = jnp.sum(exponent, axis=-1, keepdims=True)
                probs = (exponent * (1.0 / total)).astype(BF16)
                p_ref[h, rows, cols] = probs
                pair.append(dot_nn(probs, value))
            mixes.append(jnp.where(head_lanes(0), pair[0], pair[1]).astype(BF16))
        top, bottom = mixes[0], mixes[-1]
        if cross:
            outs[0][...] = top
            outs[1][...] = bottom
        else:
            outs[0][:half, :] = top
            outs[0][half:, :] = bottom
            if part_b:
                outs[1][...] = to_send(info, top, bottom)

    pl.when(info[FULL] != 0)(lambda: run(True))
    pl.when(info[FULL] == 0)(lambda: run(False))


def attend_back_kernel(group, counts, info, *refs):
    cross = group in (CROSS_A, CROSS_B)
    part_b = group in (SELF_B, CROSS_B)
    operands, at = [], 0
    for n in counts:
        operands.append(refs[at : at + n])
        at += n
    p_ref, outs = refs[at], refs[at + 1 :]
    q, k, v, g = (load_halves(info, refs, len(refs) == 3) for refs in operands)
    half = q[0].shape[0]

    def run(full):
        blocks = attention_blocks(full, cross, half)
        queries, sums = [], {}
        for s, keys, rows, cols in blocks:
            query = query_half(info, q, s)
            grad = query_half(info, g, s)
            key = jnp.concatenate([k[t] for t in keys], axis=0)
            value = jnp.concatenate([v[t] for t in keys], axis=0)
            dq, dk, dv = [], [], []
            for h in range(2):
                own = jnp.where(head_lanes(h), grad, jnp.zeros_like(grad))
                probs = p_ref[h, rows, cols]
                wide_probs = probs.astype(F32)
                grad_probs = dot_nt(own, value)
                delta = jnp.sum(wide_probs * grad_probs, axis=-1, keepdims=True)
                grad_scores = (wide_probs * (grad_probs - delta)).astype(BF16)
                dq.append(dot_nn(grad_scores, key))
                dk.append(dot_tn(grad_scores, query))
                dv.append(dot_tn(probs, grad))
            queries.append((jnp.where(head_lanes(0), dq[0], dq[1]) * SCORE_SCALE).astype(BF16))
            both = (jnp.where(head_lanes(0), dk[0], dk[1]), jnp.where(head_lanes(0), dv[0], dv[1]))
            sums[keys] = (sums[keys][0] + both[0], sums[keys][1] + both[1]) if keys in sums else both
        grads = []
        for t in range(2):
            dk, dv = (sums[(0, 1)] if full else sums[(t,)])
            rows = slice(t * half, (t + 1) * half) if full else slice(0, half)
            grads.append(((dk[rows] * SCORE_SCALE).astype(BF16), dv[rows].astype(BF16)))
        top, bottom = queries[0], queries[-1]
        if cross:
            outs[0][...] = top
            outs[1][...] = bottom
        parts = [(g0, g1) for g0, g1 in zip(*grads)]
        if not cross:
            parts = [(top, bottom)] + parts
        out_ref = outs[2] if cross else outs[0]
        for n, (first, second) in enumerate(parts):
            out_ref[n, :half, :] = first
            out_ref[n, half:, :] = second
            if part_b:
                outs[3 if cross else 1][n] = to_send(info, first, second)

    pl.when(info[FULL] != 0)(lambda: run(True))
    pl.when(info[FULL] == 0)(lambda: run(False))


def column_block(array, lead=None, row=0, column=0, rows=256):
    lanes = 2 * HEAD_DIM
    if array.ndim == 3:
        return (array, pl.BlockSpec((None, rows, lanes), lambda j, info: (lead, row, j + column)))
    return (array, pl.BlockSpec((rows, lanes), lambda j, info: (row, j + column)))


def halves_of(array, lead=None):
    return [column_block(array, lead, 0), column_block(array, lead, 1)]


def attend(info, group, operands, columns, rows=256):
    cross = group in (CROSS_A, CROSS_B)
    lanes = 2 * HEAD_DIM
    heads = columns // HEAD_DIM
    p_rows = rows if cross else 2 * rows
    half_out = ((rows, columns), BF16, pl.BlockSpec((rows, lanes), lambda j, info: (0, j)))
    mix_out = ((2 * rows, columns), BF16, pl.BlockSpec((2 * rows, lanes), lambda j, info: (0, j)))
    outs = [half_out, half_out] if cross else [mix_out] + ([half_out] if group == SELF_B else [])
    p_block = pl.BlockSpec((2, p_rows, 2 * rows), lambda j, info: (j, 0, 0))
    p_out = ((heads, p_rows, 2 * rows), BF16, p_block, True)
    return call(
        functools.partial(attend_kernel, group, [len(o) for o in operands]),
        info,
        heads // 2,
        sum(operands, []),
        outs + [p_out],
        [pltpu.VMEM((p_rows, 2 * rows), F32)],
        "attend",
        10,
        heads * 2 // 3,
    )


def attend_back(info, group, operands, probs, columns, rows=256):
    cross = group in (CROSS_A, CROSS_B)
    part_b = group in (SELF_B, CROSS_B)
    lanes = 2 * HEAD_DIM
    half_out = ((rows, columns), BF16, pl.BlockSpec((rows, lanes), lambda j, info: (0, j)))
    count = 2 if cross else 3

    def stacked(height):
        return ((count, height, columns), BF16, pl.BlockSpec((count, height, lanes), lambda j, info: (0, 0, j)))

    outs = [half_out, half_out] if cross else []
    outs = outs + [stacked(2 * rows)] + ([stacked(rows)] if part_b else [])
    p_block = pl.BlockSpec((2,) + probs.shape[1:], lambda j, info: (j, 0, 0))
    return call(
        functools.partial(attend_back_kernel, group, [len(o) for o in operands]),
        info,
        probs.shape[0] // 2,
        sum(operands, []) + [(probs, p_block)],
        outs,
        [],
        "attend_back",
        11,
        probs.shape[0],
    )


def first_project_kernel(info, a_ref, kept_ref, received_ref, norms_ref, w_ref, rows_ref, normed_ref, out_ref):
    @pl.when(pl.program_id(0) == 0)
    def _():
        rows = joined_rows(info, a_ref, kept_ref, received_ref)
        rows_ref[...] = rows
        normal, _ = norm_stats(rows.astype(F32))
        normed_ref[...] = (normal * norms_ref[0:1, :] + norms_ref[1:2, :]).astype(BF16)

    out_ref[...] = dot_nn(normed_ref[...], w_ref[...]).astype(BF16)


def first_project(info, tokens, received, norms, w_self):
    count, width, cols = w_self.shape
    rows = tokens.shape[1] + received.shape[0]
    return call(
        first_project_kernel,
        info,
        count,
        part_rows(tokens) + [whole_in(received), whole_in(norms), (w_self, lead_spec(width, cols))],
        [whole_out(rows, width), whole_out(rows, width), ((count, rows, cols), BF16, lead_spec(rows, cols))],
        [],
        "first_project",
        12,
        4,
    )


def other_project_kernel(info, normed_ref, own_b_ref, mine_ref, theirs_ref, out_ref, send_ref):
    weights = joined_pieces(info, mine_ref[...], theirs_ref[...], 0)
    out = dot_nn(normed_ref[...], weights).astype(BF16)
    out_ref[...] = out
    part_b = out.shape[0] - own_b_ref.shape[0]
    send_ref[...] = to_send(info, own_b_ref[...], out[part_b:])


def other_project(info, normed, qkv_own, mine, theirs, part_b):
    count, half, cols = mine.shape
    rows = normed.shape[0]
    own_b = pl.BlockSpec((None, part_b, cols), lambda j, info: (j, rows // part_b - 1, 0))
    return call(
        other_project_kernel,
        info,
        count,
        [whole_in(normed), (qkv_own, own_b), (mine, lead_spec(half, cols)), (theirs, lead_spec(half, cols))],
        [
            ((count, rows, cols), BF16, lead_spec(rows, cols)),
            ((count, part_b, cols), BF16, lead_spec(part_b, cols)),
        ],
        [],
        "other_project",
        9,
        3,
    )


def put_query_parts(info, value, far_ref, near_ref, left_ref, right_ref, send_ref):
    rows = left_ref.shape[0]
    cols = left_ref.shape[1]
    for h in range(2):
        at = slice(h * cols, (h + 1) * cols)
        far_ref[:, at] = value[h][:rows]
        near_ref[:, at] = value[h][rows : 2 * rows]
    left, right = value[0][2 * rows :], value[1][2 * rows :]
    left_ref[...] = left
    right_ref[...] = right
    send_ref[...] = to_send(info, left, right)


def query_outs(rows, width):
    whole, half = whole_out(rows, width), whole_out(rows, width // 2)
    return [whole, whole, half, half, half]


def self_mixes(info, mix0_ref, mix1_ref, slots_ref, received_ref):
    rows = received_ref.shape[0]
    parts = exchanged(info, TOP_BIG, slots_ref[:rows, :], slots_ref[rows:, :], received_ref[...])
    return [
        jnp.concatenate([ref[...], part], axis=0) for ref, part in zip((mix0_ref, mix1_ref), parts)
    ]


def second_project_kernel(
    info, rows_ref, norms_ref, mix0_ref, mix1_ref, slots_ref, received_ref, out_ref, query_ref, mine_ref, theirs_ref,
    hidden_ref, joined_ref, *query_refs,
):
    mixes = self_mixes(info, mix0_ref, mix1_ref, slots_ref, received_ref)
    other_out = joined_pieces(info, mine_ref[0], theirs_ref[0], 1)
    hidden = rows_ref[...].astype(F32) + dot_nn(mixes[0], out_ref[...]) + dot_nn(mixes[1], other_out)
    hidden_ref[...] = hidden
    normal, _ = norm_stats(hidden)
    joined = (normal * norms_ref[2:3, :] + norms_ref[3:4, :]).astype(BF16)
    joined_ref[...] = joined
    other_query = joined_pieces(info, mine_ref[1], theirs_ref[1], 0)
    queries = [dot_nn(joined, w).astype(BF16) for w in (query_ref[...], other_query)]
    put_query_parts(info, queries, *query_refs)


def second_project(info, rows, norms, mixes, w_self_out, w_query, mine, theirs, part_b):
    shape = rows.shape
    return call(
        second_project_kernel,
        info,
        1,
        [whole_in(a) for a in (rows, norms, *mixes, w_self_out, w_query, mine, theirs)],
        [whole_out(*shape, kind=F32), whole_out(*shape)] + query_outs(part_b, shape[1]),
        [],
        "second_project",
        17,
        5,
    )


def offer_project_kernel(info, rows_ref, own_ref, mine_ref, theirs_ref, out_ref, send_ref):
    cols = own_ref.shape[1]
    rows = send_ref.shape[0]
    other = joined_pieces(info, mine_ref[...], theirs_ref[...], 0)
    parts = [dot_nn(rows_ref[...], w).astype(BF16) for w in (own_ref[...], other)]
    for h in range(2):
        out_ref[:, h * cols : (h + 1) * cols] = parts[h]
    send_ref[...] = to_send(info, parts[0][-rows:], parts[1][-rows:])


def offer_project(info, joined, w_offer, mine, theirs, part_b):
    count, width, cols = w_offer.shape
    rows = joined.shape[0]
    piece = lead_spec(cols, cols)
    return call(
        offer_project_kernel,
        info,
        count,
        [whole_in(joined), (w_offer, lead_spec(width, cols)), (mine, piece), (theirs, piece)],
        [
            ((count, rows, 2 * cols), BF16, lead_spec(rows, 2 * cols)),
            ((count, part_b, cols), BF16, lead_spec(part_b, cols)),
        ],
        [],
        "offer_project",
        9,
        4,
    )


def reader_rows(info, far_ref, near_ref, far_b_ref, near_b_ref, received_ref):
    half = far_b_ref.shape[1]
    parts = exchanged(info, TOP_MID, far_b_ref[...], near_b_ref[...], received_ref[...])
    return [
        jnp.concatenate([ref[:, h * half : (h + 1) * half] for ref in (far_ref, near_ref)] + [parts[h]], axis=0)
        for h in range(2)
    ]


def mlp_kernel(
    info, hidden_ref, norms_ref, far_ref, near_ref, far_b_ref, near_b_ref, received_ref, w_cross_ref, mine_ref,
    theirs_ref, grad_a_ref, grad_kept_ref, grad_received_ref, up_ref, down_ref, result_ref, grad_second_ref, gm_far_ref, gm_near_ref, gm_left_ref, gm_right_ref,
    gm_send_ref, up_keep_ref, up_send_ref, down_keep_ref, down_send_ref, keep_ref, send_ref, g_norms_ref, second_ref,
    rows_ref, grad_ref, sum_ref, back_ref,
):
    step = pl.program_id(0)

    def mixes():
        return reader_rows(info, far_ref, near_ref, far_b_ref, near_b_ref, received_ref)

    def cross_weights():
        return w_cross_ref[...], joined_pieces(info, mine_ref[...], theirs_ref[...], 1)

    @pl.when(step == 0)
    def _():
        grad_ref[...] = joined_rows(info, grad_a_ref, grad_kept_ref, grad_received_ref)
        second = hidden_ref[...]
        for mix, weight in zip(mixes(), cross_weights()):
            second = second + dot_nn(mix, weight)
        second_ref[...] = second
        normal, _ = norm_stats(second)
        rows_ref[...] = (normal * norms_ref[4:5, :] + norms_ref[5:6, :]).astype(BF16)
        sum_ref[...] = second
        back_ref[...] = jnp.zeros_like(back_ref)

    rows, grad, up, down = rows_ref[...], grad_ref[...], up_ref[...], down_ref[...]
    pre = dot_nn(rows, up)
    spread = lax.erf(pre * 0.7071067811865476) * 0.5 + 0.5
    slope = spread + pre * (jnp.exp(pre * pre * -0.5) * 0.3989422804014327)
    activated = (pre * spread).astype(BF16)
    grad_up = (dot_nt(grad, down) * slope).astype(BF16)
    sum_ref[...] += dot_nn(activated, down)
    back_ref[...] += dot_nt(grad_up, up)
    g_up = dot_tn(rows, grad_up).astype(BF16)
    g_down = dot_tn(activated, grad).astype(BF16)

    @pl.when(step < 2)
    def _():
        up_keep_ref[...] = g_up
        down_keep_ref[...] = g_down

    @pl.when(step >= 2)
    def _():
        up_send_ref[...] = g_up
        down_send_ref[...] = g_down

    @pl.when(step == 3)
    def _():
        result_ref[...] = sum_ref[...].astype(BF16)
        normal, inverse = norm_stats(second_ref[...])
        back, gain, shift = norm_back(back_ref[...], normal, inverse, norms_ref[4:5, :])
        g_norms_ref[0:1, :] = gain
        g_norms_ref[1:2, :] = shift
        grad_second = grad_ref[...].astype(F32) + back
        grad_second_ref[...] = grad_second
        rounded = grad_second.astype(BF16)
        parts = []
        for h, (mix, weight) in enumerate(zip(mixes(), cross_weights())):
            parts.append(dot_nt(rounded, weight).astype(BF16))
            put_pieces(info, keep_ref, send_ref, h, dot_tn(mix, rounded), 1)
        put_query_parts(info, parts, gm_far_ref, gm_near_ref, gm_left_ref, gm_right_ref, gm_send_ref)


def mlp(info, hidden, norms, mixes, w_cross, mine, theirs, cotangent, received, up, down):
    rows, width = hidden.shape
    half = width // 2
    part_b = received.shape[0]

    def pieces(index):
        return ((2, width, width), BF16, pl.BlockSpec((None, width, width), lambda j, info: (index(j), 0, 0)))

    keep, send = pieces(lambda j: jnp.minimum(j, 1)), pieces(lambda j: jnp.maximum(j - 2, 0))
    wide = pltpu.VMEM((rows, width), F32)
    narrow = pltpu.VMEM((rows, width), BF16)
    return call(
        mlp_kernel,
        info,
        4,
        [whole_in(a) for a in (hidden, norms, *mixes, w_cross)]
        + [whole_in(mine), whole_in(theirs)]
        + part_rows(cotangent)
        + [whole_in(received), (up, lead_spec(width, width)), (down, lead_spec(width, width))],
        [whole_out(rows, width), whole_out(rows, width, kind=F32)]
        + query_outs(part_b, width)
        + [keep, send, keep, send, whole_out(2, half, half), whole_out(2, half, half)]
        + [whole_out(2, width, kind=F32)],
        [wide, narrow, narrow, wide, wide],
        "mlp",
        46,
        34,
    )


def second_back_kernel(
    info, far_ref, near_ref, far_b_ref, near_b_ref, received_ref, dkv_ref, slots_ref, slots_received_ref, joined_ref,
    hidden_ref, grad_second_ref, norms_ref, offer_ref, offer_mine_ref, offer_theirs_ref, query_ref, out_ref, mine_ref,
    theirs_ref, mix0_ref, mix1_ref, mix_slots_ref, mix_received_ref, cross_keep_ref, cross_send_ref, grad_hidden_ref,
    grad_mix_ref, mix_send_ref, keep_ref, send_ref, g_norms_ref, back_ref,
):
    step = pl.program_id(0)
    half = query_ref.shape[1]
    rows = received_ref.shape[0]

    def add(at, grads, weights, first):
        joined = joined_ref[...]
        total = dot_nt(grads[0], weights[0]) + dot_nt(grads[1], weights[1])
        back_ref[...] = total if first else back_ref[...] + total
        for h in range(2):
            put_pieces(info, keep_ref, send_ref, (h, at), dot_tn(joined, grads[h]), 0)

    def add_offer(at):
        parts = exchanged(info, TOP_BIG, slots_ref[:rows, :], slots_ref[rows:, :], slots_received_ref[...])
        grads = [
            jnp.concatenate([dkv_ref[:, h * half : (h + 1) * half], parts[h]], axis=0) for h in range(2)
        ]
        other = joined_pieces(info, offer_mine_ref[...], offer_theirs_ref[...], 0)
        add(at, grads, (offer_ref[...], other), at == 0)

    pl.when(step == 0)(lambda: add_offer(0))
    pl.when(step == 1)(lambda: add_offer(1))

    @pl.when(step == 2)
    def _():
        for h in range(2):
            keep_ref[h, 4] = cross_keep_ref[h]
            send_ref[h, 4] = cross_send_ref[h]
        grads = reader_rows(info, far_ref, near_ref, far_b_ref, near_b_ref, received_ref)
        add(2, grads, (query_ref[...], joined_pieces(info, mine_ref[1], theirs_ref[1], 0)), False)
        normal, inverse = norm_stats(hidden_ref[...])
        back, gain, shift = norm_back(back_ref[...], normal, inverse, norms_ref[2:3, :])
        g_norms_ref[0:1, :] = gain
        g_norms_ref[1:2, :] = shift
        grad_hidden = grad_second_ref[...] + back
        grad_hidden_ref[...] = grad_hidden
        rounded = grad_hidden.astype(BF16)
        mixes = self_mixes(info, mix0_ref, mix1_ref, mix_slots_ref, mix_received_ref)
        parts = []
        for h, weight in enumerate((out_ref[...], joined_pieces(info, mine_ref[0], theirs_ref[0], 1))):
            part = dot_nt(rounded, weight).astype(BF16)
            grad_mix_ref[h] = part
            parts.append(part[-rows:])
            put_pieces(info, keep_ref, send_ref, (h, 3), dot_tn(mixes[h], rounded), 1)
        mix_send_ref[...] = to_send(info, *parts)


def second_back(
    info, grad_q, dkv, slots, slots_received, joined, hidden, grad_second, norms, w_offer, offer_mine, offer_theirs,
    w_query, w_self_out, mine, theirs, mixes, cross_keep, cross_send,
):
    rows, width = hidden.shape
    half = width // 2
    part_b = slots_received.shape[1]

    def offered(array, *shape):
        return (array, pl.BlockSpec((None,) + shape, lambda j, info: (jnp.minimum(j, 1), 0, 0)))

    return call(
        second_back_kernel,
        info,
        3,
        [whole_in(a) for a in grad_q]
        + [offered(dkv, *dkv.shape[1:]), offered(slots, *slots.shape[1:])]
        + [offered(slots_received, *slots_received.shape[1:])]
        + [whole_in(a) for a in (joined, hidden, grad_second, norms)]
        + [offered(w_offer, width, half), offered(offer_mine, half, half), offered(offer_theirs, half, half)]
        + [whole_in(a) for a in (w_query, w_self_out, mine, theirs, *mixes, cross_keep, cross_send)],
        [whole_out(rows, width, kind=F32), whole_out(2, rows, half), whole_out(part_b, half)]
        + [whole_out(2, 5, half, half), whole_out(2, 5, half, half), whole_out(2, width, kind=F32)],
        [pltpu.VMEM((rows, width), F32)],
        "second_back",
        35,
        12,
    )


def first_back_kernel(
    info, own_ref, other_ref, slots_ref, received_ref, rows_ref, normed_ref, grad_hidden_ref, norms_ref, w_own_ref,
    mine_ref, theirs_ref, grad_rows_ref, keep_ref, send_ref, g_norms_ref, back_ref,
):
    step = pl.program_id(0)
    rows = received_ref.shape[0]
    parts = exchanged(info, TOP_BIG, slots_ref[:rows, :], slots_ref[rows:, :], received_ref[...])
    grads = [jnp.concatenate([ref[...], part], axis=0) for ref, part in zip((own_ref, other_ref), parts)]
    normed = normed_ref[...]
    for h in range(2):
        put_pieces(info, keep_ref, send_ref, (h, step), dot_tn(normed, grads[h]), 0)
    other = joined_pieces(info, mine_ref[...], theirs_ref[...], 0)
    total = dot_nt(grads[0], w_own_ref[...]) + dot_nt(grads[1], other)

    @pl.when(step == 0)
    def _():
        back_ref[...] = total

    @pl.when(step > 0)
    def _():
        back_ref[...] += total

    @pl.when(step == pl.num_programs(0) - 1)
    def _():
        normal, inverse = norm_stats(rows_ref[...].astype(F32))
        back, gain, shift = norm_back(back_ref[...], normal, inverse, norms_ref[0:1, :])
        g_norms_ref[0:1, :] = gain
        g_norms_ref[1:2, :] = shift
        grad_rows_ref[...] = (grad_hidden_ref[...] + back).astype(BF16)


def first_back(info, own, other, slots, received, rows, normed, grad_hidden, norms, w_self, mine, theirs):
    count, half = own.shape[0], own.shape[2]
    width = rows.shape[1]
    ins = [(a, lead_spec(*a.shape[1:])) for a in (own, other, slots, received)]
    ins += [whole_in(a) for a in (rows, normed, grad_hidden, norms)]
    ins += [(a, lead_spec(*a.shape[1:])) for a in (w_self, mine, theirs)]
    pieces = whole_out(2, count, half, half)
    return call(
        first_back_kernel,
        info,
        count,
        ins,
        [whole_out(*rows.shape), pieces, pieces, whole_out(2, width, kind=F32)],
        [pltpu.VMEM(rows.shape, F32)],
        "first_back",
        24,
        11,
    )


def row_of(table, index):
    return lax.dynamic_index_in_dim(table, index, 0, keepdims=False)


def scalars(clip_len, index, across, quarter):
    core = index % 2
    is_big = index < 2 * quarter
    is_mid = jnp.logical_and(index >= 2 * quarter, index < 3 * quarter)
    first, last = core == 0, core == 1
    flags = [
        is_big,
        core,
        across,
        jnp.logical_and(is_big, index >= quarter),
        jnp.logical_and(is_big, last),
        jnp.logical_and(is_big, first),
        jnp.logical_and(is_mid, last),
        jnp.logical_and(is_mid, first),
    ]
    shared = index - core + across
    lens_a, lens_b = row_of(clip_len, across), clip_len[2]
    big_a = row_of(lens_a, jnp.minimum(index, 2 * quarter - 1))
    big_b = row_of(lens_b, jnp.minimum(shared, 2 * quarter - 1))
    sets_a = [row_of(lens_a, index % quarter + s * quarter) for s in range(2)]
    sets_b = [row_of(lens_b, shared % quarter + core * quarter)] * 2
    table = jnp.stack(
        [2 * big_a, 2 * big_a, *sets_a, 2 * big_b, 2 * big_b, *sets_b]
        + [big_a, 2 * big_a, *sets_a, big_b, 2 * big_b, *sets_b]
    )
    ends = [table[:, 0]]
    for k in range(1, 4):
        ends.append(ends[-1] + table[:, k])
    flags = jnp.stack([flag.astype(jnp.int32) for flag in flags])
    return jnp.concatenate([flags, jnp.stack(ends, axis=1).reshape(-1)])


def local(
    tokens,
    cotangent,
    clip_len,
    ln_params,
    w_self,
    w_self_out,
    w_offer,
    w_query,
    w_cross_out,
    w_up,
    w_down,
):
    index = lax.axis_index("clip")
    across = lax.axis_index("head")
    count = lax.axis_size("clip")
    quarter = count // 4
    levels = (2 * quarter).bit_length() - 1
    core = index % 2
    is_big = index < 2 * quarter
    is_mid = jnp.logical_and(index >= 2 * quarter, index < 3 * quarter)
    own_micro2 = core == across
    norms = ln_params[0]
    w_self, w_self_out, w_offer, w_query = w_self[0], w_self_out[0], w_offer[0], w_query[0]
    w_cross_out, w_up, w_down = w_cross_out[0], w_up[0], w_down[0]
    half = w_query.shape[1]
    part_a = tokens.shape[1]
    part_b = part_a // 2
    wide = 2 * half

    near = [(i, i - quarter) for i in range(2 * quarter, count)]
    far = [(i, i - 2 * quarter) for i in range(2 * quarter, 3 * quarter)]
    far += [(i, i - quarter) for i in range(3 * quarter, count)]

    def to_server(far_rows, near_rows):
        second = lax.ppermute(near_rows, "clip", near)
        return lax.ppermute(far_rows, "clip", far), second

    def to_reader(far_rows, near_rows):
        second = lax.ppermute(near_rows, "clip", [(b, a) for a, b in near])
        return lax.ppermute(far_rows, "clip", [(b, a) for a, b in far]), second

    def reader_slots(left, right, received):
        top = jnp.where(jnp.logical_and(is_mid, core == 1), received, left)
        return top, jnp.where(jnp.logical_and(is_mid, core == 0), received, right)

    def from_server(top, bottom):
        return top, bottom, other_core(jnp.where(core == 0, bottom, top))

    def over_level(part, bit):
        return over_bit(part, bit, 2 * quarter if bit == levels - 1 else None)

    def add(left, right):
        return (left.astype(F32) + right.astype(F32)).astype(BF16)

    def last_levels(total, received):
        total = add(total, received)
        for bit in range(3, levels):
            total = add(total, over_level(total, bit))
        return total

    def all_rows(mine, a_theirs, b_theirs):
        a_mine, b_mine = mine[:part_a], mine[part_a:]
        kept = jnp.where(own_micro2, b_mine, b_theirs)
        received = other_core(jnp.where(own_micro2, b_theirs, b_mine))
        micro2 = in_core_order(core, kept, received, 0)
        micro0 = jnp.where(across == 0, a_mine, a_theirs)
        micro1 = jnp.where(across == 0, a_theirs, a_mine)
        return jnp.stack([micro0, micro1, micro2])


    def over_head_rows(array, start, stop, *others):
        return over_head(after(array[start:stop], *others) if others else array[start:stop])

    self_mine = over_head(core_piece(w_self, core, 1))
    tokens_received = other_core(core_piece(tokens[2], 1 - core, 0))
    info = scalars(clip_len, index, across, quarter)
    rows, normed, qkv_own = first_project(info, tokens, tokens_received, norms, w_self)
    self_0 = [halves_of(qkv_own, n) for n in range(3)]
    mix_0, p_0 = attend(info, SELF_A, self_0, half)
    first_piece = jnp.stack([core_piece(w_self_out, core, 1), core_piece(w_query, core, 0)])
    offer_piece, up_piece, down_piece = core_piece(w_offer, core, 1), core_piece(w_up, core, 1), core_piece(w_down, core, 0)
    cross_piece = core_piece(w_cross_out, core, 1)
    (self_mine, mix_0, first_piece) = fence(self_mine, mix_0, first_piece)

    first_mine = over_head(first_piece)
    self_theirs = other_core(self_mine)
    qkv_other, qkv_send = other_project(info, normed, qkv_own, self_mine, self_theirs, part_b)
    self_1 = [halves_of(qkv_other, n) for n in range(3)]
    mix_1, p_1 = attend(info, SELF_A, self_1, half)
    qkv_received, first_mine, mix_1, offer_piece = fence(other_core(qkv_send), first_mine, mix_1, offer_piece)

    offer_mine = over_head(offer_piece)
    self_b = [
        [column_block(qkv_own, n, 2), column_block(qkv_other, n, 2), column_block(qkv_received, n)] for n in range(3)
    ]
    mix_s, mix_send, p_s = attend(info, SELF_B, self_b, half)
    first_theirs = other_core(first_mine)
    mixes = (mix_0, mix_1, mix_s, other_core(mix_send))
    hidden, joined, q_far, q_near, q_left, q_right, q_send = second_project(
        info, rows, norms, mixes, w_self_out, w_query, first_mine, first_theirs, part_b
    )
    q_far, q_near, q_top, q_bottom, joined, offer_mine, cross_piece, up_piece, down_piece, cotangent = fence(
        q_far, q_near, *reader_slots(q_left, q_right, other_core(q_send)), joined, offer_mine, cross_piece, up_piece,
        down_piece, cotangent,
    )

    up_mine = over_head(up_piece)
    asked_a = to_server(q_far, q_near)
    asked_b = to_server(q_top, q_bottom)
    offer_theirs = other_core(offer_mine)
    offer, offer_send = offer_project(info, joined, w_offer, offer_mine, offer_theirs, part_b)
    cotangent_received = other_core(core_piece(cotangent[2], 1 - core, 0))
    offer_received = other_core(offer_send)
    *asked_a, asked_b_far, asked_b_near, offer_received, cotangent_received, up_mine, down_piece, cross_piece = fence(
        *asked_a, *asked_b, offer_received, cotangent_received, up_mine, down_piece, cross_piece
    )

    down_mine = [over_head(down_piece[:320])]
    cross_a = [[column_block(asked_a[0]), column_block(asked_a[1])]] + [halves_of(offer, n) for n in range(2)]
    far_a, near_a, cross_p_a = attend(info, CROSS_A, cross_a, wide)
    far_a, near_a, asked_b_far, asked_b_near, up_mine, down_mine[0], down_piece, cross_piece = fence(
        far_a, near_a, asked_b_far, asked_b_near, up_mine, down_mine[0], down_piece, cross_piece
    )

    back_a = to_reader(far_a, near_a)
    down_mine.append(over_head(down_piece[320:]))
    cross_mine = over_head(cross_piece)
    cross_b = [[column_block(asked_b_far), column_block(asked_b_near)]] + [
        [
            column_block(offer, n, 2),
            column_block(offer, n, 2, half // (2 * HEAD_DIM)),
            column_block(offer_received, n),
        ]
        for n in range(2)
    ]
    far_b, near_b, cross_p_b = attend(info, CROSS_B, cross_b, half)
    up_theirs = other_core(up_mine)
    *back_a, far_b, near_b, cross_mine, up_mine, up_theirs, down_mine[1] = fence(
        *back_a, far_b, near_b, cross_mine, up_mine, up_theirs, down_mine[1]
    )

    back_b = from_server(*to_reader(far_b, near_b))
    down_mine = jnp.concatenate(down_mine)
    down_theirs = other_core(down_mine)
    cross_theirs = other_core(cross_mine)
    up_pieces = jnp.stack([core_piece(w_up, core, 1), up_mine, core_piece(w_up, 1 - core, 1), up_theirs])
    down_pieces = jnp.stack([core_piece(w_down, core, 0), down_mine, core_piece(w_down, 1 - core, 0), down_theirs])

    (
        result, grad_second, gm_far, gm_near, gm_left, gm_right, gm_send,
        up_keep, up_send, down_keep, down_send, cross_keep, cross_send, norms_3,
    ) = mlp(
        info, hidden, norms, (*back_a, *back_b), w_cross_out, cross_mine, cross_theirs, cotangent, cotangent_received,
        up_pieces, down_pieces,
    )

    gm_far, gm_near, gm_top, gm_bottom, result, down_send, up_send = fence(
        gm_far, gm_near, *reader_slots(gm_left, gm_right, other_core(gm_send)), result, down_send, up_send
    )

    grad_a = to_server(gm_far, gm_near)
    grad_b = to_server(gm_top, gm_bottom)
    layer_x = over_head(result)
    down = add(down_keep, other_core(down_send))
    up = add(up_keep, other_core(up_send))
    *grad_a, grad_b_far, grad_b_near, layer_x, down, up = fence(*grad_a, *grad_b, layer_x, down, up)

    down_x = [over_head(down[1, :384])]
    grad_in = [column_block(grad_a[0]), column_block(grad_a[1])]
    dq_far, dq_near, dkv_a = attend_back(info, CROSS_A, cross_a + [grad_in], cross_p_a, wide)
    dq_far, dq_near, grad_b_far, grad_b_near, down_x[0], down, up = fence(
        dq_far, dq_near, grad_b_far, grad_b_near, down_x[0], down, up
    )

    dq_a = to_reader(dq_far, dq_near)
    down_x.append(over_head(down[1, 384:]))
    up_x = [over_head(up[1, :128])]
    grad_in = [column_block(grad_b_far), column_block(grad_b_near)]
    dq_b_far, dq_b_near, dkv_b, dkv_send = attend_back(info, CROSS_B, cross_b + [grad_in], cross_p_b, half)
    *dq_a, dq_b_far, dq_b_near, down_x[1], up_x[0], up = fence(*dq_a, dq_b_far, dq_b_near, down_x[1], up_x[0], up)

    dq_b = from_server(*to_reader(dq_b_far, dq_b_near))
    dkv_received = other_core(dkv_send)
    up_x.append(over_head(up[1, 128:448]))
    down_total = add(down[0], jnp.concatenate(down_x))
    down_y = [over_level(down_total[:384], 1)]
    *dq_b, dkv_received, up_x[1], down_total, up, down_y[0] = fence(
        *dq_b, dkv_received, up_x[1], down_total, up, down_y[0]
    )

    up_x.append(over_head(up[1, 448:]))
    down_y.append(over_level(down_total[384:], 1))
    grad_hidden, grad_mix, grad_send, mid_keep, mid_send, norms_2 = second_back(
        info, (*dq_a, *dq_b), dkv_a, dkv_b, dkv_received, joined, hidden, grad_second, norms, w_offer,
        offer_mine, offer_theirs, w_query, w_self_out, first_mine, first_theirs, mixes, cross_keep, cross_send,
    )
    grad_hidden, grad_mix, grad_send, mid_keep, mid_send, up_x[2], up, down_total, down_y[1] = fence(
        grad_hidden, grad_mix, grad_send, mid_keep, mid_send, up_x[2], up, down_total, down_y[1]
    )

    mid = add(mid_keep, other_core(mid_send))
    grad_in = [column_block(grad_mix, 0, 2), column_block(grad_mix, 1, 2), column_block(other_core(grad_send))]
    (back_0,) = attend_back(info, SELF_A, self_0 + [halves_of(grad_mix, 0)], p_0, half)
    back_s, back_send = attend_back(info, SELF_B, self_b + [grad_in], p_s, half)
    up_total = add(up[0], jnp.concatenate(up_x))
    up_y = over_level(up_total, 1)
    down_total = add(down_total, jnp.concatenate(down_y))
    down_z = over_level(down_total, 2)
    back_0, back_s, back_send, mid, up_total, grad_mix, up_y, down_total, down_z = fence(
        back_0, back_s, back_send, mid, up_total, grad_mix, up_y, down_total, down_z
    )

    mid_x = [over_head(mid[1, :1])]
    up_total = add(up_total, up_y)
    up_z = over_level(up_total, 2)
    back_received = other_core(back_send)
    (back_1,) = attend_back(info, SELF_A, self_1 + [halves_of(grad_mix, 1)], p_1, half)
    back_1, back_received, mid_x[0], mid = fence(back_1, back_received, mid_x[0], mid)

    mid_x.append(over_head(mid[1, 1:3]))
    mid_total = [add(mid[0, :1], mid_x[0])]
    mid_y = [over_level(mid_total[0], 1)]
    grad_rows, self_keep, self_send, norms_1 = first_back(
        info, back_0, back_1, back_s, back_received, rows, normed, grad_hidden, norms, w_self, self_mine, self_theirs
    )
    grad_rows, self_keep, self_send, mid_x[1], mid, mid_y[0], mid_total[0], up_z = fence(
        grad_rows, self_keep, self_send, mid_x[1], mid, mid_y[0], mid_total[0], up_z
    )

    mid_x.append(over_head(mid[1, 3:]))
    mid_total.append(add(mid[0, 1:3], mid_x[1]))
    mid_y.append(over_level(mid_total[1], 1))
    mid_total[0] = add(mid_total[0], mid_y[0])
    mid_z = [over_level(mid_total[0], 2)]
    norm_grads = jnp.concatenate([norms_1, norms_2, norms_3, jnp.zeros((2, wide), F32)], axis=0)
    norm_grads = norm_grads.reshape(-1, half).astype(BF16)
    norm_grads = add(norm_grads, other_core(norm_grads))
    last = add(self_keep, other_core(self_send))
    last, norm_grads, mid_x[2], mid, grad_rows, mid_y[1], mid_total[1], mid_z[0] = fence(
        last, norm_grads, mid_x[2], mid, grad_rows, mid_y[1], mid_total[1], mid_z[0]
    )

    end = jnp.concatenate([last[:, 2], jnp.stack([norm_grads, norm_grads])], axis=1)
    last_x = over_head(last[1, :2])
    mid_total.append(add(mid[0, 3:], mid_x[2]))
    mid_y.append(over_level(mid_total[2], 1))
    mid_total[1] = add(mid_total[1], mid_y[1])
    mid_z.append(over_level(mid_total[1], 2))
    layer_x = after(layer_x, last)
    layer_out = all_rows(result, layer_x[:part_a], layer_x[part_a:])
    last_x, last, end, grad_rows, mid_y[2], mid_total[2], mid_z[1] = fence(
        last_x, last, end, grad_rows, mid_y[2], mid_total[2], mid_z[1]
    )

    end_x = over_head(end[1])
    rows_b_x = over_head(grad_rows[part_a:])
    last_total = add(last[0, :2], last_x)
    last_y = over_level(last_total, 1)
    mid_total[2] = add(mid_total[2], mid_y[2])
    mid_z.append(over_level(mid_total[2], 2))
    last_total, last_y, end_x, rows_b_x, grad_rows, end, mid_z[2] = fence(
        last_total, last_y, end_x, rows_b_x, grad_rows, end, mid_z[2]
    )

    rows_a_x = over_head(grad_rows[:part_a])
    end_total = add(end[0], end_x)
    end_total = add(end_total, over_level(end_total, 1))
    last_total = add(last_total, last_y)
    end_total = last_levels(end_total, over_level(end_total, 2))
    last_total = last_levels(last_total, over_level(last_total, 2))
    down_total = last_levels(down_total, down_z)
    up_total = last_levels(up_total, up_z)
    mid_total = [n for total, received in zip(mid_total, mid_z) for n in last_levels(total, received)]
    norms_total = end_total[half:].reshape(-1, wide)[:6]

    def whole(mine, axis):
        return in_core_order(core, mine, other_core(mine), axis).astype(F32)[None]

    return (
        layer_out,
        all_rows(grad_rows, rows_a_x, rows_b_x).astype(F32),
        norms_total.astype(F32)[None],
        whole(jnp.concatenate([last_total, end_total[None, :half]]), 1),
        whole(mid_total[3], 1),
        whole(jnp.stack(mid_total[:2]), 1),
        whole(mid_total[2], 0),
        whole(mid_total[4], 1),
        whole(up_total, 1),
        whole(down_total, 0),
    )


def solution(mesh):
    return jax.shard_map(
        local,
        mesh=mesh,
        in_specs=(
            P(None, "clip", None),
            P(None, "clip", None),
            P(),
            P("clip", None, None),
            P("clip", None, None, "head"),
            P("clip", "head", None),
            P("clip", None, None, "head"),
            P("clip", None, "head"),
            P("clip", "head", None),
            P("clip", None, "head"),
            P("clip", "head", None),
        ),
        out_specs=(
            P(None, "clip", None),
            P(None, "clip", None),
            P("clip", None, None),
            P("clip", None, None, "head"),
            P("clip", "head", None),
            P("clip", None, None, "head"),
            P("clip", None, "head"),
            P("clip", "head", None),
            P("clip", None, "head"),
            P("clip", "head", None),
        ),
        check_vma=False,
    )
```

```python
import functools

import jax
import jax.numpy as jnp
from jax import lax
from jax.experimental import pallas as pl
from jax.experimental.pallas import tpu as pltpu
from jax.sharding import PartitionSpec as P


HEAD_DIM = 64
EPSILON = 1e-06
SCORE_SCALE = 0.125
MASKED = -1e30
BF16 = jnp.bfloat16
F32 = jnp.float32
COST_BYTES = 1

FULL, CORE, ACROSS, SECOND_PLANE, TOP_BIG, BOTTOM_BIG, TOP_MID, BOTTOM_MID, ENDS = range(9)
SELF_A, SELF_B, CROSS_A, CROSS_B = range(4)


def over_head(value):
    return lax.ppermute(value, "head", [(0, 1), (1, 0)])


def over_bit(value, bit, count=None):
    count = lax.axis_size("clip") if count is None else count
    return lax.ppermute(value, "clip", [(i, i ^ (1 << bit)) for i in range(count)])


def other_core(value):
    return over_bit(value, 0)


def fence(*values):
    return lax.optimization_barrier(values)


def after(value, *others):
    return lax.optimization_barrier((value,) + others)[0]


def in_core_order(core, mine, theirs, axis):
    first = jnp.where(core == 0, mine, theirs)
    second = jnp.where(core == 0, theirs, mine)
    return jnp.concatenate([first, second], axis=axis)


def core_piece(value, piece, axis):
    size = value.shape[axis] // 2
    return lax.dynamic_slice_in_dim(value, piece * size, size, axis)


def dot_nt(left, right):
    return lax.dot_general(left, right, (((1,), (1,)), ((), ())), preferred_element_type=F32)


def dot_tn(left, right):
    return lax.dot_general(left, right, (((0,), (0,)), ((), ())), preferred_element_type=F32)


def dot_nn(left, right):
    return jnp.dot(left, right, preferred_element_type=F32)


def norm_stats(rows):
    mean = jnp.mean(rows, axis=-1, keepdims=True)
    centered = rows - mean
    variance = jnp.mean(centered * centered, axis=-1, keepdims=True)
    inverse = lax.rsqrt(variance + EPSILON)
    return centered * inverse, inverse


def norm_back(grad, normal, inverse, gain):
    scaled = grad * gain
    mean = jnp.mean(scaled, axis=-1, keepdims=True)
    along = jnp.mean(scaled * normal, axis=-1, keepdims=True)
    grad_rows = (scaled - mean - normal * along) * inverse
    gain_grad = jnp.sum(grad * normal, axis=0, keepdims=True)
    return grad_rows, gain_grad, jnp.sum(grad, axis=0, keepdims=True)


def pick(info, flag, yes, no):
    return jnp.where(info[flag] != 0, yes, no)


def core_order(info, mine, theirs):
    return pick(info, CORE, theirs, mine), pick(info, CORE, mine, theirs)


def joined_pieces(info, mine, theirs, axis):
    return jnp.concatenate(core_order(info, mine, theirs), axis=axis)


def exchanged(info, top_flag, first, second, received):
    return pick(info, top_flag, received, first), pick(info, top_flag + 1, received, second)


def to_send(info, first, second):
    return pick(info, CORE, first, second)


def put_pieces(info, keep_ref, send_ref, at, value, axis):
    size = value.shape[axis] // 2
    low, high = (value[:size], value[size:]) if axis == 0 else (value[:, :size], value[:, size:])
    mine, theirs = core_order(info, low.astype(BF16), high.astype(BF16))
    keep_ref[at] = mine
    send_ref[at] = theirs


def resident(shape, index=None):
    index = (lambda j, info: (0,) * len(shape)) if index is None else index
    return pl.BlockSpec(shape, index, pipeline_mode=pl.Buffered(1))


def whole_in(array):
    return (array, resident(array.shape))


def whole_out(*shape, kind=BF16, in_hbm=False):
    return (shape, kind, resident(shape), in_hbm)


def from_hbm(array):
    return pltpu.with_memory_space_constraint(array, pltpu.HBM)


def lead_spec(*shape):
    return pl.BlockSpec((None,) + shape, lambda j, info: (j,) + (0,) * len(shape))


def out_type(shape, kind, spec, in_hbm=False):
    return pltpu.HBM(shape, kind) if in_hbm else jax.ShapeDtypeStruct(shape, kind)


def call(kernel, info, steps, ins, outs, scratch, name, mebibytes, cost):
    return pl.pallas_call(
        kernel,
        grid_spec=pltpu.PrefetchScalarGridSpec(
            num_scalar_prefetch=1,
            grid=(steps,),
            in_specs=[spec for _, spec in ins],
            out_specs=[out[2] for out in outs],
            scratch_shapes=scratch,
        ),
        out_shape=[out_type(*out) for out in outs],
        compiler_params=pltpu.CompilerParams(vmem_limit_bytes=mebibytes * 1024 * 1024),
        cost_estimate=pl.CostEstimate(flops=0, bytes_accessed=cost * COST_BYTES, transcendentals=0),
        name=name,
    )(info, *[array for array, _ in ins])


def part_rows(array):
    _, count, width = array.shape
    return [
        (array, resident((None, count, width), lambda j, info: (info[ACROSS], 0, 0))),
        (array, resident((None, count // 2, width), lambda j, info: (2, info[CORE], 0))),
    ]


def joined_rows(info, a_ref, kept_ref, received_ref):
    own = info[CORE] == info[ACROSS]
    return jnp.concatenate([a_ref[...], jnp.where(own, kept_ref[...], received_ref[...])], axis=0)


def clip_bias(info, group, rows, cols, row_kind, col_kind):
    def clips(kind, places, shape, axis):
        base = ENDS + 16 * group + 4 * kind
        place = lax.broadcasted_iota(jnp.int32, shape, axis) + places.start
        return sum((place >= info[base + k]).astype(jnp.int32) for k in range(4))

    of_rows = clips(row_kind, rows, (rows.stop - rows.start, 128), 0)[:, :1]
    of_cols = clips(col_kind, cols, (8, cols.stop - cols.start), 1)[:1, :]
    return jnp.where(of_rows == of_cols, 0.0, MASKED)


def attention_blocks(full, cross, half):
    if full and cross:
        return [(None, (0, 1), slice(0, half), slice(0, 2 * half))]
    if full:
        return [(s, (0, 1), slice(s * half, (s + 1) * half), slice(0, 2 * half)) for s in range(2)]
    if cross:
        return [(s, (s,), slice(0, half), slice(s * half, (s + 1) * half)) for s in range(2)]
    return [(s, (s,), slice(s * half, (s + 1) * half), slice(0, half)) for s in range(2)]


def load_halves(info, refs, exchange):
    first, second = refs[0][...], refs[1][...]
    if exchange:
        first, second = exchanged(info, TOP_BIG, first, second, refs[2][...])
    return first, second


def query_half(info, halves, s):
    return pick(info, SECOND_PLANE, halves[1], halves[0]) if s is None else halves[s]


def head_lanes(h):
    first = lax.broadcasted_iota(jnp.int32, (1, 2 * HEAD_DIM), 1) < HEAD_DIM
    return first if h == 0 else jnp.logical_not(first)


def attend_kernel(group, counts, info, *refs):
    cross = group in (CROSS_A, CROSS_B)
    part_b = group in (SELF_B, CROSS_B)
    operands, at = [], 0
    for n in counts:
        operands.append(refs[at : at + n])
        at += n
    outs = refs[at:]
    bias_ref = outs[-1]
    p_ref = outs[-2]
    q, k, v = (load_halves(info, refs, len(refs) == 3) for refs in operands)
    half = q[0].shape[0]

    def run(full):
        blocks = attention_blocks(full, cross, half)

        @pl.when(pl.program_id(0) == 0)
        def _():
            for s, keys, rows, cols in blocks:
                at = rows if full else slice(0, half)
                kinds = (0, 1) if full else (2 + s, 2 + s)
                bias_ref[rows, cols] = clip_bias(info, group, at, slice(0, half * len(keys)), *kinds)

        mixes = []
        for s, keys, rows, cols in blocks:
            query = query_half(info, q, s) * jnp.asarray(SCORE_SCALE, BF16)
            key = jnp.concatenate([k[t] for t in keys], axis=0)
            value = jnp.concatenate([v[t] for t in keys], axis=0)
            pair = []
            for h in range(2):
                own = jnp.where(head_lanes(h), query, jnp.zeros_like(query))
                scores = dot_nt(own, key) + bias_ref[rows, cols]
                top = jnp.max(scores, axis=-1, keepdims=True)
                exponent = jnp.exp(scores - top)
                total = jnp.sum(exponent, axis=-1, keepdims=True)
                probs = (exponent * (1.0 / total)).astype(BF16)
                p_ref[h, rows, cols] = probs
                pair.append(dot_nn(probs, value))
            mixes.append(jnp.where(head_lanes(0), pair[0], pair[1]).astype(BF16))
        top, bottom = mixes[0], mixes[-1]
        if cross:
            outs[0][...] = top
            outs[1][...] = bottom
        else:
            outs[0][:half, :] = top
            outs[0][half:, :] = bottom
            if part_b:
                outs[1][...] = to_send(info, top, bottom)

    pl.when(info[FULL] != 0)(lambda: run(True))
    pl.when(info[FULL] == 0)(lambda: run(False))


def attend_back_kernel(group, counts, info, *refs):
    cross = group in (CROSS_A, CROSS_B)
    part_b = group in (SELF_B, CROSS_B)
    operands, at = [], 0
    for n in counts:
        operands.append(refs[at : at + n])
        at += n
    p_ref, outs = refs[at], refs[at + 1 :]
    q, k, v, g = (load_halves(info, refs, len(refs) == 3) for refs in operands)
    half = q[0].shape[0]

    def run(full):
        blocks = attention_blocks(full, cross, half)
        queries, sums = [], {}
        for s, keys, rows, cols in blocks:
            query = query_half(info, q, s)
            grad = query_half(info, g, s)
            key = jnp.concatenate([k[t] for t in keys], axis=0)
            value = jnp.concatenate([v[t] for t in keys], axis=0)
            dq, dk, dv = [], [], []
            for h in range(2):
                own = jnp.where(head_lanes(h), grad, jnp.zeros_like(grad))
                probs = p_ref[h, rows, cols]
                wide_probs = probs.astype(F32)
                grad_probs = dot_nt(own, value)
                delta = jnp.sum(wide_probs * grad_probs, axis=-1, keepdims=True)
                grad_scores = (wide_probs * (grad_probs - delta)).astype(BF16)
                dq.append(dot_nn(grad_scores, key))
                dk.append(dot_tn(grad_scores, query))
                dv.append(dot_tn(probs, grad))
            queries.append((jnp.where(head_lanes(0), dq[0], dq[1]) * SCORE_SCALE).astype(BF16))
            both = (jnp.where(head_lanes(0), dk[0], dk[1]), jnp.where(head_lanes(0), dv[0], dv[1]))
            sums[keys] = (sums[keys][0] + both[0], sums[keys][1] + both[1]) if keys in sums else both
        grads = []
        for t in range(2):
            dk, dv = (sums[(0, 1)] if full else sums[(t,)])
            rows = slice(t * half, (t + 1) * half) if full else slice(0, half)
            grads.append(((dk[rows] * SCORE_SCALE).astype(BF16), dv[rows].astype(BF16)))
        top, bottom = queries[0], queries[-1]
        if cross:
            outs[0][...] = top
            outs[1][...] = bottom
        parts = [(g0, g1) for g0, g1 in zip(*grads)]
        if not cross:
            parts = [(top, bottom)] + parts
        out_ref = outs[2] if cross else outs[0]
        for n, (first, second) in enumerate(parts):
            out_ref[n, :half, :] = first
            out_ref[n, half:, :] = second
            if part_b:
                outs[3 if cross else 1][n] = to_send(info, first, second)

    pl.when(info[FULL] != 0)(lambda: run(True))
    pl.when(info[FULL] == 0)(lambda: run(False))


def column_block(array, lead=None, row=0, column=0, rows=256):
    lanes = 2 * HEAD_DIM
    if array.ndim == 3:
        return (array, pl.BlockSpec((None, rows, lanes), lambda j, info: (lead, row, j + column)))
    return (array, pl.BlockSpec((rows, lanes), lambda j, info: (row, j + column)))


def halves_of(array, lead=None):
    return [column_block(array, lead, 0), column_block(array, lead, 1)]


def attend(info, group, operands, columns, rows=256):
    cross = group in (CROSS_A, CROSS_B)
    lanes = 2 * HEAD_DIM
    heads = columns // HEAD_DIM
    p_rows = rows if cross else 2 * rows
    half_out = ((rows, columns), BF16, pl.BlockSpec((rows, lanes), lambda j, info: (0, j)))
    mix_out = ((2 * rows, columns), BF16, pl.BlockSpec((2 * rows, lanes), lambda j, info: (0, j)))
    outs = [half_out, half_out] if cross else [mix_out] + ([half_out] if group == SELF_B else [])
    p_block = pl.BlockSpec((2, p_rows, 2 * rows), lambda j, info: (j, 0, 0))
    p_out = ((heads, p_rows, 2 * rows), BF16, p_block, True)
    return call(
        functools.partial(attend_kernel, group, [len(o) for o in operands]),
        info,
        heads // 2,
        sum(operands, []),
        outs + [p_out],
        [pltpu.VMEM((p_rows, 2 * rows), F32)],
        "attend",
        10,
        heads * 2 // 3,
    )


def attend_back(info, group, operands, probs, columns, rows=256):
    cross = group in (CROSS_A, CROSS_B)
    part_b = group in (SELF_B, CROSS_B)
    lanes = 2 * HEAD_DIM
    half_out = ((rows, columns), BF16, pl.BlockSpec((rows, lanes), lambda j, info: (0, j)))
    count = 2 if cross else 3

    def stacked(height):
        return ((count, height, columns), BF16, pl.BlockSpec((count, height, lanes), lambda j, info: (0, 0, j)))

    outs = [half_out, half_out] if cross else []
    outs = outs + [stacked(2 * rows)] + ([stacked(rows)] if part_b else [])
    p_block = pl.BlockSpec((2,) + probs.shape[1:], lambda j, info: (j, 0, 0))
    return call(
        functools.partial(attend_back_kernel, group, [len(o) for o in operands]),
        info,
        probs.shape[0] // 2,
        sum(operands, []) + [(probs, p_block)],
        outs,
        [],
        "attend_back",
        11,
        probs.shape[0],
    )


def first_project_kernel(info, a_ref, kept_ref, received_ref, norms_ref, w_ref, rows_ref, normed_ref, out_ref):
    @pl.when(pl.program_id(0) == 0)
    def _():
        rows = joined_rows(info, a_ref, kept_ref, received_ref)
        rows_ref[...] = rows
        normal, _ = norm_stats(rows.astype(F32))
        normed_ref[...] = (normal * norms_ref[0:1, :] + norms_ref[1:2, :]).astype(BF16)

    out_ref[...] = dot_nn(normed_ref[...], w_ref[...]).astype(BF16)


def first_project(info, tokens, received, norms, w_self):
    count, width, cols = w_self.shape
    rows = tokens.shape[1] + received.shape[0]
    return call(
        first_project_kernel,
        info,
        count,
        part_rows(tokens) + [whole_in(received), whole_in(norms), (w_self, lead_spec(width, cols))],
        [whole_out(rows, width, in_hbm=True), whole_out(rows, width, in_hbm=True)]
        + [((count, rows, cols), BF16, lead_spec(rows, cols))],
        [],
        "first_project",
        12,
        4,
    )


def other_project_kernel(info, normed_ref, own_b_ref, mine_ref, theirs_ref, out_ref, send_ref):
    weights = joined_pieces(info, mine_ref[...], theirs_ref[...], 0)
    out = dot_nn(normed_ref[...], weights).astype(BF16)
    out_ref[...] = out
    part_b = out.shape[0] - own_b_ref.shape[0]
    send_ref[...] = to_send(info, own_b_ref[...], out[part_b:])


def other_project(info, normed, qkv_own, mine, theirs, part_b):
    count, half, cols = mine.shape
    rows = normed.shape[0]
    own_b = pl.BlockSpec((None, part_b, cols), lambda j, info: (j, rows // part_b - 1, 0))
    return call(
        other_project_kernel,
        info,
        count,
        [whole_in(normed), (qkv_own, own_b), (mine, lead_spec(half, cols)), (theirs, lead_spec(half, cols))],
        [
            ((count, rows, cols), BF16, lead_spec(rows, cols)),
            ((count, part_b, cols), BF16, lead_spec(part_b, cols)),
        ],
        [],
        "other_project",
        9,
        3,
    )


def put_query_parts(info, value, far_ref, near_ref, left_ref, right_ref, send_ref):
    rows = left_ref.shape[0]
    cols = left_ref.shape[1]
    for h in range(2):
        at = slice(h * cols, (h + 1) * cols)
        far_ref[:, at] = value[h][:rows]
        near_ref[:, at] = value[h][rows : 2 * rows]
    left, right = value[0][2 * rows :], value[1][2 * rows :]
    left_ref[...] = left
    right_ref[...] = right
    send_ref[...] = to_send(info, left, right)


def query_outs(rows, width):
    whole, half = whole_out(rows, width), whole_out(rows, width // 2)
    return [whole, whole, half, half, half]


def self_mixes(info, mix0_ref, mix1_ref, slots_ref, received_ref):
    rows = received_ref.shape[0]
    parts = exchanged(info, TOP_BIG, slots_ref[:rows, :], slots_ref[rows:, :], received_ref[...])
    return [
        jnp.concatenate([ref[...], part], axis=0) for ref, part in zip((mix0_ref, mix1_ref), parts)
    ]


def second_project_kernel(
    info, rows_ref, norms_ref, mix0_ref, mix1_ref, slots_ref, received_ref, out_ref, query_ref, mine_ref, theirs_ref,
    hidden_ref, joined_ref, *query_refs,
):
    mixes = self_mixes(info, mix0_ref, mix1_ref, slots_ref, received_ref)
    other_out = joined_pieces(info, mine_ref[0], theirs_ref[0], 1)
    hidden = rows_ref[...].astype(F32) + dot_nn(mixes[0], out_ref[...]) + dot_nn(mixes[1], other_out)
    hidden_ref[...] = hidden
    normal, _ = norm_stats(hidden)
    joined = (normal * norms_ref[2:3, :] + norms_ref[3:4, :]).astype(BF16)
    joined_ref[...] = joined
    other_query = joined_pieces(info, mine_ref[1], theirs_ref[1], 0)
    queries = [dot_nn(joined, w).astype(BF16) for w in (query_ref[...], other_query)]
    put_query_parts(info, queries, *query_refs)


def second_project(info, rows, norms, mixes, w_self_out, w_query, mine, theirs, part_b):
    shape = rows.shape
    return call(
        second_project_kernel,
        info,
        1,
        [whole_in(a) for a in (rows, norms, *mixes, w_self_out, w_query, mine, theirs)],
        [whole_out(*shape, kind=F32, in_hbm=True), whole_out(*shape, in_hbm=True)] + query_outs(part_b, shape[1]),
        [],
        "second_project",
        17,
        5,
    )


def offer_project_kernel(info, rows_ref, own_ref, mine_ref, theirs_ref, out_ref, send_ref):
    cols = own_ref.shape[1]
    rows = send_ref.shape[0]
    other = joined_pieces(info, mine_ref[...], theirs_ref[...], 0)
    parts = [dot_nn(rows_ref[...], w).astype(BF16) for w in (own_ref[...], other)]
    for h in range(2):
        out_ref[:, h * cols : (h + 1) * cols] = parts[h]
    send_ref[...] = to_send(info, parts[0][-rows:], parts[1][-rows:])


def offer_project(info, joined, w_offer, mine, theirs, part_b):
    count, width, cols = w_offer.shape
    rows = joined.shape[0]
    piece = lead_spec(cols, cols)
    return call(
        offer_project_kernel,
        info,
        count,
        [whole_in(joined), (w_offer, lead_spec(width, cols)), (mine, piece), (theirs, piece)],
        [
            ((count, rows, 2 * cols), BF16, lead_spec(rows, 2 * cols)),
            ((count, part_b, cols), BF16, lead_spec(part_b, cols)),
        ],
        [],
        "offer_project",
        9,
        4,
    )


def reader_rows(info, far_ref, near_ref, far_b_ref, near_b_ref, received_ref):
    half = far_b_ref.shape[1]
    parts = exchanged(info, TOP_MID, far_b_ref[...], near_b_ref[...], received_ref[...])
    return [
        jnp.concatenate([ref[:, h * half : (h + 1) * half] for ref in (far_ref, near_ref)] + [parts[h]], axis=0)
        for h in range(2)
    ]


def mlp_kernel(
    info, hidden_ref, norms_ref, far_ref, near_ref, far_b_ref, near_b_ref, received_ref, w_cross_ref, mine_ref,
    theirs_ref, grad_a_ref, grad_kept_ref, grad_received_ref, up_ref, down_ref, result_ref, grad_second_ref, gm_far_ref, gm_near_ref, gm_left_ref, gm_right_ref,
    gm_send_ref, activated_ref, grad_up_ref, rows_ref, grad_ref, keep_ref, send_ref, g_norms_ref, second_ref,
    sum_ref, back_ref,
):
    step = pl.program_id(0)

    def mixes():
        return reader_rows(info, far_ref, near_ref, far_b_ref, near_b_ref, received_ref)

    def cross_weights():
        return w_cross_ref[...], joined_pieces(info, mine_ref[...], theirs_ref[...], 1)

    @pl.when(step == 0)
    def _():
        grad_ref[...] = joined_rows(info, grad_a_ref, grad_kept_ref, grad_received_ref)
        second = hidden_ref[...]
        for mix, weight in zip(mixes(), cross_weights()):
            second = second + dot_nn(mix, weight)
        second_ref[...] = second
        normal, _ = norm_stats(second)
        rows_ref[...] = (normal * norms_ref[4:5, :] + norms_ref[5:6, :]).astype(BF16)
        sum_ref[...] = second
        back_ref[...] = jnp.zeros_like(back_ref)

    rows, grad, up, down = rows_ref[...], grad_ref[...], up_ref[...], down_ref[...]
    pre = dot_nn(rows, up)
    spread = lax.erf(pre * 0.7071067811865476) * 0.5 + 0.5
    slope = spread + pre * (jnp.exp(pre * pre * -0.5) * 0.3989422804014327)
    activated = (pre * spread).astype(BF16)
    grad_up = (dot_nt(grad, down) * slope).astype(BF16)
    sum_ref[...] += dot_nn(activated, down)
    back_ref[...] += dot_nt(grad_up, up)
    activated_ref[...] = activated
    grad_up_ref[...] = grad_up

    @pl.when(step == 3)
    def _():
        result_ref[...] = sum_ref[...].astype(BF16)
        normal, inverse = norm_stats(second_ref[...])
        back, gain, shift = norm_back(back_ref[...], normal, inverse, norms_ref[4:5, :])
        g_norms_ref[0:1, :] = gain
        g_norms_ref[1:2, :] = shift
        grad_second = grad_ref[...].astype(F32) + back
        grad_second_ref[...] = grad_second
        rounded = grad_second.astype(BF16)
        parts = []
        for h, (mix, weight) in enumerate(zip(mixes(), cross_weights())):
            parts.append(dot_nt(rounded, weight).astype(BF16))
            put_pieces(info, keep_ref, send_ref, h, dot_tn(mix, rounded), 1)
        put_query_parts(info, parts, gm_far_ref, gm_near_ref, gm_left_ref, gm_right_ref, gm_send_ref)


def mlp(info, hidden, norms, mixes, w_cross, mine, theirs, cotangent, received, up, down):
    rows, width = hidden.shape
    half = width // 2
    part_b = received.shape[0]

    pieces = (up.shape[:1] + (rows, width), BF16, lead_spec(rows, width), True)
    wide = pltpu.VMEM((rows, width), F32)
    return call(
        mlp_kernel,
        info,
        4,
        [whole_in(a) for a in (hidden, norms, *mixes, w_cross)]
        + [whole_in(mine), whole_in(theirs)]
        + part_rows(cotangent)
        + [whole_in(received), (up, lead_spec(width, width)), (down, lead_spec(width, width))],
        [whole_out(rows, width), whole_out(rows, width, kind=F32, in_hbm=True)]
        + query_outs(part_b, width)
        + [pieces, pieces, whole_out(rows, width), whole_out(rows, width)]
        + [whole_out(2, half, half), whole_out(2, half, half)]
        + [whole_out(2, width, kind=F32)],
        [wide, wide, wide],
        "mlp",
        46,
        34,
    )


def mlp_weights_kernel(info, rows_ref, grad_ref, activated_ref, grad_up_ref, *outs):
    g_up = dot_tn(rows_ref[...], grad_up_ref[...]).astype(BF16)
    g_down = dot_tn(activated_ref[...], grad_ref[...]).astype(BF16)
    first = pl.program_id(0) < 2
    for keep_ref, send_ref, value in ((outs[0], outs[1], g_up), (outs[2], outs[3], g_down)):

        @pl.when(first)
        def _(keep_ref=keep_ref, value=value):
            keep_ref[...] = value

        @pl.when(jnp.logical_not(first))
        def _(send_ref=send_ref, value=value):
            send_ref[...] = value


def mlp_weights(info, rows, grad, activated, grad_up):
    count, height, width = activated.shape

    def pieces(index):
        return ((2, width, width), BF16, pl.BlockSpec((None, width, width), lambda j, info: (index(j), 0, 0)))

    keep, send = pieces(lambda j: jnp.minimum(j, 1)), pieces(lambda j: jnp.maximum(j - 2, 0))
    piece = lead_spec(height, width)
    return call(
        mlp_weights_kernel,
        info,
        count,
        [whole_in(from_hbm(rows)), whole_in(from_hbm(grad)), (from_hbm(activated), piece), (from_hbm(grad_up), piece)],
        [keep, send, keep, send],
        [],
        "mlp_weights",
        24,
        10,
    )


def second_back_kernel(
    info, far_ref, near_ref, far_b_ref, near_b_ref, received_ref, dkv_ref, slots_ref, slots_received_ref, joined_ref,
    hidden_ref, grad_second_ref, norms_ref, offer_ref, offer_mine_ref, offer_theirs_ref, query_ref, out_ref, mine_ref,
    theirs_ref, mix0_ref, mix1_ref, mix_slots_ref, mix_received_ref, cross_keep_ref, cross_send_ref, grad_hidden_ref,
    grad_mix_ref, mix_send_ref, keep_ref, send_ref, g_norms_ref, back_ref,
):
    step = pl.program_id(0)
    half = query_ref.shape[1]
    rows = received_ref.shape[0]

    def add(at, grads, weights, first):
        joined = joined_ref[...]
        total = dot_nt(grads[0], weights[0]) + dot_nt(grads[1], weights[1])
        back_ref[...] = total if first else back_ref[...] + total
        for h in range(2):
            put_pieces(info, keep_ref, send_ref, (h, at), dot_tn(joined, grads[h]), 0)

    def add_offer(at):
        parts = exchanged(info, TOP_BIG, slots_ref[:rows, :], slots_ref[rows:, :], slots_received_ref[...])
        grads = [
            jnp.concatenate([dkv_ref[:, h * half : (h + 1) * half], parts[h]], axis=0) for h in range(2)
        ]
        other = joined_pieces(info, offer_mine_ref[...], offer_theirs_ref[...], 0)
        add(at, grads, (offer_ref[...], other), at == 0)

    pl.when(step == 0)(lambda: add_offer(0))
    pl.when(step == 1)(lambda: add_offer(1))

    @pl.when(step == 2)
    def _():
        for h in range(2):
            keep_ref[h, 4] = cross_keep_ref[h]
            send_ref[h, 4] = cross_send_ref[h]
        grads = reader_rows(info, far_ref, near_ref, far_b_ref, near_b_ref, received_ref)
        add(3, grads, (query_ref[...], joined_pieces(info, mine_ref[1], theirs_ref[1], 0)), False)
        normal, inverse = norm_stats(hidden_ref[...])
        back, gain, shift = norm_back(back_ref[...], normal, inverse, norms_ref[2:3, :])
        g_norms_ref[0:1, :] = gain
        g_norms_ref[1:2, :] = shift
        grad_hidden = grad_second_ref[...] + back
        grad_hidden_ref[...] = grad_hidden
        rounded = grad_hidden.astype(BF16)
        mixes = self_mixes(info, mix0_ref, mix1_ref, mix_slots_ref, mix_received_ref)
        parts = []
        for h, weight in enumerate((out_ref[...], joined_pieces(info, mine_ref[0], theirs_ref[0], 1))):
            part = dot_nt(rounded, weight).astype(BF16)
            grad_mix_ref[h] = part
            parts.append(part[-rows:])
            put_pieces(info, keep_ref, send_ref, (h, 2), dot_tn(mixes[h], rounded), 1)
        mix_send_ref[...] = to_send(info, *parts)


def second_back(
    info, grad_q, dkv, slots, slots_received, joined, hidden, grad_second, norms, w_offer, offer_mine, offer_theirs,
    w_query, w_self_out, mine, theirs, mixes, cross_keep, cross_send,
):
    rows, width = hidden.shape
    half = width // 2
    part_b = slots_received.shape[1]

    def offered(array, *shape):
        return (array, pl.BlockSpec((None,) + shape, lambda j, info: (jnp.minimum(j, 1), 0, 0)))

    return call(
        second_back_kernel,
        info,
        3,
        [whole_in(a) for a in grad_q]
        + [offered(dkv, *dkv.shape[1:]), offered(slots, *slots.shape[1:])]
        + [offered(slots_received, *slots_received.shape[1:])]
        + [whole_in(a) for a in (joined, hidden, grad_second, norms)]
        + [offered(w_offer, width, half), offered(offer_mine, half, half), offered(offer_theirs, half, half)]
        + [whole_in(a) for a in (w_query, w_self_out, mine, theirs, *mixes, cross_keep, cross_send)],
        [whole_out(rows, width, kind=F32, in_hbm=True), whole_out(2, rows, half), whole_out(part_b, half)]
        + [whole_out(2, 5, half, half), whole_out(2, 5, half, half), whole_out(2, width, kind=F32)],
        [pltpu.VMEM((rows, width), F32)],
        "second_back",
        35,
        12,
    )


def first_grads(info, own_ref, other_ref, slots_ref, received_ref):
    rows = received_ref.shape[0]
    parts = exchanged(info, TOP_BIG, slots_ref[:rows, :], slots_ref[rows:, :], received_ref[...])
    return [jnp.concatenate([ref[...], part], axis=0) for ref, part in zip((own_ref, other_ref), parts)]


def first_weights_kernel(half, info, grad_ref, slots_ref, received_ref, normed_ref, keep_ref, send_ref):
    rows = received_ref.shape[0]
    parts = exchanged(info, TOP_BIG, slots_ref[:rows, :], slots_ref[rows:, :], received_ref[...])
    value = dot_tn(normed_ref[...], jnp.concatenate([grad_ref[...], parts[half]], axis=0))
    put_pieces(info, keep_ref, send_ref, slice(None), value, 0)


def first_ins(*arrays):
    return [(a, lead_spec(*a.shape[1:])) for a in arrays]


def first_weights(info, half_index, grads, slots, received, normed):
    half = grads.shape[2]
    piece = ((3, half, half), BF16, lead_spec(half, half))
    return call(
        functools.partial(first_weights_kernel, half_index),
        info,
        3,
        first_ins(grads, slots, received) + [whole_in(normed)],
        [piece, piece],
        [],
        "first_weights",
        12,
        3,
    )


def first_back_kernel(
    info, own_ref, other_ref, slots_ref, received_ref, rows_ref, grad_hidden_ref, norms_ref, w_own_ref, mine_ref,
    theirs_ref, grad_rows_ref, g_norms_ref, back_ref,
):
    step = pl.program_id(0)
    grads = first_grads(info, own_ref, other_ref, slots_ref, received_ref)
    other = joined_pieces(info, mine_ref[...], theirs_ref[...], 0)
    total = dot_nt(grads[0], w_own_ref[...]) + dot_nt(grads[1], other)

    @pl.when(step == 0)
    def _():
        back_ref[...] = total

    @pl.when(step > 0)
    def _():
        back_ref[...] += total

    @pl.when(step == pl.num_programs(0) - 1)
    def _():
        normal, inverse = norm_stats(rows_ref[...].astype(F32))
        back, gain, shift = norm_back(back_ref[...], normal, inverse, norms_ref[0:1, :])
        g_norms_ref[0:1, :] = gain
        g_norms_ref[1:2, :] = shift
        grad_rows = (grad_hidden_ref[...] + back).astype(BF16)
        grad_rows_ref[...] = grad_rows


def first_back(info, own, other, slots, received, rows, grad_hidden, norms, w_self, mine, theirs):
    count = own.shape[0]
    width = rows.shape[1]
    ins = first_ins(own, other, slots, received)
    ins += [whole_in(a) for a in (rows, grad_hidden, norms)]
    ins += [(a, lead_spec(*a.shape[1:])) for a in (w_self, mine, theirs)]
    return call(
        first_back_kernel,
        info,
        count,
        ins,
        [whole_out(*rows.shape), whole_out(2, width, kind=F32)],
        [pltpu.VMEM(rows.shape, F32)],
        "first_back",
        24,
        8,
    )


def row_of(table, index):
    return lax.dynamic_index_in_dim(table, index, 0, keepdims=False)


def scalars(clip_len, index, across, quarter):
    core = index % 2
    is_big = index < 2 * quarter
    is_mid = jnp.logical_and(index >= 2 * quarter, index < 3 * quarter)
    first, last = core == 0, core == 1
    flags = [
        is_big,
        core,
        across,
        jnp.logical_and(is_big, index >= quarter),
        jnp.logical_and(is_big, last),
        jnp.logical_and(is_big, first),
        jnp.logical_and(is_mid, last),
        jnp.logical_and(is_mid, first),
    ]
    shared = index - core + across
    lens_a, lens_b = row_of(clip_len, across), clip_len[2]
    big_a = row_of(lens_a, jnp.minimum(index, 2 * quarter - 1))
    big_b = row_of(lens_b, jnp.minimum(shared, 2 * quarter - 1))
    sets_a = [row_of(lens_a, index % quarter + s * quarter) for s in range(2)]
    sets_b = [row_of(lens_b, shared % quarter + core * quarter)] * 2
    table = jnp.stack(
        [2 * big_a, 2 * big_a, *sets_a, 2 * big_b, 2 * big_b, *sets_b]
        + [big_a, 2 * big_a, *sets_a, big_b, 2 * big_b, *sets_b]
    )
    ends = [table[:, 0]]
    for k in range(1, 4):
        ends.append(ends[-1] + table[:, k])
    flags = jnp.stack([flag.astype(jnp.int32) for flag in flags])
    return jnp.concatenate([flags, jnp.stack(ends, axis=1).reshape(-1)])


def local(
    tokens,
    cotangent,
    clip_len,
    ln_params,
    w_self,
    w_self_out,
    w_offer,
    w_query,
    w_cross_out,
    w_up,
    w_down,
):
    index = lax.axis_index("clip")
    across = lax.axis_index("head")
    count = lax.axis_size("clip")
    quarter = count // 4
    levels = (2 * quarter).bit_length() - 1
    core = index % 2
    is_big = index < 2 * quarter
    is_mid = jnp.logical_and(index >= 2 * quarter, index < 3 * quarter)
    own_micro2 = core == across
    norms = ln_params[0]
    w_self, w_self_out, w_offer, w_query = w_self[0], w_self_out[0], w_offer[0], w_query[0]
    w_cross_out, w_up, w_down = w_cross_out[0], w_up[0], w_down[0]
    half = w_query.shape[1]
    part_a = tokens.shape[1]
    part_b = part_a // 2
    wide = 2 * half

    near = [(i, i - quarter) for i in range(2 * quarter, count)]
    far = [(i, i - 2 * quarter) for i in range(2 * quarter, 3 * quarter)]
    far += [(i, i - quarter) for i in range(3 * quarter, count)]

    def to_server(far_rows, near_rows):
        second = lax.ppermute(near_rows, "clip", near)
        return lax.ppermute(far_rows, "clip", far), second

    def to_reader(far_rows, near_rows):
        second = lax.ppermute(near_rows, "clip", [(b, a) for a, b in near])
        return lax.ppermute(far_rows, "clip", [(b, a) for a, b in far]), second

    def reader_slots(left, right, received):
        top = jnp.where(jnp.logical_and(is_mid, core == 1), received, left)
        return top, jnp.where(jnp.logical_and(is_mid, core == 0), received, right)

    def from_server(top, bottom):
        return top, bottom, other_core(jnp.where(core == 0, bottom, top))

    def over_level(part, bit):
        return over_bit(part, bit, 2 * quarter if bit == levels - 1 else None)

    def add(left, right):
        return (left.astype(F32) + right.astype(F32)).astype(BF16)

    def last_levels(total, received):
        total = total if received is None else add(total, received)
        for bit in range(3, levels):
            total = add(total, over_level(total, bit))
        return total

    def whole(mine, axis):
        return in_core_order(core, mine, other_core(mine), axis).astype(F32)[None]

    def all_rows(a_mine, b_mine, a_theirs, b_theirs):
        kept = jnp.where(own_micro2, b_mine, b_theirs)
        received = other_core(jnp.where(own_micro2, b_theirs, b_mine))
        micro2 = in_core_order(core, kept, received, 0)
        micro0 = jnp.where(across == 0, a_mine, a_theirs)
        micro1 = jnp.where(across == 0, a_theirs, a_mine)
        return jnp.stack([micro0, micro1, micro2])


    def over_head_rows(array, start, stop, *others):
        return over_head(after(array[start:stop], *others) if others else array[start:stop])

    self_mine = over_head(core_piece(w_self, core, 1))
    tokens_received = other_core(core_piece(tokens[2], 1 - core, 0))
    info = scalars(clip_len, index, across, quarter)
    rows, normed, qkv_own = first_project(info, tokens, tokens_received, norms, w_self)
    self_0 = [halves_of(qkv_own, n) for n in range(3)]
    mix_0, p_0 = attend(info, SELF_A, self_0, half)
    first_piece = jnp.stack([core_piece(w_self_out, core, 1), core_piece(w_query, core, 0)])
    offer_piece, up_piece, down_piece = core_piece(w_offer, core, 1), core_piece(w_up, core, 1), core_piece(w_down, core, 0)
    cross_piece = core_piece(w_cross_out, core, 1)
    (self_mine, mix_0, first_piece) = fence(self_mine, mix_0, first_piece)

    first_mine = over_head(first_piece)
    self_theirs = other_core(self_mine)
    qkv_other, qkv_send = other_project(info, normed, qkv_own, self_mine, self_theirs, part_b)
    self_1 = [halves_of(qkv_other, n) for n in range(3)]
    mix_1, p_1 = attend(info, SELF_A, self_1, half)
    qkv_received, first_mine, mix_1, offer_piece = fence(other_core(qkv_send), first_mine, mix_1, offer_piece)

    offer_mine = over_head(offer_piece[0])
    self_b = [
        [column_block(qkv_own, n, 2), column_block(qkv_other, n, 2), column_block(qkv_received, n)] for n in range(3)
    ]
    mix_s, mix_send, p_s = attend(info, SELF_B, self_b, half)
    first_theirs = other_core(first_mine)
    mix_s, mix_send, offer_mine, offer_piece = fence(mix_s, mix_send, offer_mine, offer_piece)

    offer_last = over_head(offer_piece[1])
    mixes = (mix_0, mix_1, mix_s, other_core(mix_send))
    hidden, joined, q_far, q_near, q_left, q_right, q_send = second_project(
        info, rows, norms, mixes, w_self_out, w_query, first_mine, first_theirs, part_b
    )
    q_far, q_near, q_left, q_right, q_send, joined, offer_mine, offer_last, cross_piece, up_piece, down_piece, cotangent = fence(
        q_far, q_near, q_left, q_right, q_send, joined, offer_mine, offer_last, cross_piece, up_piece, down_piece, cotangent
    )

    asked_a = to_server(q_far, q_near)
    up_mine = [over_head(up_piece[:576])]
    q_top, q_bottom = reader_slots(q_left, q_right, other_core(q_send))
    offer_mine = jnp.stack([offer_mine, offer_last])
    offer_theirs = other_core(offer_mine)
    offer, offer_send = offer_project(info, joined, w_offer, offer_mine, offer_theirs, part_b)
    cotangent_received = other_core(core_piece(cotangent[2], 1 - core, 0))
    offer_received = other_core(offer_send)
    *asked_a, q_top, q_bottom, offer, offer_received, cotangent_received, up_mine[0], up_piece, cross_piece = fence(
        *asked_a, q_top, q_bottom, offer, offer_received, cotangent_received, up_mine[0], up_piece, cross_piece
    )

    asked_b = to_server(q_top, q_bottom)
    up_mine.append(over_head(up_piece[576:]))
    cross_mine = over_head(cross_piece)
    cross_a = [[column_block(asked_a[0]), column_block(asked_a[1])]] + [halves_of(offer, n) for n in range(2)]
    far_a, near_a, cross_p_a = attend(info, CROSS_A, cross_a, wide)
    far_a, near_a, asked_b_far, asked_b_near, up_mine[1], cross_mine, down_piece = fence(
        far_a, near_a, *asked_b, up_mine[1], cross_mine, down_piece
    )

    back_a = to_reader(far_a, near_a)
    down_mine = [over_head(down_piece[:576])]
    cross_b = [[column_block(asked_b_far), column_block(asked_b_near)]] + [
        [
            column_block(offer, n, 2),
            column_block(offer, n, 2, half // (2 * HEAD_DIM)),
            column_block(offer_received, n),
        ]
        for n in range(2)
    ]
    far_b, near_b, cross_p_b = attend(info, CROSS_B, cross_b, half)
    up_mine = jnp.concatenate(up_mine)
    up_theirs = other_core(up_mine)
    cross_theirs = other_core(cross_mine)
    *back_a, far_b, near_b, up_mine, up_theirs, cross_theirs, down_mine[0], down_piece = fence(
        *back_a, far_b, near_b, up_mine, up_theirs, cross_theirs, down_mine[0], down_piece
    )

    back_b = to_reader(far_b, near_b)
    down_mine = jnp.concatenate([down_mine[0], over_head(down_piece[576:])])
    up_pieces = jnp.stack([core_piece(w_up, core, 1), up_mine, core_piece(w_up, 1 - core, 1), up_theirs])
    *back_b, down_mine, up_pieces = fence(*back_b, down_mine, up_pieces)

    back_b = from_server(*back_b)
    down_theirs = other_core(down_mine)
    down_pieces = jnp.stack([core_piece(w_down, core, 0), down_mine, core_piece(w_down, 1 - core, 0), down_theirs])
    (
        result, grad_second, gm_far, gm_near, gm_left, gm_right, gm_send,
        activated, grad_up, mlp_rows, grad_out, cross_keep, cross_send, norms_3,
    ) = mlp(
        info, hidden, norms, (*back_a, *back_b), w_cross_out, cross_mine, cross_theirs, cotangent, cotangent_received,
        up_pieces, down_pieces,
    )
    result, gm_far, gm_near, gm_left, gm_right, gm_send, activated, grad_up, mlp_rows, grad_out = fence(
        result, gm_far, gm_near, gm_left, gm_right, gm_send, activated, grad_up, mlp_rows, grad_out
    )

    grad_a = to_server(gm_far, gm_near)
    layer_x = [over_head(result[:448])]
    gm_top, gm_bottom = reader_slots(gm_left, gm_right, other_core(gm_send))
    up_keep, up_send, down_keep, down_send = mlp_weights(info, mlp_rows, grad_out, activated, grad_up)
    *grad_a, gm_top, gm_bottom, layer_x[0], result, down_keep, down_send, up_keep, up_send = fence(
        *grad_a, gm_top, gm_bottom, layer_x[0], result, down_keep, down_send, up_keep, up_send
    )

    grad_b = to_server(gm_top, gm_bottom)
    layer_x.append(over_head(result[448:]))
    down_received = other_core(down_send)
    down_out = [add(down_keep[1, :576], down_received[1, :576]), add(down_keep[1, 576:], down_received[1, 576:])]
    grad_in = [column_block(grad_a[0]), column_block(grad_a[1])]
    dq_far, dq_near, dkv_a = attend_back(info, CROSS_A, cross_a + [grad_in], cross_p_a, wide)
    dq_far, dq_near, grad_b_far, grad_b_near, layer_x[1], *down_out, up_keep, up_send = fence(
        dq_far, dq_near, *grad_b, layer_x[1], *down_out, up_keep, up_send
    )

    dq_a = to_reader(dq_far, dq_near)
    down_x = [over_head(down_out[0])]
    grad_in = [column_block(grad_b_far), column_block(grad_b_near)]
    dq_b_far, dq_b_near, dkv_b, dkv_send = attend_back(info, CROSS_B, cross_b + [grad_in], cross_p_b, half)
    up_received = other_core(up_send)
    up_out = [add(up_keep[1, :192], up_received[1, :192]), add(up_keep[1, 192:], up_received[1, 192:])]
    *dq_a, dq_b_far, dq_b_near, dkv_send, down_x[0], up_out[0], up_out[1], down_out[1] = fence(
        *dq_a, dq_b_far, dq_b_near, dkv_send, down_x[0], *up_out, down_out[1]
    )

    dq_b = to_reader(dq_b_far, dq_b_near)
    dkv_received = other_core(dkv_send)
    down_x.append(over_head(down_out[1]))
    up_x = [over_head(up_out[0])]
    down_own = add(down_keep[0, :576], down_received[0, :576])
    down_own = add(down_own, down_x[0])
    down_first, down_rest = down_own[:384], down_own[384:]
    down_y = [over_level(down_first, 1)]
    *dq_b, dkv_received, down_x[1], up_x[0], up_out[1], down_first, down_rest, down_y[0] = fence(
        *dq_b, dkv_received, down_x[1], up_x[0], up_out[1], down_first, down_rest, down_y[0]
    )

    up_x.append(over_head(up_out[1]))
    down_second = add(add(down_keep[0, 576:], down_received[0, 576:]), down_x[1])
    down_second = jnp.concatenate([down_rest, down_second])
    down_y.append(over_level(down_second, 1))
    down_first = add(down_first, down_y[0])
    down_z = [over_level(down_first, 2)]
    grad_hidden, grad_mix, grad_send, mid_keep, mid_send, norms_2 = second_back(
        info, (*dq_a, *from_server(*dq_b)), dkv_a, dkv_b, dkv_received, joined, hidden, grad_second, norms, w_offer,
        offer_mine, offer_theirs, w_query, w_self_out, first_mine, first_theirs, mixes, cross_keep, cross_send,
    )
    up_own = add(up_keep[0], up_received[0])
    grad_hidden, grad_mix, grad_send, mid_keep, mid_send, up_x[1], up_own, down_second, down_y[1], down_first, down_z[0] = fence(
        grad_hidden, grad_mix, grad_send, mid_keep, mid_send, up_x[1], up_own, down_second, down_y[1], down_first, down_z[0]
    )

    (back_1,) = attend_back(info, SELF_A, self_1 + [halves_of(grad_mix, 1)], p_1, half)
    grad_received = other_core(grad_send)
    mid_received = other_core(mid_send)
    mid_out = [add(mid_keep[1, :3], mid_received[1, :3]), add(mid_keep[1, 3:], mid_received[1, 3:])]
    up_total = add(up_own, jnp.concatenate(up_x))
    up_y = [over_level(up_total[:384], 1)]
    down_second = add(down_second, down_y[1])
    down_z.append(over_level(down_second, 2))
    back_1, grad_mix, grad_received, mid_out[0], mid_out[1], up_total, up_y[0], down_second, down_z[1] = fence(
        back_1, grad_mix, grad_received, *mid_out, up_total, up_y[0], down_second, down_z[1]
    )

    mid_x = [over_head(mid_out[0])]
    up_y.append(over_level(up_total[384:], 1))
    up_first = add(up_total[:384], up_y[0])
    up_z = [over_level(up_first, 2)]
    grad_in = [column_block(grad_mix, 0, 2), column_block(grad_mix, 1, 2), column_block(grad_received)]
    back_s, back_send = attend_back(info, SELF_B, self_b + [grad_in], p_s, half)
    back_received = other_core(back_send)
    other_keep, other_send = first_weights(info, 1, back_1, back_s, back_received, normed)
    mid_own = add(mid_keep[0], mid_received[0])
    (
        back_s, back_received, other_keep, other_send, mid_x[0], mid_own, mid_out[1],
        up_total, up_y[1], up_first, up_z[0], grad_mix,
    ) = fence(
        back_s, back_received, other_keep, other_send, mid_x[0], mid_own, mid_out[1],
        up_total, up_y[1], up_first, up_z[0], grad_mix,
    )

    mid_x.append(over_head(mid_out[1]))
    mid_first = add(mid_own[:3], mid_x[0])
    mid_y = [over_level(mid_first, 1)]
    up_second = add(up_total[384:], up_y[1])
    up_z.append(over_level(up_second, 2))
    (back_0,) = attend_back(info, SELF_A, self_0 + [halves_of(grad_mix, 0)], p_0, half)
    own_keep, own_send = first_weights(info, 0, back_0, back_s, back_received, normed)
    last_out = add(other_keep, other_core(other_send))
    down_total = jnp.concatenate([last_levels(down_first, down_z[0]), last_levels(down_second, down_z[1])])
    grad_down_weight = whole(down_total, 0)
    (
        back_0, own_keep, own_send, last_out, mid_x[1], mid_first, mid_y[0], up_second, up_z[1], mid_own,
        grad_down_weight,
    ) = fence(
        back_0, own_keep, own_send, last_out, mid_x[1], mid_first, mid_y[0], up_second, up_z[1], mid_own,
        grad_down_weight,
    )

    last_x = over_head(last_out)
    mid_second = add(mid_own[3:], mid_x[1])
    mid_y.append(over_level(mid_second, 1))
    mid_first = add(mid_first, mid_y[0])
    mid_z = over_level(mid_first, 2)
    own_received = other_core(own_send)
    last_own = [add(own_keep[:2], own_received[:2]), add(own_keep[2:], own_received[2:])]
    grad_rows, norms_1 = first_back(
        info, back_0, back_1, back_s, back_received, rows, grad_hidden, norms, w_self, self_mine, self_theirs
    )
    up_total = jnp.concatenate([last_levels(up_first, up_z[0]), last_levels(up_second, up_z[1])])
    grad_up_weight = whole(up_total, 1)
    grad_rows, norms_1, last_own[0], last_own[1], last_x, mid_second, mid_y[1], mid_first, mid_z, grad_up_weight = fence(
        grad_rows, norms_1, *last_own, last_x, mid_second, mid_y[1], mid_first, mid_z, grad_up_weight
    )

    rows_x = over_head(grad_rows)
    first, second = add(last_own[0], last_x[:2]), add(last_own[1], last_x[2:])
    first_y, second_z = over_level(first, 1), over_level(second, 2)
    norm_grads = jnp.concatenate([norms_1, norms_2, norms_3], axis=0)
    norm_grads = norm_grads + other_core(norm_grads)
    norm_grads = norm_grads + over_level(norm_grads, 1)
    (
        rows_x, first, first_y, second, second_z, norm_grads, mid_first, mid_second
    ) = fence(
        rows_x, first, first_y, second, second_z, norm_grads, mid_first, mid_second
    )

    first, second = add(first, first_y), add(second, second_z)
    first_z, second_y = over_level(first, 2), over_level(second, 1)
    norm_grads = norm_grads + over_head(norm_grads)
    layer_x = after(jnp.concatenate(layer_x), first)
    layer_out = all_rows(result[:part_a], result[part_a:], layer_x[:part_a], layer_x[part_a:])
    grad_tokens = all_rows(grad_rows[:part_a], grad_rows[part_a:], rows_x[:part_a], rows_x[part_a:]).astype(F32)
    mid_total = last_levels(mid_first, mid_z)
    rest_total = add(mid_second, mid_y[1])
    for bit in range(2, levels - 1):
        rest_total = add(rest_total, over_level(rest_total, bit))

    early = [layer_out, grad_tokens, whole(mid_total[2], 1), whole(mid_total[:2], 1), whole(rest_total[0], 0)]
    early += [whole(rest_total[1], 1)]
    first, first_z, second, second_y, norm_grads, *early = fence(first, first_z, second, second_y, norm_grads, *early)
    layer_out, grad_tokens, *grad_weights = early

    for bit in range(2, levels):
        norm_grads = norm_grads + over_level(norm_grads, bit)
    last_total = jnp.concatenate([last_levels(first, first_z), last_levels(second, second_y)])
    return (layer_out, grad_tokens, norm_grads[None], whole(last_total, 1), *grad_weights, grad_up_weight, grad_down_weight)


def solution(mesh):
    return jax.shard_map(
        local,
        mesh=mesh,
        in_specs=(
            P(None, "clip", None),
            P(None, "clip", None),
            P(),
            P("clip", None, None),
            P("clip", None, None, "head"),
            P("clip", "head", None),
            P("clip", None, None, "head"),
            P("clip", None, "head"),
            P("clip", "head", None),
            P("clip", None, "head"),
            P("clip", "head", None),
        ),
        out_specs=(
            P(None, "clip", None),
            P(None, "clip", None),
            P("clip", None, None),
            P("clip", None, None, "head"),
            P("clip", "head", None),
            P("clip", None, None, "head"),
            P("clip", None, "head"),
            P("clip", "head", None),
            P("clip", None, "head"),
            P("clip", "head", None),
        ),
        check_vma=False,
    )
```

```python
import functools

import jax
import jax.numpy as jnp
from jax import lax
from jax.experimental import pallas as pl
from jax.experimental.pallas import tpu as pltpu
from jax.sharding import PartitionSpec as P


HEAD_DIM = 64
PAIRS = 3
EPSILON = 1e-06
SCORE_SCALE = 0.125
MASKED = -1e30
BF16 = jnp.bfloat16
F32 = jnp.float32
COST_BYTES = 1

FULL, CORE, ACROSS, SECOND_PLANE, TOP_BIG, BOTTOM_BIG, TOP_MID, BOTTOM_MID, ENDS = range(9)
SELF_A, SELF_B, CROSS_A, CROSS_B = range(4)


def over_head(value):
    return lax.ppermute(value, "head", [(0, 1), (1, 0)])


def over_bit(value, bit, count=None):
    count = lax.axis_size("clip") if count is None else count
    return lax.ppermute(value, "clip", [(i, i ^ (1 << bit)) for i in range(count)])


def other_core(value):
    return over_bit(value, 0)


def fence(*values):
    return lax.optimization_barrier(values)


def after(value, *others):
    return lax.optimization_barrier((value,) + others)[0]


def in_core_order(core, mine, theirs, axis):
    first = jnp.where(core == 0, mine, theirs)
    second = jnp.where(core == 0, theirs, mine)
    return jnp.concatenate([first, second], axis=axis)


def core_piece(value, piece, axis):
    size = value.shape[axis] // 2
    return lax.dynamic_slice_in_dim(value, piece * size, size, axis)


def dot_nt(left, right):
    return lax.dot_general(left, right, (((1,), (1,)), ((), ())), preferred_element_type=F32)


def dot_tn(left, right):
    return lax.dot_general(left, right, (((0,), (0,)), ((), ())), preferred_element_type=F32)


def dot_nn(left, right):
    return jnp.dot(left, right, preferred_element_type=F32)


def norm_stats(rows):
    mean = jnp.mean(rows, axis=-1, keepdims=True)
    centered = rows - mean
    variance = jnp.mean(centered * centered, axis=-1, keepdims=True)
    inverse = lax.rsqrt(variance + EPSILON)
    return centered * inverse, inverse


def norm_back(grad, normal, inverse, gain):
    scaled = grad * gain
    mean = jnp.mean(scaled, axis=-1, keepdims=True)
    along = jnp.mean(scaled * normal, axis=-1, keepdims=True)
    grad_rows = (scaled - mean - normal * along) * inverse
    gain_grad = jnp.sum(grad * normal, axis=0, keepdims=True)
    return grad_rows, gain_grad, jnp.sum(grad, axis=0, keepdims=True)


def pick(info, flag, yes, no):
    return jnp.where(info[flag] != 0, yes, no)


def core_order(info, mine, theirs):
    return pick(info, CORE, theirs, mine), pick(info, CORE, mine, theirs)


def joined_pieces(info, mine, theirs, axis):
    return jnp.concatenate(core_order(info, mine, theirs), axis=axis)


def exchanged(info, top_flag, first, second, received):
    return pick(info, top_flag, received, first), pick(info, top_flag + 1, received, second)


def to_send(info, first, second):
    return pick(info, CORE, first, second)


def put_pieces(info, keep_ref, send_ref, at, value, axis):
    size = value.shape[axis] // 2
    low, high = (value[:size], value[size:]) if axis == 0 else (value[:, :size], value[:, size:])
    mine, theirs = core_order(info, low.astype(BF16), high.astype(BF16))
    keep_ref[at] = mine
    send_ref[at] = theirs


def resident(shape, index=None):
    index = (lambda j, info: (0,) * len(shape)) if index is None else index
    return pl.BlockSpec(shape, index, pipeline_mode=pl.Buffered(1))


def whole_in(array):
    return (array, resident(array.shape))


def whole_out(*shape, kind=BF16, in_hbm=False):
    return (shape, kind, resident(shape), in_hbm)


def from_hbm(array):
    return pltpu.with_memory_space_constraint(array, pltpu.HBM)


def lead_spec(*shape):
    return pl.BlockSpec((None,) + shape, lambda j, info: (j,) + (0,) * len(shape))


def out_type(shape, kind, spec, in_hbm=False):
    return pltpu.HBM(shape, kind) if in_hbm else jax.ShapeDtypeStruct(shape, kind)


def call(kernel, info, steps, ins, outs, scratch, name, mebibytes, cost):
    return pl.pallas_call(
        kernel,
        grid_spec=pltpu.PrefetchScalarGridSpec(
            num_scalar_prefetch=1,
            grid=(steps,),
            in_specs=[spec for _, spec in ins],
            out_specs=[out[2] for out in outs],
            scratch_shapes=scratch,
        ),
        out_shape=[out_type(*out) for out in outs],
        compiler_params=pltpu.CompilerParams(vmem_limit_bytes=mebibytes * 1024 * 1024),
        cost_estimate=pl.CostEstimate(flops=0, bytes_accessed=cost * COST_BYTES, transcendentals=0),
        name=name,
    )(info, *[array for array, _ in ins])


def part_rows(array):
    _, count, width = array.shape
    return [
        (array, resident((None, count, width), lambda j, info: (info[ACROSS], 0, 0))),
        (array, resident((None, count // 2, width), lambda j, info: (2, info[CORE], 0))),
    ]


def joined_rows(info, a_ref, kept_ref, received_ref):
    own = info[CORE] == info[ACROSS]
    return jnp.concatenate([a_ref[...], jnp.where(own, kept_ref[...], received_ref[...])], axis=0)


def clip_bias(info, group, rows, cols, row_kind, col_kind):
    def clips(kind, places, shape, axis):
        base = ENDS + 16 * group + 4 * kind
        place = lax.broadcasted_iota(jnp.int32, shape, axis) + places.start
        return sum((place >= info[base + k]).astype(jnp.int32) for k in range(4))

    of_rows = clips(row_kind, rows, (rows.stop - rows.start, 128), 0)[:, :1]
    of_cols = clips(col_kind, cols, (8, cols.stop - cols.start), 1)[:1, :]
    return jnp.where(of_rows == of_cols, 0.0, MASKED)


def attention_blocks(full, cross, half):
    if full and cross:
        return [(None, (0, 1), slice(0, half), slice(0, 2 * half))]
    if full:
        return [(2, (0, 1), slice(0, 2 * half), slice(0, 2 * half))]
    if cross:
        return [(s, (s,), slice(0, half), slice(s * half, (s + 1) * half)) for s in range(2)]
    return [(s, (s,), slice(s * half, (s + 1) * half), slice(0, half)) for s in range(2)]


def load_halves(info, refs, exchange, lanes):
    first, second = refs[0][:, lanes], refs[1][:, lanes]
    if exchange:
        first, second = exchanged(info, TOP_BIG, first, second, refs[2][:, lanes])
    return first, second


def pairs_of(ref):
    size = 2 * HEAD_DIM
    return [(n, slice(n * size, (n + 1) * size)) for n in range(ref.shape[-1] // size)]


def query_half(info, halves, s):
    if s == 2:
        return jnp.concatenate(halves, axis=0)
    return pick(info, SECOND_PLANE, halves[1], halves[0]) if s is None else halves[s]


def head_lanes(h):
    first = lax.broadcasted_iota(jnp.int32, (1, 2 * HEAD_DIM), 1) < HEAD_DIM
    return first if h == 0 else jnp.logical_not(first)


def attend_kernel(group, counts, info, *refs):
    cross = group in (CROSS_A, CROSS_B)
    part_b = group in (SELF_B, CROSS_B)
    operands, at = [], 0
    for n in counts:
        operands.append(refs[at : at + n])
        at += n
    outs = refs[at:]
    bias_ref = outs[-1]
    p_ref = outs[-2]
    half = operands[0][0].shape[0]

    def run_pair(full, blocks, pair_index, lanes):
        q, k, v = (load_halves(info, refs, len(refs) == 3, lanes) for refs in operands)
        mixes = []
        for s, keys, rows, cols in blocks:
            query = query_half(info, q, s) * jnp.asarray(SCORE_SCALE, BF16)
            key = jnp.concatenate([k[t] for t in keys], axis=0)
            value = jnp.concatenate([v[t] for t in keys], axis=0)
            pair = []
            for h in range(2):
                own = jnp.where(head_lanes(h), query, jnp.zeros_like(query))
                scores = dot_nt(own, key) + bias_ref[rows, cols]
                top = jnp.max(scores, axis=-1, keepdims=True)
                exponent = jnp.exp(scores - top)
                total = jnp.sum(exponent, axis=-1, keepdims=True)
                probs = (exponent * (1.0 / total)).astype(BF16)
                p_ref[2 * pair_index + h, rows, cols] = probs
                pair.append(dot_nn(probs, value))
            mixes.append(jnp.where(head_lanes(0), pair[0], pair[1]).astype(BF16))
        top, bottom = mixes[0], mixes[-1]
        if full and not cross:
            top, bottom = top[:half], top[half:]
        if cross:
            outs[0][:, lanes] = top
            outs[1][:, lanes] = bottom
        else:
            outs[0][:half, lanes] = top
            outs[0][half:, lanes] = bottom
            if part_b:
                outs[1][:, lanes] = to_send(info, top, bottom)

    def run(full):
        blocks = attention_blocks(full, cross, half)

        @pl.when(pl.program_id(0) == 0)
        def _():
            for s, keys, rows, cols in blocks:
                at = rows if full else slice(0, half)
                kinds = (0, 1) if full else (2 + s, 2 + s)
                bias_ref[rows, cols] = clip_bias(info, group, at, slice(0, half * len(keys)), *kinds)

        for pair_index, lanes in pairs_of(outs[0]):
            run_pair(full, blocks, pair_index, lanes)

    pl.when(info[FULL] != 0)(lambda: run(True))
    pl.when(info[FULL] == 0)(lambda: run(False))


def attend_back_kernel(group, counts, info, *refs):
    cross = group in (CROSS_A, CROSS_B)
    part_b = group in (SELF_B, CROSS_B)
    operands, at = [], 0
    for n in counts:
        operands.append(refs[at : at + n])
        at += n
    p_ref, outs = refs[at], refs[at + 1 :]
    half = operands[0][0].shape[0]
    out_ref = outs[2] if cross else outs[0]

    def run_pair(full, blocks, pair_index, lanes):
        q, k, v, g = (load_halves(info, refs, len(refs) == 3, lanes) for refs in operands)
        queries, sums = [], {}
        head_rows = lax.broadcasted_iota(jnp.int32, (2 * HEAD_DIM, 1), 0) < HEAD_DIM
        for s, keys, rows, cols in blocks:
            query = query_half(info, q, s)
            grad = query_half(info, g, s)
            key = jnp.concatenate([k[t] for t in keys], axis=0)
            value = jnp.concatenate([v[t] for t in keys], axis=0)
            dq, dk, dv = [], [], []
            for h in range(2):
                own = jnp.where(head_lanes(h), grad, jnp.zeros_like(grad))
                probs = p_ref[2 * pair_index + h, rows, cols]
                wide_probs = probs.astype(F32)
                grad_probs = dot_nt(own, value)
                delta = jnp.sum(wide_probs * grad_probs, axis=-1, keepdims=True)
                grad_scores = (wide_probs * (grad_probs - delta)).astype(BF16)
                dq.append(dot_nn(grad_scores, key))
                dk.append(dot_tn(query, grad_scores))
                dv.append(dot_tn(grad, probs))
            queries.append((jnp.where(head_lanes(0), dq[0], dq[1]) * SCORE_SCALE).astype(BF16))
            both = tuple(jnp.concatenate([p[0][:HEAD_DIM], p[1][HEAD_DIM:]], axis=0).T for p in (dk, dv))
            sums[keys] = (sums[keys][0] + both[0], sums[keys][1] + both[1]) if keys in sums else both
        grads = []
        for t in range(2):
            dk, dv = (sums[(0, 1)] if full else sums[(t,)])
            rows = slice(t * half, (t + 1) * half) if full else slice(0, half)
            grads.append(((dk[rows] * SCORE_SCALE).astype(BF16), dv[rows].astype(BF16)))
        top, bottom = queries[0], queries[-1]
        if full and not cross:
            top, bottom = top[:half], top[half:]
        if cross:
            outs[0][:, lanes] = top
            outs[1][:, lanes] = bottom
        parts = [(g0, g1) for g0, g1 in zip(*grads)]
        if not cross:
            parts = [(top, bottom)] + parts
        for n, (first, second) in enumerate(parts):
            out_ref[n, :half, lanes] = first
            out_ref[n, half:, lanes] = second
            if part_b:
                outs[3 if cross else 1][n, :, lanes] = to_send(info, first, second)

    def run(full):
        blocks = attention_blocks(full, cross, half)
        for pair_index, lanes in pairs_of(out_ref):
            run_pair(full, blocks, pair_index, lanes)

    pl.when(info[FULL] != 0)(lambda: run(True))
    pl.when(info[FULL] == 0)(lambda: run(False))


def column_block(array, lead=None, row=0, column=0, rows=256):
    lanes = PAIRS * 2 * HEAD_DIM
    if array.ndim == 3:
        return (array, pl.BlockSpec((None, rows, lanes), lambda j, info: (lead, row, j + column)))
    return (array, pl.BlockSpec((rows, lanes), lambda j, info: (row, j + column)))


def halves_of(array, lead=None):
    return [column_block(array, lead, 0), column_block(array, lead, 1)]


def attend(info, group, operands, columns, rows=256):
    cross = group in (CROSS_A, CROSS_B)
    lanes = PAIRS * 2 * HEAD_DIM
    heads = columns // HEAD_DIM
    p_rows = rows if cross else 2 * rows
    half_out = ((rows, columns), BF16, pl.BlockSpec((rows, lanes), lambda j, info: (0, j)))
    mix_out = ((2 * rows, columns), BF16, pl.BlockSpec((2 * rows, lanes), lambda j, info: (0, j)))
    outs = [half_out, half_out] if cross else [mix_out] + ([half_out] if group == SELF_B else [])
    p_block = pl.BlockSpec((2 * PAIRS, p_rows, 2 * rows), lambda j, info: (j, 0, 0))
    p_out = ((heads, p_rows, 2 * rows), BF16, p_block, True)
    return call(
        functools.partial(attend_kernel, group, [len(o) for o in operands]),
        info,
        heads // (2 * PAIRS),
        sum(operands, []),
        outs + [p_out],
        [pltpu.VMEM((p_rows, 2 * rows), F32)],
        "attend",
        20,
        heads * 2 // 3,
    )


def attend_back(info, group, operands, probs, columns, rows=256):
    cross = group in (CROSS_A, CROSS_B)
    part_b = group in (SELF_B, CROSS_B)
    lanes = PAIRS * 2 * HEAD_DIM
    half_out = ((rows, columns), BF16, pl.BlockSpec((rows, lanes), lambda j, info: (0, j)))
    count = 2 if cross else 3

    def stacked(height):
        return ((count, height, columns), BF16, pl.BlockSpec((count, height, lanes), lambda j, info: (0, 0, j)))

    outs = [half_out, half_out] if cross else []
    outs = outs + [stacked(2 * rows)] + ([stacked(rows)] if part_b else [])
    p_block = pl.BlockSpec((2 * PAIRS,) + probs.shape[1:], lambda j, info: (j, 0, 0))
    return call(
        functools.partial(attend_back_kernel, group, [len(o) for o in operands]),
        info,
        probs.shape[0] // (2 * PAIRS),
        sum(operands, []) + [(probs, p_block)],
        outs,
        [],
        "attend_back",
        20,
        probs.shape[0],
    )


def first_project_kernel(info, a_ref, kept_ref, received_ref, norms_ref, w_ref, rows_ref, normed_ref, out_ref):
    @pl.when(pl.program_id(0) == 0)
    def _():
        rows = joined_rows(info, a_ref, kept_ref, received_ref)
        rows_ref[...] = rows
        normal, _ = norm_stats(rows.astype(F32))
        normed_ref[...] = (normal * norms_ref[0:1, :] + norms_ref[1:2, :]).astype(BF16)

    out_ref[...] = dot_nn(normed_ref[...], w_ref[...]).astype(BF16)


def first_project(info, tokens, received, norms, w_self):
    count, width, cols = w_self.shape
    rows = tokens.shape[1] + received.shape[0]
    return call(
        first_project_kernel,
        info,
        count,
        part_rows(tokens) + [whole_in(received), whole_in(norms), (w_self, lead_spec(width, cols))],
        [whole_out(rows, width, in_hbm=True), whole_out(rows, width, in_hbm=True)]
        + [((count, rows, cols), BF16, lead_spec(rows, cols))],
        [],
        "first_project",
        12,
        4,
    )


def other_project_kernel(info, normed_ref, own_b_ref, mine_ref, theirs_ref, out_ref, send_ref):
    weights = joined_pieces(info, mine_ref[...], theirs_ref[...], 0)
    out = dot_nn(normed_ref[...], weights).astype(BF16)
    out_ref[...] = out
    part_b = out.shape[0] - own_b_ref.shape[0]
    send_ref[...] = to_send(info, own_b_ref[...], out[part_b:])


def other_project(info, normed, qkv_own, mine, theirs, part_b):
    count, half, cols = mine.shape
    rows = normed.shape[0]
    own_b = pl.BlockSpec((None, part_b, cols), lambda j, info: (j, rows // part_b - 1, 0))
    return call(
        other_project_kernel,
        info,
        count,
        [whole_in(normed), (qkv_own, own_b), (mine, lead_spec(half, cols)), (theirs, lead_spec(half, cols))],
        [
            ((count, rows, cols), BF16, lead_spec(rows, cols)),
            ((count, part_b, cols), BF16, lead_spec(part_b, cols)),
        ],
        [],
        "other_project",
        9,
        3,
    )


def put_query_parts(info, value, far_ref, near_ref, left_ref, right_ref, send_ref):
    rows = left_ref.shape[0]
    cols = left_ref.shape[1]
    for h in range(2):
        at = slice(h * cols, (h + 1) * cols)
        far_ref[:, at] = value[h][:rows]
        near_ref[:, at] = value[h][rows : 2 * rows]
    left, right = value[0][2 * rows :], value[1][2 * rows :]
    left_ref[...] = left
    right_ref[...] = right
    send_ref[...] = to_send(info, left, right)


def query_outs(rows, width):
    whole, half = whole_out(rows, width, in_hbm=True), whole_out(rows, width // 2, in_hbm=True)
    return [whole, whole, half, half, half]


def self_mixes(info, mix0_ref, mix1_ref, slots_ref, received_ref):
    rows = received_ref.shape[0]
    parts = exchanged(info, TOP_BIG, slots_ref[:rows, :], slots_ref[rows:, :], received_ref[...])
    return [
        jnp.concatenate([ref[...], part], axis=0) for ref, part in zip((mix0_ref, mix1_ref), parts)
    ]


def second_project_kernel(
    info, rows_ref, norms_ref, mix0_ref, mix1_ref, slots_ref, received_ref, out_ref, query_ref, mine_ref, theirs_ref,
    hidden_ref, joined_ref, *query_refs,
):
    mixes = self_mixes(info, mix0_ref, mix1_ref, slots_ref, received_ref)
    other_out = joined_pieces(info, mine_ref[0], theirs_ref[0], 1)
    hidden = rows_ref[...].astype(F32) + dot_nn(mixes[0], out_ref[...]) + dot_nn(mixes[1], other_out)
    hidden_ref[...] = hidden
    normal, _ = norm_stats(hidden)
    joined = (normal * norms_ref[2:3, :] + norms_ref[3:4, :]).astype(BF16)
    joined_ref[...] = joined
    other_query = joined_pieces(info, mine_ref[1], theirs_ref[1], 0)
    queries = [dot_nn(joined, w).astype(BF16) for w in (query_ref[...], other_query)]
    put_query_parts(info, queries, *query_refs)


def second_project(info, rows, norms, mixes, w_self_out, w_query, mine, theirs, part_b):
    shape = rows.shape
    return call(
        second_project_kernel,
        info,
        1,
        [whole_in(a) for a in (rows, norms, *mixes, w_self_out, w_query, mine, theirs)],
        [whole_out(*shape, kind=F32, in_hbm=True), whole_out(*shape, in_hbm=True)] + query_outs(part_b, shape[1]),
        [],
        "second_project",
        17,
        5,
    )


def offer_project_kernel(info, rows_ref, own_ref, mine_ref, theirs_ref, out_ref, send_ref):
    cols = own_ref.shape[1]
    rows = send_ref.shape[0]
    other = joined_pieces(info, mine_ref[...], theirs_ref[...], 0)
    parts = [dot_nn(rows_ref[...], w).astype(BF16) for w in (own_ref[...], other)]
    for h in range(2):
        out_ref[:, h * cols : (h + 1) * cols] = parts[h]
    send_ref[...] = to_send(info, parts[0][-rows:], parts[1][-rows:])


def offer_project(info, joined, w_offer, mine, theirs, part_b):
    count, width, cols = w_offer.shape
    rows = joined.shape[0]
    piece = lead_spec(cols, cols)
    return call(
        offer_project_kernel,
        info,
        count,
        [whole_in(joined), (w_offer, lead_spec(width, cols)), (mine, piece), (theirs, piece)],
        [
            ((count, rows, 2 * cols), BF16, lead_spec(rows, 2 * cols)),
            ((count, part_b, cols), BF16, lead_spec(part_b, cols)),
        ],
        [],
        "offer_project",
        9,
        4,
    )


def reader_rows(info, far_ref, near_ref, far_b_ref, near_b_ref, received_ref):
    half = far_b_ref.shape[1]
    parts = exchanged(info, TOP_MID, far_b_ref[...], near_b_ref[...], received_ref[...])
    return [
        jnp.concatenate([ref[:, h * half : (h + 1) * half] for ref in (far_ref, near_ref)] + [parts[h]], axis=0)
        for h in range(2)
    ]


def mlp_kernel(
    info, hidden_ref, norms_ref, far_ref, near_ref, far_b_ref, near_b_ref, received_ref, w_cross_ref, mine_ref,
    theirs_ref, grad_a_ref, grad_kept_ref, grad_received_ref, up_ref, down_ref, result_ref, grad_second_ref, gm_far_ref, gm_near_ref, gm_left_ref, gm_right_ref,
    gm_send_ref, activated_ref, grad_up_ref, rows_ref, grad_ref, keep_ref, send_ref, g_norms_ref, second_ref,
    sum_ref, back_ref,
):
    step = pl.program_id(0)

    def mixes():
        return reader_rows(info, far_ref, near_ref, far_b_ref, near_b_ref, received_ref)

    def cross_weights():
        return w_cross_ref[...], joined_pieces(info, mine_ref[...], theirs_ref[...], 1)

    @pl.when(step == 0)
    def _():
        grad_ref[...] = joined_rows(info, grad_a_ref, grad_kept_ref, grad_received_ref)
        second = hidden_ref[...]
        for mix, weight in zip(mixes(), cross_weights()):
            second = second + dot_nn(mix, weight)
        second_ref[...] = second
        normal, _ = norm_stats(second)
        rows_ref[...] = (normal * norms_ref[4:5, :] + norms_ref[5:6, :]).astype(BF16)
        sum_ref[...] = second
        back_ref[...] = jnp.zeros_like(back_ref)

    rows, grad, up, down = rows_ref[...], grad_ref[...], up_ref[...], down_ref[...]
    pre = dot_nn(rows, up)
    spread = lax.erf(pre * 0.7071067811865476) * 0.5 + 0.5
    slope = spread + pre * (jnp.exp(pre * pre * -0.5) * 0.3989422804014327)
    activated = (pre * spread).astype(BF16)
    grad_up = (dot_nt(grad, down) * slope).astype(BF16)
    sum_ref[...] += dot_nn(activated, down)
    back_ref[...] += dot_nt(grad_up, up)
    activated_ref[...] = activated
    grad_up_ref[...] = grad_up

    @pl.when(step == 3)
    def _():
        result_ref[...] = sum_ref[...].astype(BF16)
        normal, inverse = norm_stats(second_ref[...])
        back, gain, shift = norm_back(back_ref[...], normal, inverse, norms_ref[4:5, :])
        g_norms_ref[0:1, :] = gain
        g_norms_ref[1:2, :] = shift
        grad_second = grad_ref[...].astype(F32) + back
        grad_second_ref[...] = grad_second
        rounded = grad_second.astype(BF16)
        parts = []
        for h, (mix, weight) in enumerate(zip(mixes(), cross_weights())):
            parts.append(dot_nt(rounded, weight).astype(BF16))
            put_pieces(info, keep_ref, send_ref, h, dot_tn(mix, rounded), 1)
        put_query_parts(info, parts, gm_far_ref, gm_near_ref, gm_left_ref, gm_right_ref, gm_send_ref)


def mlp(info, hidden, norms, mixes, w_cross, mine, theirs, cotangent, received, up, down):
    rows, width = hidden.shape
    half = width // 2
    part_b = received.shape[0]

    pieces = (up.shape[:1] + (rows, width), BF16, lead_spec(rows, width), True)
    wide = pltpu.VMEM((rows, width), F32)
    return call(
        mlp_kernel,
        info,
        4,
        [whole_in(a) for a in (hidden, norms, *mixes, w_cross)]
        + [whole_in(mine), whole_in(theirs)]
        + part_rows(cotangent)
        + [whole_in(received), (up, lead_spec(width, width)), (down, lead_spec(width, width))],
        [whole_out(rows, width), whole_out(rows, width, kind=F32, in_hbm=True)]
        + query_outs(part_b, width)
        + [pieces, pieces, whole_out(rows, width), whole_out(rows, width)]
        + [whole_out(2, half, half), whole_out(2, half, half)]
        + [whole_out(2, width, kind=F32)],
        [wide, wide, wide],
        "mlp",
        46,
        34,
    )


def mlp_weights_kernel(info, rows_ref, grad_ref, activated_ref, grad_up_ref, *outs):
    g_up = dot_tn(rows_ref[...], grad_up_ref[...]).astype(BF16)
    g_down = dot_tn(activated_ref[...], grad_ref[...]).astype(BF16)
    first = pl.program_id(0) < 2
    for keep_ref, send_ref, value in ((outs[0], outs[1], g_up), (outs[2], outs[3], g_down)):

        @pl.when(first)
        def _(keep_ref=keep_ref, value=value):
            keep_ref[...] = value

        @pl.when(jnp.logical_not(first))
        def _(send_ref=send_ref, value=value):
            send_ref[...] = value


def mlp_weights(info, rows, grad, activated, grad_up):
    count, height, width = activated.shape

    def pieces(index):
        return ((2, width, width), BF16, pl.BlockSpec((None, width, width), lambda j, info: (index(j), 0, 0)))

    keep, send = pieces(lambda j: jnp.minimum(j, 1)), pieces(lambda j: jnp.maximum(j - 2, 0))
    piece = lead_spec(height, width)
    return call(
        mlp_weights_kernel,
        info,
        count,
        [whole_in(from_hbm(rows)), whole_in(from_hbm(grad)), (from_hbm(activated), piece), (from_hbm(grad_up), piece)],
        [keep, send, keep, send],
        [],
        "mlp_weights",
        24,
        10,
    )


def second_back_kernel(
    info, far_ref, near_ref, far_b_ref, near_b_ref, received_ref, dkv_ref, slots_ref, slots_received_ref, joined_ref,
    hidden_ref, grad_second_ref, norms_ref, offer_ref, offer_mine_ref, offer_theirs_ref, query_ref, out_ref, mine_ref,
    theirs_ref, mix0_ref, mix1_ref, mix_slots_ref, mix_received_ref, cross_keep_ref, cross_send_ref, grad_hidden_ref,
    grad_mix_ref, mix_send_ref, keep_ref, send_ref, g_norms_ref, back_ref,
):
    step = pl.program_id(0)
    half = query_ref.shape[1]
    rows = received_ref.shape[0]

    def add(at, grads, weights, first):
        joined = joined_ref[...]
        total = dot_nt(grads[0], weights[0]) + dot_nt(grads[1], weights[1])
        back_ref[...] = total if first else back_ref[...] + total
        for h in range(2):
            put_pieces(info, keep_ref, send_ref, (h, at), dot_tn(joined, grads[h]), 0)

    def add_offer(at):
        parts = exchanged(info, TOP_BIG, slots_ref[:rows, :], slots_ref[rows:, :], slots_received_ref[...])
        grads = [
            jnp.concatenate([dkv_ref[:, h * half : (h + 1) * half], parts[h]], axis=0) for h in range(2)
        ]
        other = joined_pieces(info, offer_mine_ref[...], offer_theirs_ref[...], 0)
        add(at, grads, (offer_ref[...], other), at == 0)

    pl.when(step == 0)(lambda: add_offer(0))
    pl.when(step == 1)(lambda: add_offer(1))

    @pl.when(step == 2)
    def _():
        for h in range(2):
            keep_ref[h, 4] = cross_keep_ref[h]
            send_ref[h, 4] = cross_send_ref[h]
        grads = reader_rows(info, far_ref, near_ref, far_b_ref, near_b_ref, received_ref)
        add(3, grads, (query_ref[...], joined_pieces(info, mine_ref[1], theirs_ref[1], 0)), False)
        normal, inverse = norm_stats(hidden_ref[...])
        back, gain, shift = norm_back(back_ref[...], normal, inverse, norms_ref[2:3, :])
        g_norms_ref[0:1, :] = gain
        g_norms_ref[1:2, :] = shift
        grad_hidden = grad_second_ref[...] + back
        grad_hidden_ref[...] = grad_hidden
        rounded = grad_hidden.astype(BF16)
        mixes = self_mixes(info, mix0_ref, mix1_ref, mix_slots_ref, mix_received_ref)
        parts = []
        for h, weight in enumerate((out_ref[...], joined_pieces(info, mine_ref[0], theirs_ref[0], 1))):
            part = dot_nt(rounded, weight).astype(BF16)
            grad_mix_ref[h] = part
            parts.append(part[-rows:])
            put_pieces(info, keep_ref, send_ref, (h, 2), dot_tn(mixes[h], rounded), 1)
        mix_send_ref[...] = to_send(info, *parts)


def second_back(
    info, grad_q, dkv, slots, slots_received, joined, hidden, grad_second, norms, w_offer, offer_mine, offer_theirs,
    w_query, w_self_out, mine, theirs, mixes, cross_keep, cross_send,
):
    rows, width = hidden.shape
    half = width // 2
    part_b = slots_received.shape[1]

    def offered(array, *shape):
        return (array, pl.BlockSpec((None,) + shape, lambda j, info: (jnp.minimum(j, 1), 0, 0)))

    return call(
        second_back_kernel,
        info,
        3,
        [whole_in(a) for a in grad_q]
        + [offered(dkv, *dkv.shape[1:]), offered(slots, *slots.shape[1:])]
        + [offered(slots_received, *slots_received.shape[1:])]
        + [whole_in(a) for a in (joined, hidden, grad_second, norms)]
        + [offered(w_offer, width, half), offered(offer_mine, half, half), offered(offer_theirs, half, half)]
        + [whole_in(a) for a in (w_query, w_self_out, mine, theirs, *mixes, cross_keep, cross_send)],
        [whole_out(rows, width, kind=F32, in_hbm=True), whole_out(2, rows, half), whole_out(part_b, half)]
        + [whole_out(2, 5, half, half), whole_out(2, 5, half, half), whole_out(2, width, kind=F32)],
        [pltpu.VMEM((rows, width), F32)],
        "second_back",
        35,
        12,
    )


def first_grads(info, own_ref, other_ref, slots_ref, received_ref):
    rows = received_ref.shape[0]
    parts = exchanged(info, TOP_BIG, slots_ref[:rows, :], slots_ref[rows:, :], received_ref[...])
    return [jnp.concatenate([ref[...], part], axis=0) for ref, part in zip((own_ref, other_ref), parts)]


def first_weights_kernel(half, info, grad_ref, slots_ref, received_ref, normed_ref, keep_ref, send_ref):
    rows = received_ref.shape[0]
    parts = exchanged(info, TOP_BIG, slots_ref[:rows, :], slots_ref[rows:, :], received_ref[...])
    value = dot_tn(normed_ref[...], jnp.concatenate([grad_ref[...], parts[half]], axis=0))
    put_pieces(info, keep_ref, send_ref, slice(None), value, 0)


def first_ins(*arrays):
    return [(a, lead_spec(*a.shape[1:])) for a in arrays]


def first_weights(info, half_index, grads, slots, received, normed):
    half = grads.shape[2]
    piece = ((3, half, half), BF16, lead_spec(half, half))
    return call(
        functools.partial(first_weights_kernel, half_index),
        info,
        3,
        first_ins(grads, slots, received) + [whole_in(normed)],
        [piece, piece],
        [],
        "first_weights",
        12,
        3,
    )


def first_back_kernel(
    info, own_ref, other_ref, slots_ref, received_ref, rows_ref, grad_hidden_ref, norms_ref, w_own_ref, mine_ref,
    theirs_ref, grad_early_ref, grad_late_ref, g_norms_ref, back_ref,
):
    step = pl.program_id(0)
    grads = first_grads(info, own_ref, other_ref, slots_ref, received_ref)
    other = joined_pieces(info, mine_ref[...], theirs_ref[...], 0)
    total = dot_nt(grads[0], w_own_ref[...]) + dot_nt(grads[1], other)

    @pl.when(step == 0)
    def _():
        back_ref[...] = total

    @pl.when(step > 0)
    def _():
        back_ref[...] += total

    @pl.when(step == pl.num_programs(0) - 1)
    def _():
        normal, inverse = norm_stats(rows_ref[...].astype(F32))
        back, gain, shift = norm_back(back_ref[...], normal, inverse, norms_ref[0:1, :])
        g_norms_ref[0:1, :] = gain
        g_norms_ref[1:2, :] = shift
        grad_rows = (grad_hidden_ref[...] + back).astype(BF16)
        late = grad_late_ref.shape[0]
        grad_late_ref[...] = grad_rows[:late]
        grad_early_ref[...] = grad_rows[late:]


def first_back(info, own, other, slots, received, rows, grad_hidden, norms, w_self, mine, theirs):
    count = own.shape[0]
    width = rows.shape[1]
    late = received.shape[1]
    ins = first_ins(own, other, slots, received)
    ins += [whole_in(a) for a in (rows, grad_hidden, norms)]
    ins += [(a, lead_spec(*a.shape[1:])) for a in (w_self, mine, theirs)]
    return call(
        first_back_kernel,
        info,
        count,
        ins,
        [whole_out(2 * late, width), whole_out(late, width), whole_out(2, width, kind=F32)],
        [pltpu.VMEM(rows.shape, F32)],
        "first_back",
        24,
        8,
    )


def row_of(table, index):
    return lax.dynamic_index_in_dim(table, index, 0, keepdims=False)


def scalars(clip_len, index, across, quarter):
    core = index % 2
    is_big = index < 2 * quarter
    is_mid = jnp.logical_and(index >= 2 * quarter, index < 3 * quarter)
    first, last = core == 0, core == 1
    flags = [
        is_big,
        core,
        across,
        jnp.logical_and(is_big, index >= quarter),
        jnp.logical_and(is_big, last),
        jnp.logical_and(is_big, first),
        jnp.logical_and(is_mid, last),
        jnp.logical_and(is_mid, first),
    ]
    shared = index - core + across
    lens_a, lens_b = row_of(clip_len, across), clip_len[2]
    big_a = row_of(lens_a, jnp.minimum(index, 2 * quarter - 1))
    big_b = row_of(lens_b, jnp.minimum(shared, 2 * quarter - 1))
    sets_a = [row_of(lens_a, index % quarter + s * quarter) for s in range(2)]
    sets_b = [row_of(lens_b, shared % quarter + core * quarter)] * 2
    table = jnp.stack(
        [2 * big_a, 2 * big_a, *sets_a, 2 * big_b, 2 * big_b, *sets_b]
        + [big_a, 2 * big_a, *sets_a, big_b, 2 * big_b, *sets_b]
    )
    ends = [table[:, 0]]
    for k in range(1, 4):
        ends.append(ends[-1] + table[:, k])
    flags = jnp.stack([flag.astype(jnp.int32) for flag in flags])
    return jnp.concatenate([flags, jnp.stack(ends, axis=1).reshape(-1)])


def local(
    tokens,
    cotangent,
    clip_len,
    ln_params,
    w_self,
    w_self_out,
    w_offer,
    w_query,
    w_cross_out,
    w_up,
    w_down,
):
    index = lax.axis_index("clip")
    across = lax.axis_index("head")
    count = lax.axis_size("clip")
    quarter = count // 4
    levels = (2 * quarter).bit_length() - 1
    core = index % 2
    is_big = index < 2 * quarter
    is_mid = jnp.logical_and(index >= 2 * quarter, index < 3 * quarter)
    own_micro2 = core == across
    norms = ln_params[0]
    w_self, w_self_out, w_offer, w_query = w_self[0], w_self_out[0], w_offer[0], w_query[0]
    w_cross_out, w_up, w_down = w_cross_out[0], w_up[0], w_down[0]
    half = w_query.shape[1]
    part_a = tokens.shape[1]
    part_b = part_a // 2
    wide = 2 * half

    near = [(i, i - quarter) for i in range(2 * quarter, count)]
    far = [(i, i - 2 * quarter) for i in range(2 * quarter, 3 * quarter)]
    far += [(i, i - quarter) for i in range(3 * quarter, count)]

    def to_server(far_rows, near_rows):
        second = lax.ppermute(near_rows, "clip", near)
        return lax.ppermute(far_rows, "clip", far), second

    def to_reader(far_rows, near_rows):
        second = lax.ppermute(near_rows, "clip", [(b, a) for a, b in near])
        return lax.ppermute(far_rows, "clip", [(b, a) for a, b in far]), second

    def reader_slots(left, right, received):
        top = jnp.where(jnp.logical_and(is_mid, core == 1), received, left)
        return top, jnp.where(jnp.logical_and(is_mid, core == 0), received, right)

    def from_server(top, bottom):
        return top, bottom, other_core(jnp.where(core == 0, bottom, top))

    def over_level(part, bit):
        return over_bit(part, bit, 2 * quarter if bit == levels - 1 else None)

    def add(left, right):
        return (left.astype(F32) + right.astype(F32)).astype(BF16)

    def last_levels(total, received):
        total = total if received is None else add(total, received)
        for bit in range(3, levels):
            total = add(total, over_level(total, bit))
        return total

    def whole(mine, axis):
        return in_core_order(core, mine, other_core(mine), axis).astype(F32)[None]

    def all_rows(a_mine, b_mine, a_theirs, b_theirs):
        kept = jnp.where(own_micro2, b_mine, b_theirs)
        received = other_core(jnp.where(own_micro2, b_theirs, b_mine))
        micro2 = in_core_order(core, kept, received, 0)
        micro0 = jnp.where(across == 0, a_mine, a_theirs)
        micro1 = jnp.where(across == 0, a_theirs, a_mine)
        return jnp.stack([micro0, micro1, micro2])


    def over_head_rows(array, start, stop, *others):
        return over_head(after(array[start:stop], *others) if others else array[start:stop])

    def rows_piece(array, piece):
        return lax.dynamic_slice(array, (2, piece * part_b, 0), (1, part_b, wide))[0]

    self_mine = over_head(core_piece(w_self, core, 1))
    tokens_received = other_core(rows_piece(tokens, 1 - core))
    info = scalars(clip_len, index, across, quarter)
    rows, normed, qkv_own = first_project(info, tokens, tokens_received, norms, w_self)
    self_0 = [halves_of(qkv_own, n) for n in range(3)]
    mix_0, p_0 = attend(info, SELF_A, self_0, half)
    first_piece = jnp.stack([core_piece(w_self_out, core, 1), core_piece(w_query, core, 0)])
    offer_piece, up_piece, down_piece = core_piece(w_offer, core, 1), core_piece(w_up, core, 1), core_piece(w_down, core, 0)
    cross_piece = core_piece(w_cross_out, core, 1)
    (self_mine, mix_0, first_piece) = fence(self_mine, mix_0, first_piece)

    first_mine = over_head(first_piece)
    self_theirs = other_core(self_mine)
    qkv_other, qkv_send = other_project(info, normed, qkv_own, self_mine, self_theirs, part_b)
    self_1 = [halves_of(qkv_other, n) for n in range(3)]
    mix_1, p_1 = attend(info, SELF_A, self_1, half)
    qkv_received, first_mine, mix_1, offer_piece = fence(other_core(qkv_send), first_mine, mix_1, offer_piece)

    offer_mine = over_head(offer_piece[0])
    self_b = [
        [column_block(qkv_own, n, 2), column_block(qkv_other, n, 2), column_block(qkv_received, n)] for n in range(3)
    ]
    mix_s, mix_send, p_s = attend(info, SELF_B, self_b, half)
    first_theirs = other_core(first_mine)
    mix_s, mix_send, offer_mine, offer_piece = fence(mix_s, mix_send, offer_mine, offer_piece)

    offer_last = over_head(offer_piece[1])
    mixes = (mix_0, mix_1, mix_s, other_core(mix_send))
    hidden, joined, q_far, q_near, q_left, q_right, q_send = second_project(
        info, rows, norms, mixes, w_self_out, w_query, first_mine, first_theirs, part_b
    )
    q_far, q_near, q_left, q_right, q_send, joined, offer_mine, offer_last, cross_piece, up_piece, down_piece, cotangent = fence(
        q_far, q_near, q_left, q_right, q_send, joined, offer_mine, offer_last, cross_piece, up_piece, down_piece, cotangent
    )

    asked_a = to_server(q_far, q_near)
    up_mine = [over_head(up_piece[:576])]
    q_top, q_bottom = reader_slots(q_left, q_right, other_core(q_send))
    offer_mine = jnp.stack([offer_mine, offer_last])
    offer_theirs = other_core(offer_mine)
    offer, offer_send = offer_project(info, joined, w_offer, offer_mine, offer_theirs, part_b)
    cotangent_received = other_core(rows_piece(cotangent, 1 - core))
    offer_received = other_core(offer_send)
    *asked_a, q_top, q_bottom, offer, offer_received, cotangent_received, up_mine[0], up_piece, cross_piece = fence(
        *asked_a, q_top, q_bottom, offer, offer_received, cotangent_received, up_mine[0], up_piece, cross_piece
    )

    asked_b = to_server(q_top, q_bottom)
    up_mine.append(over_head(up_piece[576:]))
    cross_mine = over_head(cross_piece)
    cross_a = [[column_block(asked_a[0]), column_block(asked_a[1])]] + [halves_of(offer, n) for n in range(2)]
    far_a, near_a, cross_p_a = attend(info, CROSS_A, cross_a, wide)
    far_a, near_a, asked_b_far, asked_b_near, up_mine[1], cross_mine, down_piece = fence(
        far_a, near_a, *asked_b, up_mine[1], cross_mine, down_piece
    )

    back_a = to_reader(far_a, near_a)
    down_mine = [over_head(down_piece[:576])]
    cross_b = [[column_block(asked_b_far), column_block(asked_b_near)]] + [
        [
            column_block(offer, n, 2),
            column_block(offer, n, 2, half // (PAIRS * 2 * HEAD_DIM)),
            column_block(offer_received, n),
        ]
        for n in range(2)
    ]
    far_b, near_b, cross_p_b = attend(info, CROSS_B, cross_b, half)
    up_mine = jnp.concatenate(up_mine)
    up_theirs = other_core(up_mine)
    cross_theirs = other_core(cross_mine)
    *back_a, far_b, near_b, up_mine, up_theirs, cross_theirs, down_mine[0], down_piece = fence(
        *back_a, far_b, near_b, up_mine, up_theirs, cross_theirs, down_mine[0], down_piece
    )

    back_b = to_reader(far_b, near_b)
    down_mine = jnp.concatenate([down_mine[0], over_head(down_piece[576:])])
    up_pieces = jnp.stack([core_piece(w_up, core, 1), up_mine, core_piece(w_up, 1 - core, 1), up_theirs])
    *back_b, down_mine, up_pieces = fence(*back_b, down_mine, up_pieces)

    back_b = from_server(*back_b)
    down_theirs = other_core(down_mine)
    down_pieces = jnp.stack([core_piece(w_down, core, 0), down_mine, core_piece(w_down, 1 - core, 0), down_theirs])
    (
        result, grad_second, gm_far, gm_near, gm_left, gm_right, gm_send,
        activated, grad_up, mlp_rows, grad_out, cross_keep, cross_send, norms_3,
    ) = mlp(
        info, hidden, norms, (*back_a, *back_b), w_cross_out, cross_mine, cross_theirs, cotangent, cotangent_received,
        up_pieces, down_pieces,
    )
    result, gm_far, gm_near, gm_left, gm_right, gm_send, activated, grad_up, mlp_rows, grad_out = fence(
        result, gm_far, gm_near, gm_left, gm_right, gm_send, activated, grad_up, mlp_rows, grad_out
    )

    grad_a = to_server(gm_far, gm_near)
    layer_x = [over_head(result[:448])]
    gm_top, gm_bottom = reader_slots(gm_left, gm_right, other_core(gm_send))
    up_keep, up_send, down_keep, down_send = mlp_weights(info, mlp_rows, grad_out, activated, grad_up)
    *grad_a, gm_top, gm_bottom, layer_x[0], result, down_keep, down_send, up_keep, up_send = fence(
        *grad_a, gm_top, gm_bottom, layer_x[0], result, down_keep, down_send, up_keep, up_send
    )

    grad_b = to_server(gm_top, gm_bottom)
    layer_x.append(over_head(result[448:]))
    down_received = other_core(down_send)
    down_out = [add(down_keep[1, :576], down_received[1, :576]), add(down_keep[1, 576:], down_received[1, 576:])]
    grad_in = [column_block(grad_a[0]), column_block(grad_a[1])]
    dq_far, dq_near, dkv_a = attend_back(info, CROSS_A, cross_a + [grad_in], cross_p_a, wide)
    dq_far, dq_near, grad_b_far, grad_b_near, layer_x[1], *down_out, up_keep, up_send = fence(
        dq_far, dq_near, *grad_b, layer_x[1], *down_out, up_keep, up_send
    )

    dq_a = to_reader(dq_far, dq_near)
    down_x = [over_head(down_out[0])]
    grad_in = [column_block(grad_b_far), column_block(grad_b_near)]
    dq_b_far, dq_b_near, dkv_b, dkv_send = attend_back(info, CROSS_B, cross_b + [grad_in], cross_p_b, half)
    up_received = other_core(up_send)
    up_out = [add(up_keep[1, :192], up_received[1, :192]), add(up_keep[1, 192:], up_received[1, 192:])]
    down_out[1] = jnp.concatenate([down_out[1], up_out[0]])
    *dq_a, dq_b_far, dq_b_near, dkv_send, down_x[0], up_out[1], down_out[1] = fence(
        *dq_a, dq_b_far, dq_b_near, dkv_send, down_x[0], up_out[1], down_out[1]
    )

    dq_b = to_reader(dq_b_far, dq_b_near)
    both_x = over_head(down_out[1])
    down_own = add(down_keep[0, :576], down_received[0, :576])
    down_own = add(down_own, down_x[0])
    down_first, down_rest = down_own[:384], down_own[384:]
    down_y = [over_level(down_first, 1)]
    *dq_b, dkv_send, both_x, up_out[1], down_first, down_rest, down_y[0] = fence(
        *dq_b, dkv_send, both_x, up_out[1], down_first, down_rest, down_y[0]
    )

    dkv_received = other_core(dkv_send)
    down_x.append(both_x[:192])
    up_x = [both_x[192:], over_head(up_out[1])]
    down_second = add(add(down_keep[0, 576:], down_received[0, 576:]), down_x[1])
    down_second = jnp.concatenate([down_rest, down_second])
    down_y.append(over_level(down_second, 1))
    down_first = add(down_first, down_y[0])
    down_z = [over_level(down_first, 2)]
    grad_hidden, grad_mix, grad_send, mid_keep, mid_send, norms_2 = second_back(
        info, (*dq_a, *from_server(*dq_b)), dkv_a, dkv_b, dkv_received, joined, hidden, grad_second, norms, w_offer,
        offer_mine, offer_theirs, w_query, w_self_out, first_mine, first_theirs, mixes, cross_keep, cross_send,
    )
    up_own = add(up_keep[0], up_received[0])
    grad_hidden, grad_mix, grad_send, mid_keep, mid_send, up_x[1], up_own, down_second, down_y[1], down_first, down_z[0] = fence(
        grad_hidden, grad_mix, grad_send, mid_keep, mid_send, up_x[1], up_own, down_second, down_y[1], down_first, down_z[0]
    )

    (back_1,) = attend_back(info, SELF_A, self_1 + [halves_of(grad_mix, 1)], p_1, half)
    grad_received = other_core(grad_send)
    mid_received = other_core(mid_send)
    mid_out = [add(mid_keep[1, :3], mid_received[1, :3]), add(mid_keep[1, 3:], mid_received[1, 3:])]
    up_total = add(up_own, jnp.concatenate(up_x))
    up_y = [over_level(up_total[:384], 1)]
    down_second = add(down_second, down_y[1])
    down_z.append(over_level(down_second, 2))
    back_1, grad_mix, grad_received, mid_out[0], mid_out[1], up_total, up_y[0], down_second, down_z[1] = fence(
        back_1, grad_mix, grad_received, *mid_out, up_total, up_y[0], down_second, down_z[1]
    )

    mid_x = [over_head(mid_out[0])]
    up_y.append(over_level(up_total[384:], 1))
    up_first = add(up_total[:384], up_y[0])
    up_z = [over_level(up_first, 2)]
    grad_in = [column_block(grad_mix, 0, 2), column_block(grad_mix, 1, 2), column_block(grad_received)]
    back_s, back_send = attend_back(info, SELF_B, self_b + [grad_in], p_s, half)
    back_received = other_core(back_send)
    other_keep, other_send = first_weights(info, 1, back_1, back_s, back_received, normed)
    mid_own = add(mid_keep[0], mid_received[0])
    (
        back_s, back_received, other_keep, other_send, mid_x[0], mid_own, mid_out[1],
        up_total, up_y[1], up_first, up_z[0], grad_mix,
    ) = fence(
        back_s, back_received, other_keep, other_send, mid_x[0], mid_own, mid_out[1],
        up_total, up_y[1], up_first, up_z[0], grad_mix,
    )

    mid_x.append(over_head(mid_out[1]))
    mid_first = add(mid_own[:3], mid_x[0])
    mid_y = [over_level(mid_first, 1)]
    up_second = add(up_total[384:], up_y[1])
    up_z.append(over_level(up_second, 2))
    (back_0,) = attend_back(info, SELF_A, self_0 + [halves_of(grad_mix, 0)], p_0, half)
    own_keep, own_send = first_weights(info, 0, back_0, back_s, back_received, normed)
    last_out = add(other_keep, other_core(other_send))
    down_total = jnp.concatenate([last_levels(down_first, down_z[0]), last_levels(down_second, down_z[1])])
    grad_down_weight = whole(down_total, 0)
    (
        back_0, own_keep, own_send, last_out, mid_x[1], mid_first, mid_y[0], up_second, up_z[1], mid_own,
        grad_down_weight,
    ) = fence(
        back_0, own_keep, own_send, last_out, mid_x[1], mid_first, mid_y[0], up_second, up_z[1], mid_own,
        grad_down_weight,
    )

    last_x = over_head(last_out)
    mid_second = add(mid_own[3:], mid_x[1])
    mid_y.append(over_level(mid_second, 1))
    mid_first = add(mid_first, mid_y[0])
    mid_z = over_level(mid_first, 2)
    own_received = other_core(own_send)
    last_own = [add(own_keep[:2], own_received[:2]), add(own_keep[2:], own_received[2:])]
    grad_early, grad_late, norms_1 = first_back(
        info, back_0, back_1, back_s, back_received, rows, grad_hidden, norms, w_self, self_mine, self_theirs
    )
    up_total = jnp.concatenate([last_levels(up_first, up_z[0]), last_levels(up_second, up_z[1])])
    grad_up_weight = whole(up_total, 1)
    grad_early, grad_late, norms_1, last_own[0], last_own[1], last_x, mid_second, mid_y[1], mid_first, mid_z, grad_up_weight = fence(
        grad_early, grad_late, norms_1, *last_own, last_x, mid_second, mid_y[1], mid_first, mid_z, grad_up_weight
    )

    early_x = over_head(grad_early)
    first, second = add(last_own[0], last_x[:2]), add(last_own[1], last_x[2:])
    first_y, second_z = over_level(first, 1), over_level(second, 2)
    norm_grads = jnp.concatenate([norms_1, norms_2, norms_3], axis=0)
    norm_grads = norm_grads + other_core(norm_grads)
    norm_grads = norm_grads + over_level(norm_grads, 1)
    (
        early_x, grad_late, first, first_y, second, second_z, norm_grads, mid_first, mid_second
    ) = fence(
        early_x, grad_late, first, first_y, second, second_z, norm_grads, mid_first, mid_second
    )

    late_x = over_head(grad_late)
    first, second = add(first, first_y), add(second, second_z)
    first_z, second_y = over_level(first, 2), over_level(second, 1)
    norm_grads = norm_grads + over_head(norm_grads)
    layer_x = after(jnp.concatenate(layer_x), first)
    layer_out = all_rows(result[:part_a], result[part_a:], layer_x[:part_a], layer_x[part_a:])
    mid_total = last_levels(mid_first, mid_z)
    rest_total = add(mid_second, mid_y[1])
    for bit in range(2, levels - 1):
        rest_total = add(rest_total, over_level(rest_total, bit))

    early = [layer_out, late_x, whole(mid_total[2], 1), whole(mid_total[:2], 1), whole(rest_total[0], 0)]
    early += [whole(rest_total[1], 1)]
    first, first_z, second, second_y, norm_grads, *early = fence(first, first_z, second, second_y, norm_grads, *early)
    layer_out, late_x, *grad_weights = early
    a_mine, a_theirs = (jnp.concatenate([x, y[:part_b]]) for x, y in ((grad_late, grad_early), (late_x, early_x)))
    grad_tokens = all_rows(a_mine, grad_early[part_b:], a_theirs, early_x[part_b:]).astype(F32)

    for bit in range(2, levels):
        norm_grads = norm_grads + over_level(norm_grads, bit)
    last_total = jnp.concatenate([last_levels(first, first_z), last_levels(second, second_y)])
    return (layer_out, grad_tokens, norm_grads[None], whole(last_total, 1), *grad_weights, grad_up_weight, grad_down_weight)


def solution(mesh):
    return jax.shard_map(
        local,
        mesh=mesh,
        in_specs=(
            P(None, "clip", None),
            P(None, "clip", None),
            P(),
            P("clip", None, None),
            P("clip", None, None, "head"),
            P("clip", "head", None),
            P("clip", None, None, "head"),
            P("clip", None, "head"),
            P("clip", "head", None),
            P("clip", None, "head"),
            P("clip", "head", None),
        ),
        out_specs=(
            P(None, "clip", None),
            P(None, "clip", None),
            P("clip", None, None),
            P("clip", None, None, "head"),
            P("clip", "head", None),
            P("clip", None, None, "head"),
            P("clip", None, "head"),
            P("clip", "head", None),
            P("clip", None, "head"),
            P("clip", "head", None),
        ),
        check_vma=False,
    )
```

```python
import functools

import jax
import jax.numpy as jnp
from jax import lax
from jax.experimental import pallas as pl
from jax.experimental.pallas import tpu as pltpu
from jax.sharding import PartitionSpec as P


HEAD_DIM = 64
PAIRS = 3
EPSILON = 1e-06
SCORE_SCALE = 0.125
MASKED = -1e30
BF16 = jnp.bfloat16
F32 = jnp.float32
COST_BYTES = 1

FULL, CORE, ACROSS, SECOND_PLANE, TOP_BIG, BOTTOM_BIG, TOP_MID, BOTTOM_MID, ENDS = range(9)
SELF_A, SELF_B, CROSS_A, CROSS_B = range(4)


def over_head(value):
    return lax.ppermute(value, "head", [(0, 1), (1, 0)])


def over_bit(value, bit, count=None):
    count = lax.axis_size("clip") if count is None else count
    return lax.ppermute(value, "clip", [(i, i ^ (1 << bit)) for i in range(count)])


def other_core(value):
    return over_bit(value, 0)


def fence(*values):
    return lax.optimization_barrier(values)


def after(value, *others):
    return lax.optimization_barrier((value,) + others)[0]


def in_core_order(core, mine, theirs, axis):
    first = jnp.where(core == 0, mine, theirs)
    second = jnp.where(core == 0, theirs, mine)
    return jnp.concatenate([first, second], axis=axis)


def core_piece(value, piece, axis):
    size = value.shape[axis] // 2
    return lax.dynamic_slice_in_dim(value, piece * size, size, axis)


def dot_nt(left, right):
    return lax.dot_general(left, right, (((1,), (1,)), ((), ())), preferred_element_type=F32)


def dot_tn(left, right):
    return lax.dot_general(left, right, (((0,), (0,)), ((), ())), preferred_element_type=F32)


def dot_nn(left, right):
    return jnp.dot(left, right, preferred_element_type=F32)


def norm_stats(rows):
    mean = jnp.mean(rows, axis=-1, keepdims=True)
    centered = rows - mean
    variance = jnp.mean(centered * centered, axis=-1, keepdims=True)
    inverse = lax.rsqrt(variance + EPSILON)
    return centered * inverse, inverse


def norm_back(grad, normal, inverse, gain):
    scaled = grad * gain
    mean = jnp.mean(scaled, axis=-1, keepdims=True)
    along = jnp.mean(scaled * normal, axis=-1, keepdims=True)
    grad_rows = (scaled - mean - normal * along) * inverse
    gain_grad = jnp.sum(grad * normal, axis=0, keepdims=True)
    return grad_rows, gain_grad, jnp.sum(grad, axis=0, keepdims=True)


def pick(info, flag, yes, no):
    return jnp.where(info[flag] != 0, yes, no)


def core_order(info, mine, theirs):
    return pick(info, CORE, theirs, mine), pick(info, CORE, mine, theirs)


def joined_pieces(info, mine, theirs, axis):
    return jnp.concatenate(core_order(info, mine, theirs), axis=axis)


def exchanged(info, top_flag, first, second, received):
    return pick(info, top_flag, received, first), pick(info, top_flag + 1, received, second)


def to_send(info, first, second):
    return pick(info, CORE, first, second)


def put_pieces(info, keep_ref, send_ref, at, value, axis):
    size = value.shape[axis] // 2
    low, high = (value[:size], value[size:]) if axis == 0 else (value[:, :size], value[:, size:])
    mine, theirs = core_order(info, low.astype(BF16), high.astype(BF16))
    keep_ref[at] = mine
    send_ref[at] = theirs


def resident(shape, index=None):
    index = (lambda j, info: (0,) * len(shape)) if index is None else index
    return pl.BlockSpec(shape, index, pipeline_mode=pl.Buffered(1))


def whole_in(array):
    return (array, resident(array.shape))


def whole_out(*shape, kind=BF16, in_hbm=False):
    return (shape, kind, resident(shape), in_hbm)


def from_hbm(array):
    return pltpu.with_memory_space_constraint(array, pltpu.HBM)


def lead_spec(*shape):
    return pl.BlockSpec((None,) + shape, lambda j, info: (j,) + (0,) * len(shape))


def out_type(shape, kind, spec, in_hbm=False):
    return pltpu.HBM(shape, kind) if in_hbm else jax.ShapeDtypeStruct(shape, kind)


def call(kernel, info, steps, ins, outs, scratch, name, mebibytes, cost):
    return pl.pallas_call(
        kernel,
        grid_spec=pltpu.PrefetchScalarGridSpec(
            num_scalar_prefetch=1,
            grid=(steps,),
            in_specs=[spec for _, spec in ins],
            out_specs=[out[2] for out in outs],
            scratch_shapes=scratch,
        ),
        out_shape=[out_type(*out) for out in outs],
        compiler_params=pltpu.CompilerParams(vmem_limit_bytes=mebibytes * 1024 * 1024),
        cost_estimate=pl.CostEstimate(flops=0, bytes_accessed=cost * COST_BYTES, transcendentals=0),
        name=name,
    )(info, *[array for array, _ in ins])


def part_rows(array):
    _, count, width = array.shape
    return [
        (array, resident((None, count, width), lambda j, info: (info[ACROSS], 0, 0))),
        (array, resident((None, count // 2, width), lambda j, info: (2, info[CORE], 0))),
    ]


def joined_rows(info, a_ref, kept_ref, received_ref):
    own = info[CORE] == info[ACROSS]
    return jnp.concatenate([a_ref[...], jnp.where(own, kept_ref[...], received_ref[...])], axis=0)


def clip_bias(info, group, rows, cols, row_kind, col_kind):
    def clips(kind, places, shape, axis):
        base = ENDS + 16 * group + 4 * kind
        place = lax.broadcasted_iota(jnp.int32, shape, axis) + places.start
        return sum((place >= info[base + k]).astype(jnp.int32) for k in range(4))

    of_rows = clips(row_kind, rows, (rows.stop - rows.start, 128), 0)[:, :1]
    of_cols = clips(col_kind, cols, (8, cols.stop - cols.start), 1)[:1, :]
    return jnp.where(of_rows == of_cols, 0.0, MASKED)


def attention_blocks(full, cross, half):
    if full and cross:
        return [(None, (0, 1), slice(0, half), slice(0, 2 * half))]
    if full:
        return [(2, (0, 1), slice(0, 2 * half), slice(0, 2 * half))]
    if cross:
        return [(s, (s,), slice(0, half), slice(s * half, (s + 1) * half)) for s in range(2)]
    return [(s, (s,), slice(s * half, (s + 1) * half), slice(0, half)) for s in range(2)]


def load_halves(info, refs, exchange, lanes):
    first, second = refs[0][:, lanes], refs[1][:, lanes]
    if exchange:
        first, second = exchanged(info, TOP_BIG, first, second, refs[2][:, lanes])
    return first, second


def pairs_of(ref):
    size = 2 * HEAD_DIM
    return [(n, slice(n * size, (n + 1) * size)) for n in range(ref.shape[-1] // size)]


def query_half(info, halves, s):
    if s == 2:
        return jnp.concatenate(halves, axis=0)
    return pick(info, SECOND_PLANE, halves[1], halves[0]) if s is None else halves[s]


def head_lanes(h):
    first = lax.broadcasted_iota(jnp.int32, (1, 2 * HEAD_DIM), 1) < HEAD_DIM
    return first if h == 0 else jnp.logical_not(first)


def attend_kernel(group, counts, info, *refs):
    cross = group in (CROSS_A, CROSS_B)
    part_b = group in (SELF_B, CROSS_B)
    operands, at = [], 0
    for n in counts:
        operands.append(refs[at : at + n])
        at += n
    outs = refs[at:]
    bias_ref = outs[-1]
    p_ref = outs[-2]
    half = operands[0][0].shape[0]

    def run_pair(full, blocks, pair_index, lanes):
        q, k, v = (load_halves(info, refs, len(refs) == 3, lanes) for refs in operands)
        mixes = []
        for s, keys, rows, cols in blocks:
            query = query_half(info, q, s) * jnp.asarray(SCORE_SCALE, BF16)
            key = jnp.concatenate([k[t] for t in keys], axis=0)
            value = jnp.concatenate([v[t] for t in keys], axis=0)
            pair = []
            for h in range(2):
                own = jnp.where(head_lanes(h), query, jnp.zeros_like(query))
                scores = dot_nt(own, key) + bias_ref[rows, cols]
                top = jnp.max(scores, axis=-1, keepdims=True)
                exponent = jnp.exp(scores - top)
                total = jnp.sum(exponent, axis=-1, keepdims=True)
                probs = (exponent * (1.0 / total)).astype(BF16)
                p_ref[2 * pair_index + h, rows, cols] = probs
                pair.append(dot_nn(probs, value))
            mixes.append(jnp.where(head_lanes(0), pair[0], pair[1]).astype(BF16))
        top, bottom = mixes[0], mixes[-1]
        if full and not cross:
            top, bottom = top[:half], top[half:]
        if cross:
            outs[0][:, lanes] = top
            outs[1][:, lanes] = bottom
        else:
            outs[0][:half, lanes] = top
            outs[0][half:, lanes] = bottom
            if part_b:
                outs[1][:, lanes] = to_send(info, top, bottom)

    def run(full):
        blocks = attention_blocks(full, cross, half)

        @pl.when(pl.program_id(0) == 0)
        def _():
            for s, keys, rows, cols in blocks:
                at = rows if full else slice(0, half)
                kinds = (0, 1) if full else (2 + s, 2 + s)
                bias_ref[rows, cols] = clip_bias(info, group, at, slice(0, half * len(keys)), *kinds)

        for pair_index, lanes in pairs_of(outs[0]):
            run_pair(full, blocks, pair_index, lanes)

    pl.when(info[FULL] != 0)(lambda: run(True))
    pl.when(info[FULL] == 0)(lambda: run(False))


def attend_back_kernel(group, counts, info, *refs):
    cross = group in (CROSS_A, CROSS_B)
    part_b = group in (SELF_B, CROSS_B)
    operands, at = [], 0
    for n in counts:
        operands.append(refs[at : at + n])
        at += n
    p_ref, outs = refs[at], refs[at + 1 :]
    half = operands[0][0].shape[0]
    out_ref = outs[2] if cross else outs[0]

    def run_pair(full, blocks, pair_index, lanes):
        q, k, v, g = (load_halves(info, refs, len(refs) == 3, lanes) for refs in operands)
        queries, sums = [], {}
        head_rows = lax.broadcasted_iota(jnp.int32, (2 * HEAD_DIM, 1), 0) < HEAD_DIM
        for s, keys, rows, cols in blocks:
            query = query_half(info, q, s)
            grad = query_half(info, g, s)
            key = jnp.concatenate([k[t] for t in keys], axis=0)
            value = jnp.concatenate([v[t] for t in keys], axis=0)
            dq, dk, dv = [], [], []
            for h in range(2):
                own = jnp.where(head_lanes(h), grad, jnp.zeros_like(grad))
                probs = p_ref[2 * pair_index + h, rows, cols]
                wide_probs = probs.astype(F32)
                grad_probs = dot_nt(own, value)
                delta = jnp.sum(wide_probs * grad_probs, axis=-1, keepdims=True)
                grad_scores = (wide_probs * (grad_probs - delta)).astype(BF16)
                dq.append(dot_nn(grad_scores, key))
                dk.append(dot_tn(query, grad_scores))
                dv.append(dot_tn(grad, probs))
            queries.append((jnp.where(head_lanes(0), dq[0], dq[1]) * SCORE_SCALE).astype(BF16))
            both = tuple(jnp.concatenate([p[0][:HEAD_DIM], p[1][HEAD_DIM:]], axis=0).T for p in (dk, dv))
            sums[keys] = (sums[keys][0] + both[0], sums[keys][1] + both[1]) if keys in sums else both
        grads = []
        for t in range(2):
            dk, dv = (sums[(0, 1)] if full else sums[(t,)])
            rows = slice(t * half, (t + 1) * half) if full else slice(0, half)
            grads.append(((dk[rows] * SCORE_SCALE).astype(BF16), dv[rows].astype(BF16)))
        top, bottom = queries[0], queries[-1]
        if full and not cross:
            top, bottom = top[:half], top[half:]
        if cross:
            outs[0][:, lanes] = top
            outs[1][:, lanes] = bottom
        parts = [(g0, g1) for g0, g1 in zip(*grads)]
        if not cross:
            parts = [(top, bottom)] + parts
        for n, (first, second) in enumerate(parts):
            out_ref[n, :half, lanes] = first
            out_ref[n, half:, lanes] = second
            if part_b:
                outs[3 if cross else 1][n, :, lanes] = to_send(info, first, second)

    def run(full):
        blocks = attention_blocks(full, cross, half)
        for pair_index, lanes in pairs_of(out_ref):
            run_pair(full, blocks, pair_index, lanes)

    pl.when(info[FULL] != 0)(lambda: run(True))
    pl.when(info[FULL] == 0)(lambda: run(False))


def column_block(array, lead=None, row=0, column=0, rows=256):
    lanes = PAIRS * 2 * HEAD_DIM
    if array.ndim == 3:
        return (array, pl.BlockSpec((None, rows, lanes), lambda j, info: (lead, row, j + column)))
    return (array, pl.BlockSpec((rows, lanes), lambda j, info: (row, j + column)))


def halves_of(array, lead=None):
    return [column_block(array, lead, 0), column_block(array, lead, 1)]


def attend(info, group, operands, columns, rows=256):
    cross = group in (CROSS_A, CROSS_B)
    lanes = PAIRS * 2 * HEAD_DIM
    heads = columns // HEAD_DIM
    p_rows = rows if cross else 2 * rows
    half_out = ((rows, columns), BF16, pl.BlockSpec((rows, lanes), lambda j, info: (0, j)))
    mix_out = ((2 * rows, columns), BF16, pl.BlockSpec((2 * rows, lanes), lambda j, info: (0, j)))
    outs = [half_out, half_out] if cross else [mix_out] + ([half_out] if group == SELF_B else [])
    p_block = pl.BlockSpec((2 * PAIRS, p_rows, 2 * rows), lambda j, info: (j, 0, 0))
    p_out = ((heads, p_rows, 2 * rows), BF16, p_block, True)
    return call(
        functools.partial(attend_kernel, group, [len(o) for o in operands]),
        info,
        heads // (2 * PAIRS),
        sum(operands, []),
        outs + [p_out],
        [pltpu.VMEM((p_rows, 2 * rows), F32)],
        "attend",
        20,
        heads * 2 // 3,
    )


def attend_back(info, group, operands, probs, columns, rows=256):
    cross = group in (CROSS_A, CROSS_B)
    part_b = group in (SELF_B, CROSS_B)
    lanes = PAIRS * 2 * HEAD_DIM
    half_out = ((rows, columns), BF16, pl.BlockSpec((rows, lanes), lambda j, info: (0, j)))
    count = 2 if cross else 3

    def stacked(height):
        return ((count, height, columns), BF16, pl.BlockSpec((count, height, lanes), lambda j, info: (0, 0, j)))

    outs = [half_out, half_out] if cross else []
    outs = outs + [stacked(2 * rows)] + ([stacked(rows)] if part_b else [])
    p_block = pl.BlockSpec((2 * PAIRS,) + probs.shape[1:], lambda j, info: (j, 0, 0))
    return call(
        functools.partial(attend_back_kernel, group, [len(o) for o in operands]),
        info,
        probs.shape[0] // (2 * PAIRS),
        sum(operands, []) + [(probs, p_block)],
        outs,
        [],
        "attend_back",
        20,
        probs.shape[0],
    )


def first_project_kernel(info, a_ref, kept_ref, received_ref, norms_ref, w_ref, rows_ref, normed_ref, out_ref):
    @pl.when(pl.program_id(0) == 0)
    def _():
        rows = joined_rows(info, a_ref, kept_ref, received_ref)
        rows_ref[...] = rows
        normal, _ = norm_stats(rows.astype(F32))
        normed_ref[...] = (normal * norms_ref[0:1, :] + norms_ref[1:2, :]).astype(BF16)

    out_ref[...] = dot_nn(normed_ref[...], w_ref[...]).astype(BF16)


def first_project(info, tokens, received, norms, w_self):
    count, width, cols = w_self.shape
    rows = tokens.shape[1] + received.shape[0]
    return call(
        first_project_kernel,
        info,
        count,
        part_rows(tokens) + [whole_in(received), whole_in(norms), (w_self, lead_spec(width, cols))],
        [whole_out(rows, width, in_hbm=True), whole_out(rows, width, in_hbm=True)]
        + [((count, rows, cols), BF16, lead_spec(rows, cols))],
        [],
        "first_project",
        12,
        4,
    )


def other_project_kernel(info, normed_ref, own_b_ref, mine_ref, theirs_ref, out_ref, send_ref):
    weights = joined_pieces(info, mine_ref[...], theirs_ref[...], 0)
    out = dot_nn(normed_ref[...], weights).astype(BF16)
    out_ref[...] = out
    part_b = out.shape[0] - own_b_ref.shape[0]
    send_ref[...] = to_send(info, own_b_ref[...], out[part_b:])


def other_project(info, normed, qkv_own, mine, theirs, part_b):
    count, half, cols = mine.shape
    rows = normed.shape[0]
    own_b = pl.BlockSpec((None, part_b, cols), lambda j, info: (j, rows // part_b - 1, 0))
    return call(
        other_project_kernel,
        info,
        count,
        [whole_in(normed), (qkv_own, own_b), (mine, lead_spec(half, cols)), (theirs, lead_spec(half, cols))],
        [
            ((count, rows, cols), BF16, lead_spec(rows, cols)),
            ((count, part_b, cols), BF16, lead_spec(part_b, cols)),
        ],
        [],
        "other_project",
        9,
        3,
    )


def put_query_parts(info, value, far_ref, near_ref, left_ref, right_ref, send_ref):
    rows = left_ref.shape[0]
    cols = left_ref.shape[1]
    for h in range(2):
        at = slice(h * cols, (h + 1) * cols)
        far_ref[:, at] = value[h][:rows]
        near_ref[:, at] = value[h][rows : 2 * rows]
    left, right = value[0][2 * rows :], value[1][2 * rows :]
    left_ref[...] = left
    right_ref[...] = right
    send_ref[...] = to_send(info, left, right)


def query_outs(rows, width):
    whole, half = whole_out(rows, width, in_hbm=True), whole_out(rows, width // 2, in_hbm=True)
    return [whole, whole, half, half, half]


def self_mixes(info, mix0_ref, mix1_ref, slots_ref, received_ref):
    rows = received_ref.shape[0]
    parts = exchanged(info, TOP_BIG, slots_ref[:rows, :], slots_ref[rows:, :], received_ref[...])
    return [
        jnp.concatenate([ref[...], part], axis=0) for ref, part in zip((mix0_ref, mix1_ref), parts)
    ]


def second_project_kernel(
    info, rows_ref, norms_ref, mix0_ref, mix1_ref, slots_ref, received_ref, out_ref, query_ref, mine_ref, theirs_ref,
    hidden_ref, joined_ref, *query_refs,
):
    mixes = self_mixes(info, mix0_ref, mix1_ref, slots_ref, received_ref)
    other_out = joined_pieces(info, mine_ref[0], theirs_ref[0], 1)
    hidden = rows_ref[...].astype(F32) + dot_nn(mixes[0], out_ref[...]) + dot_nn(mixes[1], other_out)
    hidden_ref[...] = hidden
    normal, _ = norm_stats(hidden)
    joined = (normal * norms_ref[2:3, :] + norms_ref[3:4, :]).astype(BF16)
    joined_ref[...] = joined
    other_query = joined_pieces(info, mine_ref[1], theirs_ref[1], 0)
    queries = [dot_nn(joined, w).astype(BF16) for w in (query_ref[...], other_query)]
    put_query_parts(info, queries, *query_refs)


def second_project(info, rows, norms, mixes, w_self_out, w_query, mine, theirs, part_b):
    shape = rows.shape
    return call(
        second_project_kernel,
        info,
        1,
        [whole_in(a) for a in (rows, norms, *mixes, w_self_out, w_query, mine, theirs)],
        [whole_out(*shape, kind=F32, in_hbm=True), whole_out(*shape, in_hbm=True)] + query_outs(part_b, shape[1]),
        [],
        "second_project",
        17,
        5,
    )


def offer_project_kernel(info, rows_ref, own_ref, mine_ref, theirs_ref, out_ref, send_ref):
    cols = own_ref.shape[1]
    rows = send_ref.shape[0]
    other = joined_pieces(info, mine_ref[...], theirs_ref[...], 0)
    parts = [dot_nn(rows_ref[...], w).astype(BF16) for w in (own_ref[...], other)]
    for h in range(2):
        out_ref[:, h * cols : (h + 1) * cols] = parts[h]
    send_ref[...] = to_send(info, parts[0][-rows:], parts[1][-rows:])


def offer_project(info, joined, w_offer, mine, theirs, part_b):
    count, width, cols = w_offer.shape
    rows = joined.shape[0]
    piece = lead_spec(cols, cols)
    return call(
        offer_project_kernel,
        info,
        count,
        [whole_in(joined), (w_offer, lead_spec(width, cols)), (mine, piece), (theirs, piece)],
        [
            ((count, rows, 2 * cols), BF16, lead_spec(rows, 2 * cols)),
            ((count, part_b, cols), BF16, lead_spec(part_b, cols)),
        ],
        [],
        "offer_project",
        9,
        4,
    )


def reader_rows(info, far_ref, near_ref, far_b_ref, near_b_ref, received_ref):
    half = far_b_ref.shape[1]
    parts = exchanged(info, TOP_MID, far_b_ref[...], near_b_ref[...], received_ref[...])
    return [
        jnp.concatenate([ref[:, h * half : (h + 1) * half] for ref in (far_ref, near_ref)] + [parts[h]], axis=0)
        for h in range(2)
    ]


def mlp_kernel(
    info, hidden_ref, norms_ref, far_ref, near_ref, far_b_ref, near_b_ref, received_ref, w_cross_ref, mine_ref,
    theirs_ref, grad_a_ref, grad_kept_ref, grad_received_ref, up_ref, down_ref, result_ref, grad_second_ref, gm_far_ref, gm_near_ref, gm_left_ref, gm_right_ref,
    gm_send_ref, activated_ref, grad_up_ref, rows_ref, grad_ref, keep_ref, send_ref, g_norms_ref, second_ref,
    sum_ref, back_ref,
):
    step = pl.program_id(0)

    def mixes():
        return reader_rows(info, far_ref, near_ref, far_b_ref, near_b_ref, received_ref)

    def cross_weights():
        return w_cross_ref[...], joined_pieces(info, mine_ref[...], theirs_ref[...], 1)

    @pl.when(step == 0)
    def _():
        grad_ref[...] = joined_rows(info, grad_a_ref, grad_kept_ref, grad_received_ref)
        second = hidden_ref[...]
        for mix, weight in zip(mixes(), cross_weights()):
            second = second + dot_nn(mix, weight)
        second_ref[...] = second
        normal, _ = norm_stats(second)
        rows_ref[...] = (normal * norms_ref[4:5, :] + norms_ref[5:6, :]).astype(BF16)
        sum_ref[...] = second
        back_ref[...] = jnp.zeros_like(back_ref)

    rows, grad, up, down = rows_ref[...], grad_ref[...], up_ref[...], down_ref[...]
    pre = dot_nn(rows, up)
    spread = lax.erf(pre * 0.7071067811865476) * 0.5 + 0.5
    slope = spread + pre * (jnp.exp(pre * pre * -0.5) * 0.3989422804014327)
    activated = (pre * spread).astype(BF16)
    grad_up = (dot_nt(grad, down) * slope).astype(BF16)
    sum_ref[...] += dot_nn(activated, down)
    back_ref[...] += dot_nt(grad_up, up)
    activated_ref[...] = activated
    grad_up_ref[...] = grad_up

    @pl.when(step == 3)
    def _():
        result_ref[...] = sum_ref[...].astype(BF16)
        normal, inverse = norm_stats(second_ref[...])
        back, gain, shift = norm_back(back_ref[...], normal, inverse, norms_ref[4:5, :])
        g_norms_ref[0:1, :] = gain
        g_norms_ref[1:2, :] = shift
        grad_second = grad_ref[...].astype(F32) + back
        grad_second_ref[...] = grad_second
        rounded = grad_second.astype(BF16)
        parts = []
        for h, (mix, weight) in enumerate(zip(mixes(), cross_weights())):
            parts.append(dot_nt(rounded, weight).astype(BF16))
            put_pieces(info, keep_ref, send_ref, h, dot_tn(mix, rounded), 1)
        put_query_parts(info, parts, gm_far_ref, gm_near_ref, gm_left_ref, gm_right_ref, gm_send_ref)


def mlp(info, hidden, norms, mixes, w_cross, mine, theirs, cotangent, received, up, down):
    rows, width = hidden.shape
    half = width // 2
    part_b = received.shape[0]

    pieces = (up.shape[:1] + (rows, width), BF16, lead_spec(rows, width), True)
    wide = pltpu.VMEM((rows, width), F32)
    return call(
        mlp_kernel,
        info,
        4,
        [whole_in(from_hbm(a)) for a in (hidden, norms, *mixes, w_cross, mine, theirs)]
        + part_rows(cotangent)
        + [whole_in(from_hbm(received)), (up, lead_spec(width, width)), (down, lead_spec(width, width))],
        [whole_out(rows, width), whole_out(rows, width, kind=F32, in_hbm=True)]
        + query_outs(part_b, width)
        + [pieces, pieces, whole_out(rows, width), whole_out(rows, width)]
        + [whole_out(2, half, half), whole_out(2, half, half)]
        + [whole_out(2, width, kind=F32)],
        [wide, wide, wide],
        "mlp",
        46,
        34,
    )


def mlp_weights_kernel(info, rows_ref, grad_ref, activated_ref, grad_up_ref, *outs):
    g_up = dot_tn(rows_ref[...], grad_up_ref[...]).astype(BF16)
    g_down = dot_tn(activated_ref[...], grad_ref[...]).astype(BF16)
    first = pl.program_id(0) < 2
    for keep_ref, send_ref, value in ((outs[0], outs[1], g_up), (outs[2], outs[3], g_down)):

        @pl.when(first)
        def _(keep_ref=keep_ref, value=value):
            keep_ref[...] = value

        @pl.when(jnp.logical_not(first))
        def _(send_ref=send_ref, value=value):
            send_ref[...] = value


def mlp_weights(info, rows, grad, activated, grad_up):
    count, height, width = activated.shape

    def pieces(index):
        return ((2, width, width), BF16, pl.BlockSpec((None, width, width), lambda j, info: (index(j), 0, 0)))

    keep, send = pieces(lambda j: jnp.minimum(j, 1)), pieces(lambda j: jnp.maximum(j - 2, 0))
    piece = lead_spec(height, width)
    return call(
        mlp_weights_kernel,
        info,
        count,
        [whole_in(from_hbm(rows)), whole_in(from_hbm(grad)), (from_hbm(activated), piece), (from_hbm(grad_up), piece)],
        [keep, send, keep, send],
        [],
        "mlp_weights",
        24,
        10,
    )


def second_back_kernel(
    info, far_ref, near_ref, far_b_ref, near_b_ref, received_ref, dkv_ref, slots_ref, slots_received_ref, joined_ref,
    hidden_ref, grad_second_ref, norms_ref, offer_ref, offer_mine_ref, offer_theirs_ref, query_ref, out_ref, mine_ref,
    theirs_ref, mix0_ref, mix1_ref, mix_slots_ref, mix_received_ref, cross_keep_ref, cross_send_ref, grad_hidden_ref,
    grad_mix_ref, mix_send_ref, keep_ref, send_ref, g_norms_ref, back_ref,
):
    step = pl.program_id(0)
    half = query_ref.shape[1]
    rows = received_ref.shape[0]

    def add(at, grads, weights, first):
        joined = joined_ref[...]
        total = dot_nt(grads[0], weights[0]) + dot_nt(grads[1], weights[1])
        back_ref[...] = total if first else back_ref[...] + total
        for h in range(2):
            put_pieces(info, keep_ref, send_ref, (h, at), dot_tn(joined, grads[h]), 0)

    def add_offer(at):
        parts = exchanged(info, TOP_BIG, slots_ref[:rows, :], slots_ref[rows:, :], slots_received_ref[...])
        grads = [
            jnp.concatenate([dkv_ref[:, h * half : (h + 1) * half], parts[h]], axis=0) for h in range(2)
        ]
        other = joined_pieces(info, offer_mine_ref[...], offer_theirs_ref[...], 0)
        add(at, grads, (offer_ref[...], other), at == 0)

    pl.when(step == 0)(lambda: add_offer(0))
    pl.when(step == 1)(lambda: add_offer(1))

    @pl.when(step == 2)
    def _():
        for h in range(2):
            keep_ref[h, 4] = cross_keep_ref[h]
            send_ref[h, 4] = cross_send_ref[h]
        grads = reader_rows(info, far_ref, near_ref, far_b_ref, near_b_ref, received_ref)
        add(3, grads, (query_ref[...], joined_pieces(info, mine_ref[1], theirs_ref[1], 0)), False)
        normal, inverse = norm_stats(hidden_ref[...])
        back, gain, shift = norm_back(back_ref[...], normal, inverse, norms_ref[2:3, :])
        g_norms_ref[0:1, :] = gain
        g_norms_ref[1:2, :] = shift
        grad_hidden = grad_second_ref[...] + back
        grad_hidden_ref[...] = grad_hidden
        rounded = grad_hidden.astype(BF16)
        mixes = self_mixes(info, mix0_ref, mix1_ref, mix_slots_ref, mix_received_ref)
        parts = []
        for h, weight in enumerate((out_ref[...], joined_pieces(info, mine_ref[0], theirs_ref[0], 1))):
            part = dot_nt(rounded, weight).astype(BF16)
            grad_mix_ref[h] = part
            parts.append(part[-rows:])
            put_pieces(info, keep_ref, send_ref, (h, 2), dot_tn(mixes[h], rounded), 1)
        mix_send_ref[...] = to_send(info, *parts)


def second_back(
    info, grad_q, dkv, slots, slots_received, joined, hidden, grad_second, norms, w_offer, offer_mine, offer_theirs,
    w_query, w_self_out, mine, theirs, mixes, cross_keep, cross_send,
):
    rows, width = hidden.shape
    half = width // 2
    part_b = slots_received.shape[1]

    def offered(array, *shape):
        return (array, pl.BlockSpec((None,) + shape, lambda j, info: (jnp.minimum(j, 1), 0, 0)))

    return call(
        second_back_kernel,
        info,
        3,
        [whole_in(from_hbm(a)) for a in grad_q]
        + [offered(dkv, *dkv.shape[1:]), offered(slots, *slots.shape[1:])]
        + [offered(slots_received, *slots_received.shape[1:])]
        + [whole_in(a) for a in (joined, hidden, grad_second, norms)]
        + [offered(w_offer, width, half), offered(offer_mine, half, half), offered(offer_theirs, half, half)]
        + [whole_in(a) for a in (w_query, w_self_out, mine, theirs, *mixes, cross_keep, cross_send)],
        [whole_out(rows, width, kind=F32, in_hbm=True), whole_out(2, rows, half), whole_out(part_b, half)]
        + [whole_out(2, 5, half, half), whole_out(2, 5, half, half), whole_out(2, width, kind=F32)],
        [pltpu.VMEM((rows, width), F32)],
        "second_back",
        35,
        12,
    )


def first_grads(info, own_ref, other_ref, slots_ref, received_ref):
    rows = received_ref.shape[0]
    parts = exchanged(info, TOP_BIG, slots_ref[:rows, :], slots_ref[rows:, :], received_ref[...])
    return [jnp.concatenate([ref[...], part], axis=0) for ref, part in zip((own_ref, other_ref), parts)]


def first_weights_kernel(half, info, grad_ref, slots_ref, received_ref, normed_ref, keep_ref, send_ref):
    rows = received_ref.shape[0]
    parts = exchanged(info, TOP_BIG, slots_ref[:rows, :], slots_ref[rows:, :], received_ref[...])
    value = dot_tn(normed_ref[...], jnp.concatenate([grad_ref[...], parts[half]], axis=0))
    put_pieces(info, keep_ref, send_ref, slice(None), value, 0)


def first_ins(*arrays):
    return [(a, lead_spec(*a.shape[1:])) for a in arrays]


def first_weights(info, half_index, grads, slots, received, normed):
    half = grads.shape[2]
    piece = ((3, half, half), BF16, lead_spec(half, half))
    return call(
        functools.partial(first_weights_kernel, half_index),
        info,
        3,
        first_ins(grads, slots, received) + [whole_in(normed)],
        [piece, piece],
        [],
        "first_weights",
        12,
        3,
    )


def first_back_kernel(
    info, own_ref, other_ref, slots_ref, received_ref, rows_ref, grad_hidden_ref, norms_ref, w_own_ref, mine_ref,
    theirs_ref, grad_early_ref, grad_late_ref, g_norms_ref, back_ref,
):
    step = pl.program_id(0)
    grads = first_grads(info, own_ref, other_ref, slots_ref, received_ref)
    other = joined_pieces(info, mine_ref[...], theirs_ref[...], 0)
    total = dot_nt(grads[0], w_own_ref[...]) + dot_nt(grads[1], other)

    @pl.when(step == 0)
    def _():
        back_ref[...] = total

    @pl.when(step > 0)
    def _():
        back_ref[...] += total

    @pl.when(step == pl.num_programs(0) - 1)
    def _():
        normal, inverse = norm_stats(rows_ref[...].astype(F32))
        back, gain, shift = norm_back(back_ref[...], normal, inverse, norms_ref[0:1, :])
        g_norms_ref[0:1, :] = gain
        g_norms_ref[1:2, :] = shift
        grad_rows = (grad_hidden_ref[...] + back).astype(BF16)
        late = grad_late_ref.shape[0]
        grad_late_ref[...] = grad_rows[:late]
        grad_early_ref[...] = grad_rows[late:]


def first_back(info, own, other, slots, received, rows, grad_hidden, norms, w_self, mine, theirs):
    count = own.shape[0]
    width = rows.shape[1]
    late = received.shape[1]
    ins = first_ins(own, other, slots, received)
    ins += [whole_in(a) for a in (rows, grad_hidden, norms)]
    ins += [(a, lead_spec(*a.shape[1:])) for a in (w_self, mine, theirs)]
    return call(
        first_back_kernel,
        info,
        count,
        ins,
        [whole_out(2 * late, width), whole_out(late, width), whole_out(2, width, kind=F32)],
        [pltpu.VMEM(rows.shape, F32)],
        "first_back",
        24,
        8,
    )


def row_of(table, index):
    return lax.dynamic_index_in_dim(table, index, 0, keepdims=False)


def scalars(clip_len, index, across, quarter):
    core = index % 2
    is_big = index < 2 * quarter
    is_mid = jnp.logical_and(index >= 2 * quarter, index < 3 * quarter)
    first, last = core == 0, core == 1
    flags = [
        is_big,
        core,
        across,
        jnp.logical_and(is_big, index >= quarter),
        jnp.logical_and(is_big, last),
        jnp.logical_and(is_big, first),
        jnp.logical_and(is_mid, last),
        jnp.logical_and(is_mid, first),
    ]
    shared = index - core + across
    lens_a, lens_b = row_of(clip_len, across), clip_len[2]
    big_a = row_of(lens_a, jnp.minimum(index, 2 * quarter - 1))
    big_b = row_of(lens_b, jnp.minimum(shared, 2 * quarter - 1))
    sets_a = [row_of(lens_a, index % quarter + s * quarter) for s in range(2)]
    sets_b = [row_of(lens_b, shared % quarter + core * quarter)] * 2
    table = jnp.stack(
        [2 * big_a, 2 * big_a, *sets_a, 2 * big_b, 2 * big_b, *sets_b]
        + [big_a, 2 * big_a, *sets_a, big_b, 2 * big_b, *sets_b]
    )
    ends = [table[:, 0]]
    for k in range(1, 4):
        ends.append(ends[-1] + table[:, k])
    flags = jnp.stack([flag.astype(jnp.int32) for flag in flags])
    return jnp.concatenate([flags, jnp.stack(ends, axis=1).reshape(-1)])


def local(
    tokens,
    cotangent,
    clip_len,
    ln_params,
    w_self,
    w_self_out,
    w_offer,
    w_query,
    w_cross_out,
    w_up,
    w_down,
):
    index = lax.axis_index("clip")
    across = lax.axis_index("head")
    count = lax.axis_size("clip")
    quarter = count // 4
    levels = (2 * quarter).bit_length() - 1
    core = index % 2
    is_big = index < 2 * quarter
    is_mid = jnp.logical_and(index >= 2 * quarter, index < 3 * quarter)
    own_micro2 = core == across
    norms = ln_params[0]
    w_self, w_self_out, w_offer, w_query = w_self[0], w_self_out[0], w_offer[0], w_query[0]
    w_cross_out, w_up, w_down = w_cross_out[0], w_up[0], w_down[0]
    half = w_query.shape[1]
    part_a = tokens.shape[1]
    part_b = part_a // 2
    wide = 2 * half

    near = [(i, i - quarter) for i in range(2 * quarter, count)]
    far = [(i, i - 2 * quarter) for i in range(2 * quarter, 3 * quarter)]
    far += [(i, i - quarter) for i in range(3 * quarter, count)]

    def to_server(far_rows, near_rows):
        second = lax.ppermute(near_rows, "clip", near)
        return lax.ppermute(far_rows, "clip", far), second

    def to_reader(far_rows, near_rows):
        second = lax.ppermute(near_rows, "clip", [(b, a) for a, b in near])
        return lax.ppermute(far_rows, "clip", [(b, a) for a, b in far]), second

    def reader_slots(left, right, received):
        top = jnp.where(jnp.logical_and(is_mid, core == 1), received, left)
        return top, jnp.where(jnp.logical_and(is_mid, core == 0), received, right)

    def from_server(top, bottom):
        return top, bottom, other_core(jnp.where(core == 0, bottom, top))

    def over_level(part, bit):
        return over_bit(part, bit, 2 * quarter if bit == levels - 1 else None)

    def add(left, right):
        return (left.astype(F32) + right.astype(F32)).astype(BF16)

    def last_levels(total, received):
        total = total if received is None else add(total, received)
        for bit in range(3, levels):
            total = add(total, over_level(total, bit))
        return total

    def whole(mine, axis):
        return in_core_order(core, mine, other_core(mine), axis).astype(F32)[None]

    def all_rows(a_mine, b_mine, a_theirs, b_theirs):
        kept = jnp.where(own_micro2, b_mine, b_theirs)
        received = other_core(jnp.where(own_micro2, b_theirs, b_mine))
        micro2 = in_core_order(core, kept, received, 0)
        micro0 = jnp.where(across == 0, a_mine, a_theirs)
        micro1 = jnp.where(across == 0, a_theirs, a_mine)
        return jnp.stack([micro0, micro1, micro2])


    def over_head_rows(array, start, stop, *others):
        return over_head(after(array[start:stop], *others) if others else array[start:stop])

    def rows_piece(array, piece):
        return lax.dynamic_slice(array, (2, piece * part_b, 0), (1, part_b, wide))[0]

    self_mine = over_head(core_piece(w_self, core, 1))
    tokens_received = other_core(rows_piece(tokens, 1 - core))
    info = scalars(clip_len, index, across, quarter)
    rows, normed, qkv_own = first_project(info, tokens, tokens_received, norms, w_self)
    self_0 = [halves_of(qkv_own, n) for n in range(3)]
    mix_0, p_0 = attend(info, SELF_A, self_0, half)
    first_piece = jnp.stack([core_piece(w_self_out, core, 1), core_piece(w_query, core, 0)])
    offer_piece, up_piece, down_piece = core_piece(w_offer, core, 1), core_piece(w_up, core, 1), core_piece(w_down, core, 0)
    cross_piece = core_piece(w_cross_out, core, 1)
    (self_mine, mix_0, first_piece) = fence(self_mine, mix_0, first_piece)

    first_mine = over_head(first_piece)
    self_theirs = other_core(self_mine)
    qkv_other, qkv_send = other_project(info, normed, qkv_own, self_mine, self_theirs, part_b)
    self_1 = [halves_of(qkv_other, n) for n in range(3)]
    mix_1, p_1 = attend(info, SELF_A, self_1, half)
    qkv_received, first_mine, mix_1, offer_piece = fence(other_core(qkv_send), first_mine, mix_1, offer_piece)

    offer_mine = over_head(offer_piece[0])
    self_b = [
        [column_block(qkv_own, n, 2), column_block(qkv_other, n, 2), column_block(qkv_received, n)] for n in range(3)
    ]
    mix_s, mix_send, p_s = attend(info, SELF_B, self_b, half)
    first_theirs = other_core(first_mine)
    mix_s, mix_send, offer_mine, offer_piece = fence(mix_s, mix_send, offer_mine, offer_piece)

    offer_last = over_head(offer_piece[1])
    mixes = (mix_0, mix_1, mix_s, other_core(mix_send))
    hidden, joined, q_far, q_near, q_left, q_right, q_send = second_project(
        info, rows, norms, mixes, w_self_out, w_query, first_mine, first_theirs, part_b
    )
    q_far, q_near, q_left, q_right, q_send, joined, offer_mine, offer_last, cross_piece, up_piece, down_piece, cotangent = fence(
        q_far, q_near, q_left, q_right, q_send, joined, offer_mine, offer_last, cross_piece, up_piece, down_piece, cotangent
    )

    asked_a = to_server(q_far, q_near)
    up_mine = [over_head(up_piece[:576])]
    q_top, q_bottom = reader_slots(q_left, q_right, other_core(q_send))
    offer_mine = jnp.stack([offer_mine, offer_last])
    offer_theirs = other_core(offer_mine)
    offer, offer_send = offer_project(info, joined, w_offer, offer_mine, offer_theirs, part_b)
    cotangent_received = other_core(rows_piece(cotangent, 1 - core))
    offer_received = other_core(offer_send)
    *asked_a, q_top, q_bottom, offer, offer_received, cotangent_received, up_mine[0], up_piece, cross_piece = fence(
        *asked_a, q_top, q_bottom, offer, offer_received, cotangent_received, up_mine[0], up_piece, cross_piece
    )

    asked_b = to_server(q_top, q_bottom)
    up_mine.append(over_head(up_piece[576:]))
    cross_mine = over_head(cross_piece)
    cross_a = [[column_block(asked_a[0]), column_block(asked_a[1])]] + [halves_of(offer, n) for n in range(2)]
    far_a, near_a, cross_p_a = attend(info, CROSS_A, cross_a, wide)
    far_a, near_a, asked_b_far, asked_b_near, up_mine[1], cross_mine, down_piece = fence(
        far_a, near_a, *asked_b, up_mine[1], cross_mine, down_piece
    )

    back_a = to_reader(far_a, near_a)
    down_mine = [over_head(down_piece[:576])]
    cross_b = [[column_block(asked_b_far), column_block(asked_b_near)]] + [
        [
            column_block(offer, n, 2),
            column_block(offer, n, 2, half // (PAIRS * 2 * HEAD_DIM)),
            column_block(offer_received, n),
        ]
        for n in range(2)
    ]
    far_b, near_b, cross_p_b = attend(info, CROSS_B, cross_b, half)
    up_mine = jnp.concatenate(up_mine)
    up_theirs = other_core(up_mine)
    cross_theirs = other_core(cross_mine)
    *back_a, far_b, near_b, up_mine, up_theirs, cross_theirs, down_mine[0], down_piece = fence(
        *back_a, far_b, near_b, up_mine, up_theirs, cross_theirs, down_mine[0], down_piece
    )

    back_b = to_reader(far_b, near_b)
    down_mine = jnp.concatenate([down_mine[0], over_head(down_piece[576:])])
    up_pieces = jnp.stack([core_piece(w_up, core, 1), up_mine, core_piece(w_up, 1 - core, 1), up_theirs])
    *back_b, down_mine, up_pieces = fence(*back_b, down_mine, up_pieces)

    back_b = from_server(*back_b)
    down_theirs = other_core(down_mine)
    down_pieces = jnp.stack([core_piece(w_down, core, 0), down_mine, core_piece(w_down, 1 - core, 0), down_theirs])
    (
        result, grad_second, gm_far, gm_near, gm_left, gm_right, gm_send,
        activated, grad_up, mlp_rows, grad_out, cross_keep, cross_send, norms_3,
    ) = mlp(
        info, hidden, norms, (*back_a, *back_b), w_cross_out, cross_mine, cross_theirs, cotangent, cotangent_received,
        up_pieces, down_pieces,
    )
    result, gm_far, gm_near, gm_left, gm_right, gm_send, activated, grad_up, mlp_rows, grad_out = fence(
        result, gm_far, gm_near, gm_left, gm_right, gm_send, activated, grad_up, mlp_rows, grad_out
    )

    grad_a = to_server(gm_far, gm_near)
    layer_x = [over_head(result[:448])]
    gm_top, gm_bottom = reader_slots(gm_left, gm_right, other_core(gm_send))
    up_keep, up_send, down_keep, down_send = mlp_weights(info, mlp_rows, grad_out, activated, grad_up)
    *grad_a, gm_top, gm_bottom, layer_x[0], result, down_keep, down_send, up_keep, up_send = fence(
        *grad_a, gm_top, gm_bottom, layer_x[0], result, down_keep, down_send, up_keep, up_send
    )

    grad_b = to_server(gm_top, gm_bottom)
    layer_x.append(over_head(result[448:]))
    down_received = other_core(down_send)
    down_out = [add(down_keep[1, :576], down_received[1, :576]), add(down_keep[1, 576:], down_received[1, 576:])]
    grad_in = [column_block(grad_a[0]), column_block(grad_a[1])]
    dq_far, dq_near, dkv_a = attend_back(info, CROSS_A, cross_a + [grad_in], cross_p_a, wide)
    dq_far, dq_near, grad_b_far, grad_b_near, layer_x[1], *down_out, up_keep, up_send = fence(
        dq_far, dq_near, *grad_b, layer_x[1], *down_out, up_keep, up_send
    )

    dq_a = to_reader(dq_far, dq_near)
    down_x = [over_head(down_out[0])]
    grad_in = [column_block(grad_b_far), column_block(grad_b_near)]
    dq_b_far, dq_b_near, dkv_b, dkv_send = attend_back(info, CROSS_B, cross_b + [grad_in], cross_p_b, half)
    up_received = other_core(up_send)
    up_out = [add(up_keep[1, :192], up_received[1, :192]), add(up_keep[1, 192:], up_received[1, 192:])]
    down_out[1] = jnp.concatenate([down_out[1], up_out[0]])
    *dq_a, dq_b_far, dq_b_near, dkv_send, down_x[0], up_out[1], down_out[1] = fence(
        *dq_a, dq_b_far, dq_b_near, dkv_send, down_x[0], up_out[1], down_out[1]
    )

    dq_b = to_reader(dq_b_far, dq_b_near)
    both_x = over_head(down_out[1])
    down_own = add(down_keep[0, :576], down_received[0, :576])
    down_own = add(down_own, down_x[0])
    down_first, down_rest = down_own[:384], down_own[384:]
    down_y = [over_level(down_first, 1)]
    *dq_b, dkv_send, both_x, up_out[1], down_first, down_rest, down_y[0] = fence(
        *dq_b, dkv_send, both_x, up_out[1], down_first, down_rest, down_y[0]
    )

    dkv_received = other_core(dkv_send)
    down_x.append(both_x[:192])
    up_x = [both_x[192:], over_head(up_out[1])]
    down_second = add(add(down_keep[0, 576:], down_received[0, 576:]), down_x[1])
    down_second = jnp.concatenate([down_rest, down_second])
    down_y.append(over_level(down_second, 1))
    down_first = add(down_first, down_y[0])
    down_z = [over_level(down_first, 2)]
    grad_hidden, grad_mix, grad_send, mid_keep, mid_send, norms_2 = second_back(
        info, (*dq_a, *from_server(*dq_b)), dkv_a, dkv_b, dkv_received, joined, hidden, grad_second, norms, w_offer,
        offer_mine, offer_theirs, w_query, w_self_out, first_mine, first_theirs, mixes, cross_keep, cross_send,
    )
    up_own = add(up_keep[0], up_received[0])
    grad_hidden, grad_mix, grad_send, mid_keep, mid_send, up_x[1], up_own, down_second, down_y[1], down_first, down_z[0] = fence(
        grad_hidden, grad_mix, grad_send, mid_keep, mid_send, up_x[1], up_own, down_second, down_y[1], down_first, down_z[0]
    )

    (back_1,) = attend_back(info, SELF_A, self_1 + [halves_of(grad_mix, 1)], p_1, half)
    grad_received = other_core(grad_send)
    mid_received = other_core(mid_send)
    mid_out = [add(mid_keep[1, :3], mid_received[1, :3]), add(mid_keep[1, 3:], mid_received[1, 3:])]
    up_total = add(up_own, jnp.concatenate(up_x))
    up_y = [over_level(up_total[:384], 1)]
    down_second = add(down_second, down_y[1])
    down_z.append(over_level(down_second, 2))
    back_1, grad_mix, grad_received, mid_out[0], mid_out[1], up_total, up_y[0], down_second, down_z[1] = fence(
        back_1, grad_mix, grad_received, *mid_out, up_total, up_y[0], down_second, down_z[1]
    )

    mid_x = [over_head(mid_out[0])]
    up_y.append(over_level(up_total[384:], 1))
    up_first = add(up_total[:384], up_y[0])
    up_z = [over_level(up_first, 2)]
    grad_in = [column_block(grad_mix, 0, 2), column_block(grad_mix, 1, 2), column_block(grad_received)]
    back_s, back_send = attend_back(info, SELF_B, self_b + [grad_in], p_s, half)
    back_received = other_core(back_send)
    other_keep, other_send = first_weights(info, 1, back_1, back_s, back_received, normed)
    mid_own = add(mid_keep[0], mid_received[0])
    (
        back_s, back_received, other_keep, other_send, mid_x[0], mid_own, mid_out[1],
        up_total, up_y[1], up_first, up_z[0], grad_mix,
    ) = fence(
        back_s, back_received, other_keep, other_send, mid_x[0], mid_own, mid_out[1],
        up_total, up_y[1], up_first, up_z[0], grad_mix,
    )

    mid_x.append(over_head(mid_out[1]))
    mid_first = add(mid_own[:2], mid_x[0][:2])
    mid_y = [over_level(mid_first, 1)]
    up_second = add(up_total[384:], up_y[1])
    up_z.append(over_level(up_second, 2))
    (back_0,) = attend_back(info, SELF_A, self_0 + [halves_of(grad_mix, 0)], p_0, half)
    own_keep, own_send = first_weights(info, 0, back_0, back_s, back_received, normed)
    last_out = add(other_keep, other_core(other_send))
    down_total = jnp.concatenate([last_levels(down_first, down_z[0]), last_levels(down_second, down_z[1])])
    grad_down_weight = whole(down_total, 0)
    (
        back_0, own_keep, own_send, last_out, mid_x[1], mid_first, mid_y[0], up_second, up_z[1], mid_own,
        grad_down_weight,
    ) = fence(
        back_0, own_keep, own_send, last_out, mid_x[1], mid_first, mid_y[0], up_second, up_z[1], mid_own,
        grad_down_weight,
    )

    last_x = over_head(last_out)
    mid_second = add(mid_own[2:], jnp.concatenate([mid_x[0][2:], mid_x[1]]))
    mid_y.append(over_level(mid_second, 1))
    mid_first = add(mid_first, mid_y[0])
    mid_z = over_level(mid_first, 2)
    own_received = other_core(own_send)
    last_own = [add(own_keep[:2], own_received[:2]), add(own_keep[2:], own_received[2:])]
    grad_early, grad_late, norms_1 = first_back(
        info, back_0, back_1, back_s, back_received, rows, grad_hidden, norms, w_self, self_mine, self_theirs
    )
    up_total = jnp.concatenate([last_levels(up_first, up_z[0]), last_levels(up_second, up_z[1])])
    grad_up_weight = whole(up_total, 1)
    grad_early, grad_late, norms_1, last_own[0], last_own[1], last_x, mid_second, mid_y[1], mid_first, mid_z, grad_up_weight = fence(
        grad_early, grad_late, norms_1, *last_own, last_x, mid_second, mid_y[1], mid_first, mid_z, grad_up_weight
    )

    early_x = over_head(grad_early)
    first, second = add(last_own[0], last_x[:2]), add(last_own[1], last_x[2:])
    second = jnp.concatenate([second, add(mid_second[:1], mid_y[1][:1])])
    first_y, second_z = over_level(first, 1), over_level(second, 2)
    norm_grads = jnp.concatenate([norms_1, norms_2, norms_3], axis=0)
    norm_grads = norm_grads + other_core(norm_grads)
    norm_grads = norm_grads + over_level(norm_grads, 1)
    (
        early_x, grad_late, first, first_y, second, second_z, norm_grads, mid_first, mid_second
    ) = fence(
        early_x, grad_late, first, first_y, second, second_z, norm_grads, mid_first, mid_second
    )

    late_x = over_head(grad_late)
    first, second = add(first, first_y), add(second, second_z)
    first_z, second_y = over_level(first, 2), over_level(second[:1], 1)
    norm_grads = norm_grads + over_head(norm_grads)
    layer_x = after(jnp.concatenate(layer_x), first)
    layer_out = all_rows(result[:part_a], result[part_a:], layer_x[:part_a], layer_x[part_a:])
    mid_total = last_levels(mid_first, mid_z)
    out_total = last_levels(second[1:], None)
    rest_total = add(mid_second[1:], mid_y[1][1:])
    for bit in range(2, levels - 1):
        rest_total = add(rest_total, over_level(rest_total, bit))

    early = [layer_out, late_x, whole(out_total[0], 1), whole(mid_total, 1), whole(rest_total[0], 0)]
    early += [whole(rest_total[1], 1)]
    first, first_z, second, second_y, norm_grads, *early = fence(first, first_z, second, second_y, norm_grads, *early)
    layer_out, late_x, *grad_weights = early
    a_mine, a_theirs = (jnp.concatenate([x, y[:part_b]]) for x, y in ((grad_late, grad_early), (late_x, early_x)))
    grad_tokens = all_rows(a_mine, grad_early[part_b:], a_theirs, early_x[part_b:]).astype(F32)

    for bit in range(2, levels):
        norm_grads = norm_grads + over_level(norm_grads, bit)
    last_total = jnp.concatenate([last_levels(first, first_z), last_levels(second[:1], second_y)])
    return (layer_out, grad_tokens, norm_grads[None], whole(last_total, 1), *grad_weights, grad_up_weight, grad_down_weight)


def solution(mesh):
    return jax.shard_map(
        local,
        mesh=mesh,
        in_specs=(
            P(None, "clip", None),
            P(None, "clip", None),
            P(),
            P("clip", None, None),
            P("clip", None, None, "head"),
            P("clip", "head", None),
            P("clip", None, None, "head"),
            P("clip", None, "head"),
            P("clip", "head", None),
            P("clip", None, "head"),
            P("clip", "head", None),
        ),
        out_specs=(
            P(None, "clip", None),
            P(None, "clip", None),
            P("clip", None, None),
            P("clip", None, None, "head"),
            P("clip", "head", None),
            P("clip", None, None, "head"),
            P("clip", None, "head"),
            P("clip", "head", None),
            P("clip", None, "head"),
            P("clip", "head", None),
        ),
        check_vma=False,
    )
```

```python
import functools

import jax
import jax.numpy as jnp
from jax import lax
from jax.experimental import pallas as pl
from jax.experimental.pallas import tpu as pltpu
from jax.sharding import PartitionSpec as P


HEAD_DIM = 64
PAIRS = 3
EPSILON = 1e-06
SCORE_SCALE = 0.125
MASKED = -1e30
BF16 = jnp.bfloat16
F32 = jnp.float32
COST_BYTES = 1

FULL, CORE, ACROSS, SECOND_PLANE, TOP_BIG, BOTTOM_BIG, TOP_MID, BOTTOM_MID, ENDS = range(9)
SELF_A, SELF_B, CROSS_A, CROSS_B = range(4)


def over_head(value):
    return lax.ppermute(value, "head", [(0, 1), (1, 0)])


def over_bit(value, bit, count=None):
    count = lax.axis_size("clip") if count is None else count
    return lax.ppermute(value, "clip", [(i, i ^ (1 << bit)) for i in range(count)])


def other_core(value):
    return over_bit(value, 0)


def fence(*values):
    return lax.optimization_barrier(values)


def after(value, *others):
    return lax.optimization_barrier((value,) + others)[0]


def in_core_order(core, mine, theirs, axis):
    first = jnp.where(core == 0, mine, theirs)
    second = jnp.where(core == 0, theirs, mine)
    return jnp.concatenate([first, second], axis=axis)


def core_piece(value, piece, axis):
    size = value.shape[axis] // 2
    return lax.dynamic_slice_in_dim(value, piece * size, size, axis)


def dot_nt(left, right):
    return lax.dot_general(left, right, (((1,), (1,)), ((), ())), preferred_element_type=F32)


def dot_tn(left, right):
    return lax.dot_general(left, right, (((0,), (0,)), ((), ())), preferred_element_type=F32)


def dot_nn(left, right):
    return jnp.dot(left, right, preferred_element_type=F32)


def norm_stats(rows):
    mean = jnp.mean(rows, axis=-1, keepdims=True)
    centered = rows - mean
    variance = jnp.mean(centered * centered, axis=-1, keepdims=True)
    inverse = lax.rsqrt(variance + EPSILON)
    return centered * inverse, inverse


def norm_back(grad, normal, inverse, gain):
    scaled = grad * gain
    mean = jnp.mean(scaled, axis=-1, keepdims=True)
    along = jnp.mean(scaled * normal, axis=-1, keepdims=True)
    grad_rows = (scaled - mean - normal * along) * inverse
    gain_grad = jnp.sum(grad * normal, axis=0, keepdims=True)
    return grad_rows, gain_grad, jnp.sum(grad, axis=0, keepdims=True)


def pick(info, flag, yes, no):
    return jnp.where(info[flag] != 0, yes, no)


def core_order(info, mine, theirs):
    return pick(info, CORE, theirs, mine), pick(info, CORE, mine, theirs)


def joined_pieces(info, mine, theirs, axis):
    return jnp.concatenate(core_order(info, mine, theirs), axis=axis)


def exchanged(info, top_flag, first, second, received):
    return pick(info, top_flag, received, first), pick(info, top_flag + 1, received, second)


def to_send(info, first, second):
    return pick(info, CORE, first, second)


def put_pieces(info, keep_ref, send_ref, at, value, axis):
    size = value.shape[axis] // 2
    low, high = (value[:size], value[size:]) if axis == 0 else (value[:, :size], value[:, size:])
    mine, theirs = core_order(info, low.astype(BF16), high.astype(BF16))
    keep_ref[at] = mine
    send_ref[at] = theirs


def resident(shape, index=None):
    index = (lambda j, info: (0,) * len(shape)) if index is None else index
    return pl.BlockSpec(shape, index, pipeline_mode=pl.Buffered(1))


def whole_in(array):
    return (array, resident(array.shape))


def whole_out(*shape, kind=BF16, in_hbm=False):
    return (shape, kind, resident(shape), in_hbm)


def from_hbm(array):
    return pltpu.with_memory_space_constraint(array, pltpu.HBM)


def lead_spec(*shape):
    return pl.BlockSpec((None,) + shape, lambda j, info: (j,) + (0,) * len(shape))


def out_type(shape, kind, spec, in_hbm=False):
    return pltpu.HBM(shape, kind) if in_hbm else jax.ShapeDtypeStruct(shape, kind)


def call(kernel, info, steps, ins, outs, scratch, name, mebibytes, cost):
    return pl.pallas_call(
        kernel,
        grid_spec=pltpu.PrefetchScalarGridSpec(
            num_scalar_prefetch=1,
            grid=(steps,),
            in_specs=[spec for _, spec in ins],
            out_specs=[out[2] for out in outs],
            scratch_shapes=scratch,
        ),
        out_shape=[out_type(*out) for out in outs],
        compiler_params=pltpu.CompilerParams(vmem_limit_bytes=mebibytes * 1024 * 1024),
        cost_estimate=pl.CostEstimate(flops=0, bytes_accessed=cost * COST_BYTES, transcendentals=0),
        name=name,
    )(info, *[array for array, _ in ins])


def part_rows(array):
    _, count, width = array.shape
    return [
        (array, resident((None, count, width), lambda j, info: (info[ACROSS], 0, 0))),
        (array, resident((None, count // 2, width), lambda j, info: (2, info[CORE], 0))),
    ]


def joined_rows(info, a_ref, kept_ref, received_ref):
    own = info[CORE] == info[ACROSS]
    return jnp.concatenate([a_ref[...], jnp.where(own, kept_ref[...], received_ref[...])], axis=0)


def clip_bias(info, group, rows, cols, row_kind, col_kind):
    def clips(kind, places, shape, axis):
        base = ENDS + 16 * group + 4 * kind
        place = lax.broadcasted_iota(jnp.int32, shape, axis) + places.start
        return sum((place >= info[base + k]).astype(jnp.int32) for k in range(4))

    of_rows = clips(row_kind, rows, (rows.stop - rows.start, 128), 0)[:, :1]
    of_cols = clips(col_kind, cols, (8, cols.stop - cols.start), 1)[:1, :]
    return jnp.where(of_rows == of_cols, 0.0, MASKED)


def attention_blocks(full, cross, half):
    if full and cross:
        return [(None, (0, 1), slice(0, half), slice(0, 2 * half))]
    if full:
        return [(2, (0, 1), slice(0, 2 * half), slice(0, 2 * half))]
    if cross:
        return [(s, (s,), slice(0, half), slice(s * half, (s + 1) * half)) for s in range(2)]
    return [(s, (s,), slice(s * half, (s + 1) * half), slice(0, half)) for s in range(2)]


def load_halves(info, refs, exchange, lanes):
    first, second = refs[0][:, lanes], refs[1][:, lanes]
    if exchange:
        first, second = exchanged(info, TOP_BIG, first, second, refs[2][:, lanes])
    return first, second


def pairs_of(ref):
    size = 2 * HEAD_DIM
    return [(n, slice(n * size, (n + 1) * size)) for n in range(ref.shape[-1] // size)]


def query_half(info, halves, s):
    if s == 2:
        return jnp.concatenate(halves, axis=0)
    return pick(info, SECOND_PLANE, halves[1], halves[0]) if s is None else halves[s]


def head_lanes(h):
    first = lax.broadcasted_iota(jnp.int32, (1, 2 * HEAD_DIM), 1) < HEAD_DIM
    return first if h == 0 else jnp.logical_not(first)


def attend_kernel(group, counts, info, *refs):
    cross = group in (CROSS_A, CROSS_B)
    part_b = group in (SELF_B, CROSS_B)
    operands, at = [], 0
    for n in counts:
        operands.append(refs[at : at + n])
        at += n
    outs = refs[at:]
    bias_ref = outs[-1]
    p_ref = outs[-2]
    half = operands[0][0].shape[0]

    def run_pair(full, blocks, pair_index, lanes):
        q, k, v = (load_halves(info, refs, len(refs) == 3, lanes) for refs in operands)
        mixes = []
        for s, keys, rows, cols in blocks:
            query = query_half(info, q, s) * jnp.asarray(SCORE_SCALE, BF16)
            key = jnp.concatenate([k[t] for t in keys], axis=0)
            value = jnp.concatenate([v[t] for t in keys], axis=0)
            pair = []
            for h in range(2):
                own = jnp.where(head_lanes(h), query, jnp.zeros_like(query))
                scores = dot_nt(own, key) + bias_ref[rows, cols]
                top = jnp.max(scores, axis=-1, keepdims=True)
                exponent = jnp.exp(scores - top)
                total = jnp.sum(exponent, axis=-1, keepdims=True)
                probs = (exponent * (1.0 / total)).astype(BF16)
                p_ref[2 * pair_index + h, rows, cols] = probs
                pair.append(dot_nn(probs, value))
            mixes.append(jnp.where(head_lanes(0), pair[0], pair[1]).astype(BF16))
        top, bottom = mixes[0], mixes[-1]
        if full and not cross:
            top, bottom = top[:half], top[half:]
        if cross:
            outs[0][:, lanes] = top
            outs[1][:, lanes] = bottom
        else:
            outs[0][:half, lanes] = top
            outs[0][half:, lanes] = bottom
            if part_b:
                outs[1][:, lanes] = to_send(info, top, bottom)

    def run(full):
        blocks = attention_blocks(full, cross, half)

        @pl.when(pl.program_id(0) == 0)
        def _():
            for s, keys, rows, cols in blocks:
                at = rows if full else slice(0, half)
                kinds = (0, 1) if full else (2 + s, 2 + s)
                bias_ref[rows, cols] = clip_bias(info, group, at, slice(0, half * len(keys)), *kinds)

        for pair_index, lanes in pairs_of(outs[0]):
            run_pair(full, blocks, pair_index, lanes)

    pl.when(info[FULL] != 0)(lambda: run(True))
    pl.when(info[FULL] == 0)(lambda: run(False))


def attend_back_kernel(group, counts, info, *refs):
    cross = group in (CROSS_A, CROSS_B)
    part_b = group in (SELF_B, CROSS_B)
    operands, at = [], 0
    for n in counts:
        operands.append(refs[at : at + n])
        at += n
    p_ref, outs = refs[at], refs[at + 1 :]
    half = operands[0][0].shape[0]
    out_ref = outs[2] if cross else outs[0]

    def run_pair(full, blocks, pair_index, lanes):
        q, k, v, g = (load_halves(info, refs, len(refs) == 3, lanes) for refs in operands)
        queries, sums = [], {}
        head_rows = lax.broadcasted_iota(jnp.int32, (2 * HEAD_DIM, 1), 0) < HEAD_DIM
        for s, keys, rows, cols in blocks:
            query = query_half(info, q, s)
            grad = query_half(info, g, s)
            key = jnp.concatenate([k[t] for t in keys], axis=0)
            value = jnp.concatenate([v[t] for t in keys], axis=0)
            dq, dk, dv = [], [], []
            for h in range(2):
                own = jnp.where(head_lanes(h), grad, jnp.zeros_like(grad))
                probs = p_ref[2 * pair_index + h, rows, cols]
                wide_probs = probs.astype(F32)
                grad_probs = dot_nt(own, value)
                delta = jnp.sum(wide_probs * grad_probs, axis=-1, keepdims=True)
                grad_scores = (wide_probs * (grad_probs - delta)).astype(BF16)
                dq.append(dot_nn(grad_scores, key))
                dk.append(dot_tn(query, grad_scores))
                dv.append(dot_tn(grad, probs))
            queries.append((jnp.where(head_lanes(0), dq[0], dq[1]) * SCORE_SCALE).astype(BF16))
            both = tuple(jnp.concatenate([p[0][:HEAD_DIM], p[1][HEAD_DIM:]], axis=0).T for p in (dk, dv))
            sums[keys] = (sums[keys][0] + both[0], sums[keys][1] + both[1]) if keys in sums else both
        grads = []
        for t in range(2):
            dk, dv = (sums[(0, 1)] if full else sums[(t,)])
            rows = slice(t * half, (t + 1) * half) if full else slice(0, half)
            grads.append(((dk[rows] * SCORE_SCALE).astype(BF16), dv[rows].astype(BF16)))
        top, bottom = queries[0], queries[-1]
        if full and not cross:
            top, bottom = top[:half], top[half:]
        if cross:
            outs[0][:, lanes] = top
            outs[1][:, lanes] = bottom
        parts = [(g0, g1) for g0, g1 in zip(*grads)]
        if not cross:
            parts = [(top, bottom)] + parts
        for n, (first, second) in enumerate(parts):
            out_ref[n, :half, lanes] = first
            out_ref[n, half:, lanes] = second
            if part_b:
                outs[3 if cross else 1][n, :, lanes] = to_send(info, first, second)

    def run(full):
        blocks = attention_blocks(full, cross, half)
        for pair_index, lanes in pairs_of(out_ref):
            run_pair(full, blocks, pair_index, lanes)

    pl.when(info[FULL] != 0)(lambda: run(True))
    pl.when(info[FULL] == 0)(lambda: run(False))


def column_block(array, lead=None, row=0, column=0, rows=256):
    lanes = PAIRS * 2 * HEAD_DIM
    if array.ndim == 3:
        return (array, pl.BlockSpec((None, rows, lanes), lambda j, info: (lead, row, j + column)))
    return (array, pl.BlockSpec((rows, lanes), lambda j, info: (row, j + column)))


def halves_of(array, lead=None):
    return [column_block(array, lead, 0), column_block(array, lead, 1)]


def attend(info, group, operands, columns, rows=256):
    cross = group in (CROSS_A, CROSS_B)
    lanes = PAIRS * 2 * HEAD_DIM
    heads = columns // HEAD_DIM
    p_rows = rows if cross else 2 * rows
    half_out = ((rows, columns), BF16, pl.BlockSpec((rows, lanes), lambda j, info: (0, j)))
    mix_out = ((2 * rows, columns), BF16, pl.BlockSpec((2 * rows, lanes), lambda j, info: (0, j)))
    outs = [half_out, half_out] if cross else [mix_out] + ([half_out] if group == SELF_B else [])
    p_block = pl.BlockSpec((2 * PAIRS, p_rows, 2 * rows), lambda j, info: (j, 0, 0))
    p_out = ((heads, p_rows, 2 * rows), BF16, p_block, True)
    return call(
        functools.partial(attend_kernel, group, [len(o) for o in operands]),
        info,
        heads // (2 * PAIRS),
        sum(operands, []),
        outs + [p_out],
        [pltpu.VMEM((p_rows, 2 * rows), F32)],
        "attend",
        20,
        heads * 2 // 3,
    )


def attend_back(info, group, operands, probs, columns, rows=256):
    cross = group in (CROSS_A, CROSS_B)
    part_b = group in (SELF_B, CROSS_B)
    lanes = PAIRS * 2 * HEAD_DIM
    half_out = ((rows, columns), BF16, pl.BlockSpec((rows, lanes), lambda j, info: (0, j)))
    count = 2 if cross else 3

    def stacked(height):
        return ((count, height, columns), BF16, pl.BlockSpec((count, height, lanes), lambda j, info: (0, 0, j)))

    outs = [half_out, half_out] if cross else []
    outs = outs + [stacked(2 * rows)] + ([stacked(rows)] if part_b else [])
    p_block = pl.BlockSpec((2 * PAIRS,) + probs.shape[1:], lambda j, info: (j, 0, 0))
    return call(
        functools.partial(attend_back_kernel, group, [len(o) for o in operands]),
        info,
        probs.shape[0] // (2 * PAIRS),
        sum(operands, []) + [(probs, p_block)],
        outs,
        [],
        "attend_back",
        20,
        probs.shape[0],
    )


def first_project_kernel(info, a_ref, kept_ref, received_ref, norms_ref, w_ref, rows_ref, normed_ref, out_ref):
    @pl.when(pl.program_id(0) == 0)
    def _():
        rows = joined_rows(info, a_ref, kept_ref, received_ref)
        rows_ref[...] = rows
        normal, _ = norm_stats(rows.astype(F32))
        normed_ref[...] = (normal * norms_ref[0:1, :] + norms_ref[1:2, :]).astype(BF16)

    out_ref[...] = dot_nn(normed_ref[...], w_ref[...]).astype(BF16)


def first_project(info, tokens, received, norms, w_self):
    count, width, cols = w_self.shape
    rows = tokens.shape[1] + received.shape[0]
    return call(
        first_project_kernel,
        info,
        count,
        part_rows(tokens) + [whole_in(received), whole_in(norms), (w_self, lead_spec(width, cols))],
        [whole_out(rows, width, in_hbm=True), whole_out(rows, width, in_hbm=True)]
        + [((count, rows, cols), BF16, lead_spec(rows, cols))],
        [],
        "first_project",
        12,
        4,
    )


def other_project_kernel(info, normed_ref, own_b_ref, mine_ref, theirs_ref, out_ref, send_ref):
    weights = joined_pieces(info, mine_ref[...], theirs_ref[...], 0)
    out = dot_nn(normed_ref[...], weights).astype(BF16)
    out_ref[...] = out
    part_b = out.shape[0] - own_b_ref.shape[0]
    send_ref[...] = to_send(info, own_b_ref[...], out[part_b:])


def other_project(info, normed, qkv_own, mine, theirs, part_b):
    count, half, cols = mine.shape
    rows = normed.shape[0]
    own_b = pl.BlockSpec((None, part_b, cols), lambda j, info: (j, rows // part_b - 1, 0))
    return call(
        other_project_kernel,
        info,
        count,
        [whole_in(normed), (qkv_own, own_b), (mine, lead_spec(half, cols)), (theirs, lead_spec(half, cols))],
        [
            ((count, rows, cols), BF16, lead_spec(rows, cols)),
            ((count, part_b, cols), BF16, lead_spec(part_b, cols)),
        ],
        [],
        "other_project",
        9,
        3,
    )


def put_query_parts(info, value, far_ref, near_ref, left_ref, right_ref, send_ref):
    rows = left_ref.shape[0]
    cols = left_ref.shape[1]
    for h in range(2):
        at = slice(h * cols, (h + 1) * cols)
        far_ref[:, at] = value[h][:rows]
        near_ref[:, at] = value[h][rows : 2 * rows]
    left, right = value[0][2 * rows :], value[1][2 * rows :]
    left_ref[...] = left
    right_ref[...] = right
    send_ref[...] = to_send(info, left, right)


def query_outs(rows, width):
    whole, half = whole_out(rows, width, in_hbm=True), whole_out(rows, width // 2, in_hbm=True)
    return [whole, whole, half, half, half]


def self_mixes(info, mix0_ref, mix1_ref, slots_ref, received_ref):
    rows = received_ref.shape[0]
    parts = exchanged(info, TOP_BIG, slots_ref[:rows, :], slots_ref[rows:, :], received_ref[...])
    return [
        jnp.concatenate([ref[...], part], axis=0) for ref, part in zip((mix0_ref, mix1_ref), parts)
    ]


def second_project_kernel(
    info, rows_ref, norms_ref, mix0_ref, mix1_ref, slots_ref, received_ref, out_ref, query_ref, mine_ref, theirs_ref,
    hidden_ref, joined_ref, *query_refs,
):
    mixes = self_mixes(info, mix0_ref, mix1_ref, slots_ref, received_ref)
    other_out = joined_pieces(info, mine_ref[0], theirs_ref[0], 1)
    hidden = rows_ref[...].astype(F32) + dot_nn(mixes[0], out_ref[...]) + dot_nn(mixes[1], other_out)
    hidden_ref[...] = hidden
    normal, _ = norm_stats(hidden)
    joined = (normal * norms_ref[2:3, :] + norms_ref[3:4, :]).astype(BF16)
    joined_ref[...] = joined
    other_query = joined_pieces(info, mine_ref[1], theirs_ref[1], 0)
    queries = [dot_nn(joined, w).astype(BF16) for w in (query_ref[...], other_query)]
    put_query_parts(info, queries, *query_refs)


def second_project(info, rows, norms, mixes, w_self_out, w_query, mine, theirs, part_b):
    shape = rows.shape
    return call(
        second_project_kernel,
        info,
        1,
        [whole_in(a) for a in (rows, norms, *mixes, w_self_out, w_query, mine, theirs)],
        [whole_out(*shape, kind=F32, in_hbm=True), whole_out(*shape, in_hbm=True)] + query_outs(part_b, shape[1]),
        [],
        "second_project",
        17,
        5,
    )


def offer_project_kernel(info, rows_ref, own_ref, mine_ref, theirs_ref, out_ref, send_ref):
    cols = own_ref.shape[1]
    rows = send_ref.shape[0]
    other = joined_pieces(info, mine_ref[...], theirs_ref[...], 0)
    parts = [dot_nn(rows_ref[...], w).astype(BF16) for w in (own_ref[...], other)]
    for h in range(2):
        out_ref[:, h * cols : (h + 1) * cols] = parts[h]
    send_ref[...] = to_send(info, parts[0][-rows:], parts[1][-rows:])


def offer_project(info, joined, w_offer, mine, theirs, part_b):
    count, width, cols = w_offer.shape
    rows = joined.shape[0]
    piece = lead_spec(cols, cols)
    return call(
        offer_project_kernel,
        info,
        count,
        [whole_in(joined), (w_offer, lead_spec(width, cols)), (mine, piece), (theirs, piece)],
        [
            ((count, rows, 2 * cols), BF16, lead_spec(rows, 2 * cols)),
            ((count, part_b, cols), BF16, lead_spec(part_b, cols)),
        ],
        [],
        "offer_project",
        9,
        4,
    )


def reader_rows(info, far_ref, near_ref, far_b_ref, near_b_ref, received_ref):
    half = far_b_ref.shape[1]
    parts = exchanged(info, TOP_MID, far_b_ref[...], near_b_ref[...], received_ref[...])
    return [
        jnp.concatenate([ref[:, h * half : (h + 1) * half] for ref in (far_ref, near_ref)] + [parts[h]], axis=0)
        for h in range(2)
    ]


def mlp_kernel(
    info, hidden_ref, norms_ref, far_ref, near_ref, far_b_ref, near_b_ref, received_ref, w_cross_ref, mine_ref,
    theirs_ref, grad_a_ref, grad_kept_ref, grad_received_ref, up_ref, down_ref, result_ref, grad_second_ref, gm_far_ref, gm_near_ref, gm_left_ref, gm_right_ref,
    gm_send_ref, activated_ref, grad_up_ref, rows_ref, grad_ref, keep_ref, send_ref, g_norms_ref, second_ref,
    sum_ref, back_ref,
):
    step = pl.program_id(0)

    def mixes():
        return reader_rows(info, far_ref, near_ref, far_b_ref, near_b_ref, received_ref)

    def cross_weights():
        return w_cross_ref[...], joined_pieces(info, mine_ref[...], theirs_ref[...], 1)

    @pl.when(step == 0)
    def _():
        grad_ref[...] = joined_rows(info, grad_a_ref, grad_kept_ref, grad_received_ref)
        second = hidden_ref[...]
        for mix, weight in zip(mixes(), cross_weights()):
            second = second + dot_nn(mix, weight)
        second_ref[...] = second
        normal, _ = norm_stats(second)
        rows_ref[...] = (normal * norms_ref[4:5, :] + norms_ref[5:6, :]).astype(BF16)
        sum_ref[...] = second
        back_ref[...] = jnp.zeros_like(back_ref)

    rows, grad, up, down = rows_ref[...], grad_ref[...], up_ref[...], down_ref[...]
    pre = dot_nn(rows, up)
    spread = lax.erf(pre * 0.7071067811865476) * 0.5 + 0.5
    slope = spread + pre * (jnp.exp(pre * pre * -0.5) * 0.3989422804014327)
    activated = (pre * spread).astype(BF16)
    grad_up = (dot_nt(grad, down) * slope).astype(BF16)
    sum_ref[...] += dot_nn(activated, down)
    back_ref[...] += dot_nt(grad_up, up)
    activated_ref[...] = activated
    grad_up_ref[...] = grad_up

    @pl.when(step == 3)
    def _():
        result_ref[...] = sum_ref[...].astype(BF16)
        normal, inverse = norm_stats(second_ref[...])
        back, gain, shift = norm_back(back_ref[...], normal, inverse, norms_ref[4:5, :])
        g_norms_ref[0:1, :] = gain
        g_norms_ref[1:2, :] = shift
        grad_second = grad_ref[...].astype(F32) + back
        grad_second_ref[...] = grad_second
        rounded = grad_second.astype(BF16)
        parts = []
        for h, (mix, weight) in enumerate(zip(mixes(), cross_weights())):
            parts.append(dot_nt(rounded, weight).astype(BF16))
            put_pieces(info, keep_ref, send_ref, h, dot_tn(mix, rounded), 1)
        put_query_parts(info, parts, gm_far_ref, gm_near_ref, gm_left_ref, gm_right_ref, gm_send_ref)


def mlp(info, hidden, norms, mixes, w_cross, mine, theirs, cotangent, received, up, down):
    rows, width = hidden.shape
    half = width // 2
    part_b = received.shape[0]

    pieces = (up.shape[:1] + (rows, width), BF16, lead_spec(rows, width), True)
    wide = pltpu.VMEM((rows, width), F32)
    return call(
        mlp_kernel,
        info,
        4,
        [whole_in(from_hbm(a)) for a in (hidden, norms, *mixes, w_cross, mine, theirs)]
        + part_rows(cotangent)
        + [whole_in(from_hbm(received)), (up, lead_spec(width, width)), (down, lead_spec(width, width))],
        [whole_out(rows, width), whole_out(rows, width, kind=F32, in_hbm=True)]
        + query_outs(part_b, width)
        + [pieces, pieces, whole_out(rows, width, in_hbm=True), whole_out(rows, width, in_hbm=True)]
        + [whole_out(2, half, half, in_hbm=True), whole_out(2, half, half, in_hbm=True)]
        + [whole_out(2, width, kind=F32)],
        [wide, wide, wide],
        "mlp",
        46,
        34,
    )


def mlp_weights_kernel(info, rows_ref, grad_ref, activated_ref, grad_up_ref, *outs):
    g_up = dot_tn(rows_ref[...], grad_up_ref[...]).astype(BF16)
    g_down = dot_tn(activated_ref[...], grad_ref[...]).astype(BF16)
    first = pl.program_id(0) < 2
    for keep_ref, send_ref, value in ((outs[0], outs[1], g_up), (outs[2], outs[3], g_down)):

        @pl.when(first)
        def _(keep_ref=keep_ref, value=value):
            keep_ref[...] = value

        @pl.when(jnp.logical_not(first))
        def _(send_ref=send_ref, value=value):
            send_ref[...] = value


def mlp_weights(info, rows, grad, activated, grad_up):
    count, height, width = activated.shape

    def pieces(index):
        return ((2, width, width), BF16, pl.BlockSpec((None, width, width), lambda j, info: (index(j), 0, 0)))

    keep, send = pieces(lambda j: jnp.minimum(j, 1)), pieces(lambda j: jnp.maximum(j - 2, 0))
    piece = lead_spec(height, width)
    return call(
        mlp_weights_kernel,
        info,
        count,
        [whole_in(from_hbm(rows)), whole_in(from_hbm(grad)), (from_hbm(activated), piece), (from_hbm(grad_up), piece)],
        [keep, send, keep, send],
        [],
        "mlp_weights",
        24,
        10,
    )


def second_back_kernel(
    info, far_ref, near_ref, far_b_ref, near_b_ref, received_ref, dkv_ref, slots_ref, slots_received_ref, joined_ref,
    hidden_ref, grad_second_ref, norms_ref, offer_ref, offer_mine_ref, offer_theirs_ref, query_ref, out_ref, mine_ref,
    theirs_ref, mix0_ref, mix1_ref, mix_slots_ref, mix_received_ref, cross_keep_ref, cross_send_ref, grad_hidden_ref,
    grad_mix_ref, mix_send_ref, keep_ref, send_ref, g_norms_ref, back_ref,
):
    step = pl.program_id(0)
    half = query_ref.shape[1]
    rows = received_ref.shape[0]

    def add(at, grads, weights, first):
        joined = joined_ref[...]
        total = dot_nt(grads[0], weights[0]) + dot_nt(grads[1], weights[1])
        back_ref[...] = total if first else back_ref[...] + total
        for h in range(2):
            put_pieces(info, keep_ref, send_ref, (h, at), dot_tn(joined, grads[h]), 0)

    def add_offer(at):
        parts = exchanged(info, TOP_BIG, slots_ref[:rows, :], slots_ref[rows:, :], slots_received_ref[...])
        grads = [
            jnp.concatenate([dkv_ref[:, h * half : (h + 1) * half], parts[h]], axis=0) for h in range(2)
        ]
        other = joined_pieces(info, offer_mine_ref[...], offer_theirs_ref[...], 0)
        add(at, grads, (offer_ref[...], other), at == 0)

    pl.when(step == 0)(lambda: add_offer(0))
    pl.when(step == 1)(lambda: add_offer(1))

    @pl.when(step == 2)
    def _():
        for h in range(2):
            keep_ref[h, 4] = cross_keep_ref[h]
            send_ref[h, 4] = cross_send_ref[h]
        grads = reader_rows(info, far_ref, near_ref, far_b_ref, near_b_ref, received_ref)
        add(3, grads, (query_ref[...], joined_pieces(info, mine_ref[1], theirs_ref[1], 0)), False)
        normal, inverse = norm_stats(hidden_ref[...])
        back, gain, shift = norm_back(back_ref[...], normal, inverse, norms_ref[2:3, :])
        g_norms_ref[0:1, :] = gain
        g_norms_ref[1:2, :] = shift
        grad_hidden = grad_second_ref[...] + back
        grad_hidden_ref[...] = grad_hidden
        rounded = grad_hidden.astype(BF16)
        mixes = self_mixes(info, mix0_ref, mix1_ref, mix_slots_ref, mix_received_ref)
        parts = []
        for h, weight in enumerate((out_ref[...], joined_pieces(info, mine_ref[0], theirs_ref[0], 1))):
            part = dot_nt(rounded, weight).astype(BF16)
            grad_mix_ref[h] = part
            parts.append(part[-rows:])
            put_pieces(info, keep_ref, send_ref, (h, 2), dot_tn(mixes[h], rounded), 1)
        mix_send_ref[...] = to_send(info, *parts)


def second_back(
    info, grad_q, dkv, slots, slots_received, joined, hidden, grad_second, norms, w_offer, offer_mine, offer_theirs,
    w_query, w_self_out, mine, theirs, mixes, cross_keep, cross_send,
):
    rows, width = hidden.shape
    half = width // 2
    part_b = slots_received.shape[1]

    def offered(array, *shape):
        return (array, pl.BlockSpec((None,) + shape, lambda j, info: (jnp.minimum(j, 1), 0, 0)))

    return call(
        second_back_kernel,
        info,
        3,
        [whole_in(from_hbm(a)) for a in grad_q]
        + [offered(dkv, *dkv.shape[1:]), offered(slots, *slots.shape[1:])]
        + [offered(slots_received, *slots_received.shape[1:])]
        + [whole_in(a) for a in (joined, hidden, grad_second, norms)]
        + [offered(w_offer, width, half), offered(offer_mine, half, half), offered(offer_theirs, half, half)]
        + [whole_in(a) for a in (w_query, w_self_out, mine, theirs, *mixes, cross_keep, cross_send)],
        [whole_out(rows, width, kind=F32, in_hbm=True), whole_out(2, rows, half), whole_out(part_b, half)]
        + [whole_out(2, 5, half, half), whole_out(2, 5, half, half), whole_out(2, width, kind=F32)],
        [pltpu.VMEM((rows, width), F32)],
        "second_back",
        35,
        12,
    )


def first_grads(info, own_ref, other_ref, slots_ref, received_ref):
    rows = received_ref.shape[0]
    parts = exchanged(info, TOP_BIG, slots_ref[:rows, :], slots_ref[rows:, :], received_ref[...])
    return [jnp.concatenate([ref[...], part], axis=0) for ref, part in zip((own_ref, other_ref), parts)]


def first_weights_kernel(half, info, grad_ref, slots_ref, received_ref, normed_ref, keep_ref, send_ref):
    rows = received_ref.shape[0]
    parts = exchanged(info, TOP_BIG, slots_ref[:rows, :], slots_ref[rows:, :], received_ref[...])
    value = dot_tn(normed_ref[...], jnp.concatenate([grad_ref[...], parts[half]], axis=0))
    put_pieces(info, keep_ref, send_ref, slice(None), value, 0)


def first_ins(*arrays):
    return [(a, lead_spec(*a.shape[1:])) for a in arrays]


def first_weights(info, half_index, grads, slots, received, normed):
    half = grads.shape[2]
    piece = ((3, half, half), BF16, lead_spec(half, half))
    return call(
        functools.partial(first_weights_kernel, half_index),
        info,
        3,
        first_ins(grads, slots, received) + [whole_in(normed)],
        [piece, piece],
        [],
        "first_weights",
        12,
        3,
    )


def first_back_kernel(
    info, own_ref, other_ref, slots_ref, received_ref, rows_ref, grad_hidden_ref, norms_ref, w_own_ref, mine_ref,
    theirs_ref, grad_early_ref, grad_late_ref, g_norms_ref, back_ref,
):
    step = pl.program_id(0)
    grads = first_grads(info, own_ref, other_ref, slots_ref, received_ref)
    other = joined_pieces(info, mine_ref[...], theirs_ref[...], 0)
    total = dot_nt(grads[0], w_own_ref[...]) + dot_nt(grads[1], other)

    @pl.when(step == 0)
    def _():
        back_ref[...] = total

    @pl.when(step > 0)
    def _():
        back_ref[...] += total

    @pl.when(step == pl.num_programs(0) - 1)
    def _():
        normal, inverse = norm_stats(rows_ref[...].astype(F32))
        back, gain, shift = norm_back(back_ref[...], normal, inverse, norms_ref[0:1, :])
        g_norms_ref[0:1, :] = gain
        g_norms_ref[1:2, :] = shift
        grad_rows = (grad_hidden_ref[...] + back).astype(BF16)
        late = grad_late_ref.shape[0]
        grad_late_ref[...] = grad_rows[:late]
        grad_early_ref[...] = grad_rows[late:]


def first_back(info, own, other, slots, received, rows, grad_hidden, norms, w_self, mine, theirs):
    count = own.shape[0]
    width = rows.shape[1]
    late = received.shape[1]
    ins = first_ins(own, other, slots, received)
    ins += [whole_in(a) for a in (rows, grad_hidden, norms)]
    ins += [(a, lead_spec(*a.shape[1:])) for a in (w_self, mine, theirs)]
    return call(
        first_back_kernel,
        info,
        count,
        ins,
        [whole_out(2 * late, width), whole_out(late, width), whole_out(2, width, kind=F32)],
        [pltpu.VMEM(rows.shape, F32)],
        "first_back",
        24,
        8,
    )


def row_of(table, index):
    return lax.dynamic_index_in_dim(table, index, 0, keepdims=False)


def scalars(clip_len, index, across, quarter):
    core = index % 2
    is_big = index < 2 * quarter
    is_mid = jnp.logical_and(index >= 2 * quarter, index < 3 * quarter)
    first, last = core == 0, core == 1
    flags = [
        is_big,
        core,
        across,
        jnp.logical_and(is_big, index >= quarter),
        jnp.logical_and(is_big, last),
        jnp.logical_and(is_big, first),
        jnp.logical_and(is_mid, last),
        jnp.logical_and(is_mid, first),
    ]
    shared = index - core + across
    lens_a, lens_b = row_of(clip_len, across), clip_len[2]
    big_a = row_of(lens_a, jnp.minimum(index, 2 * quarter - 1))
    big_b = row_of(lens_b, jnp.minimum(shared, 2 * quarter - 1))
    sets_a = [row_of(lens_a, index % quarter + s * quarter) for s in range(2)]
    sets_b = [row_of(lens_b, shared % quarter + core * quarter)] * 2
    table = jnp.stack(
        [2 * big_a, 2 * big_a, *sets_a, 2 * big_b, 2 * big_b, *sets_b]
        + [big_a, 2 * big_a, *sets_a, big_b, 2 * big_b, *sets_b]
    )
    ends = [table[:, 0]]
    for k in range(1, 4):
        ends.append(ends[-1] + table[:, k])
    flags = jnp.stack([flag.astype(jnp.int32) for flag in flags])
    return jnp.concatenate([flags, jnp.stack(ends, axis=1).reshape(-1)])


def local(
    tokens,
    cotangent,
    clip_len,
    ln_params,
    w_self,
    w_self_out,
    w_offer,
    w_query,
    w_cross_out,
    w_up,
    w_down,
):
    index = lax.axis_index("clip")
    across = lax.axis_index("head")
    count = lax.axis_size("clip")
    quarter = count // 4
    levels = (2 * quarter).bit_length() - 1
    core = index % 2
    is_big = index < 2 * quarter
    is_mid = jnp.logical_and(index >= 2 * quarter, index < 3 * quarter)
    own_micro2 = core == across
    norms = ln_params[0]
    w_self, w_self_out, w_offer, w_query = w_self[0], w_self_out[0], w_offer[0], w_query[0]
    w_cross_out, w_up, w_down = w_cross_out[0], w_up[0], w_down[0]
    half = w_query.shape[1]
    part_a = tokens.shape[1]
    part_b = part_a // 2
    wide = 2 * half

    near = [(i, i - quarter) for i in range(2 * quarter, count)]
    far = [(i, i - 2 * quarter) for i in range(2 * quarter, 3 * quarter)]
    far += [(i, i - quarter) for i in range(3 * quarter, count)]

    def to_server(far_rows, near_rows):
        second = lax.ppermute(near_rows, "clip", near)
        return lax.ppermute(far_rows, "clip", far), second

    def to_reader(far_rows, near_rows):
        second = lax.ppermute(near_rows, "clip", [(b, a) for a, b in near])
        return lax.ppermute(far_rows, "clip", [(b, a) for a, b in far]), second

    def reader_slots(left, right, received):
        top = jnp.where(jnp.logical_and(is_mid, core == 1), received, left)
        return top, jnp.where(jnp.logical_and(is_mid, core == 0), received, right)

    def from_server(top, bottom):
        return top, bottom, other_core(jnp.where(core == 0, bottom, top))

    def over_level(part, bit):
        return over_bit(part, bit, 2 * quarter if bit == levels - 1 else None)

    def add(left, right):
        return (left.astype(F32) + right.astype(F32)).astype(BF16)

    def last_levels(total, received):
        total = total if received is None else add(total, received)
        for bit in range(3, levels):
            total = add(total, over_level(total, bit))
        return total

    def whole(mine, axis):
        return in_core_order(core, mine, other_core(mine), axis).astype(F32)[None]

    def all_rows(a_mine, b_mine, a_theirs, b_theirs):
        kept = jnp.where(own_micro2, b_mine, b_theirs)
        received = other_core(jnp.where(own_micro2, b_theirs, b_mine))
        micro2 = in_core_order(core, kept, received, 0)
        micro0 = jnp.where(across == 0, a_mine, a_theirs)
        micro1 = jnp.where(across == 0, a_theirs, a_mine)
        return jnp.stack([micro0, micro1, micro2])


    def over_head_rows(array, start, stop, *others):
        return over_head(after(array[start:stop], *others) if others else array[start:stop])

    def rows_piece(array, piece):
        return lax.dynamic_slice(array, (2, piece * part_b, 0), (1, part_b, wide))[0]

    self_mine = over_head(core_piece(w_self, core, 1))
    tokens_received = other_core(rows_piece(tokens, 1 - core))
    info = scalars(clip_len, index, across, quarter)
    rows, normed, qkv_own = first_project(info, tokens, tokens_received, norms, w_self)
    self_0 = [halves_of(qkv_own, n) for n in range(3)]
    mix_0, p_0 = attend(info, SELF_A, self_0, half)
    first_piece = jnp.stack([core_piece(w_self_out, core, 1), core_piece(w_query, core, 0)])
    offer_piece, up_piece, down_piece = core_piece(w_offer, core, 1), core_piece(w_up, core, 1), core_piece(w_down, core, 0)
    cross_piece = core_piece(w_cross_out, core, 1)
    (self_mine, mix_0, first_piece) = fence(self_mine, mix_0, first_piece)

    first_mine = over_head(first_piece)
    self_theirs = other_core(self_mine)
    qkv_other, qkv_send = other_project(info, normed, qkv_own, self_mine, self_theirs, part_b)
    self_1 = [halves_of(qkv_other, n) for n in range(3)]
    mix_1, p_1 = attend(info, SELF_A, self_1, half)
    qkv_received, first_mine, mix_1, offer_piece = fence(other_core(qkv_send), first_mine, mix_1, offer_piece)

    offer_mine = over_head(offer_piece[0])
    self_b = [
        [column_block(qkv_own, n, 2), column_block(qkv_other, n, 2), column_block(qkv_received, n)] for n in range(3)
    ]
    mix_s, mix_send, p_s = attend(info, SELF_B, self_b, half)
    first_theirs = other_core(first_mine)
    mix_s, mix_send, offer_mine, offer_piece = fence(mix_s, mix_send, offer_mine, offer_piece)

    offer_last = over_head(offer_piece[1])
    mixes = (mix_0, mix_1, mix_s, other_core(mix_send))
    hidden, joined, q_far, q_near, q_left, q_right, q_send = second_project(
        info, rows, norms, mixes, w_self_out, w_query, first_mine, first_theirs, part_b
    )
    q_far, q_near, q_left, q_right, q_send, joined, offer_mine, offer_last, cross_piece, up_piece, down_piece, cotangent = fence(
        q_far, q_near, q_left, q_right, q_send, joined, offer_mine, offer_last, cross_piece, up_piece, down_piece, cotangent
    )

    asked_a = to_server(q_far, q_near)
    up_mine = [over_head(up_piece[:576])]
    q_top, q_bottom = reader_slots(q_left, q_right, other_core(q_send))
    offer_mine = jnp.stack([offer_mine, offer_last])
    offer_theirs = other_core(offer_mine)
    offer, offer_send = offer_project(info, joined, w_offer, offer_mine, offer_theirs, part_b)
    cotangent_received = other_core(rows_piece(cotangent, 1 - core))
    offer_received = other_core(offer_send)
    *asked_a, q_top, q_bottom, offer, offer_received, cotangent_received, up_mine[0], up_piece, cross_piece = fence(
        *asked_a, q_top, q_bottom, offer, offer_received, cotangent_received, up_mine[0], up_piece, cross_piece
    )

    asked_b = to_server(q_top, q_bottom)
    up_mine.append(over_head(up_piece[576:]))
    cross_mine = over_head(cross_piece)
    cross_a = [[column_block(asked_a[0]), column_block(asked_a[1])]] + [halves_of(offer, n) for n in range(2)]
    far_a, near_a, cross_p_a = attend(info, CROSS_A, cross_a, wide)
    far_a, near_a, asked_b_far, asked_b_near, up_mine[1], cross_mine, down_piece = fence(
        far_a, near_a, *asked_b, up_mine[1], cross_mine, down_piece
    )

    back_a = to_reader(far_a, near_a)
    down_mine = [over_head(down_piece[:576])]
    cross_b = [[column_block(asked_b_far), column_block(asked_b_near)]] + [
        [
            column_block(offer, n, 2),
            column_block(offer, n, 2, half // (PAIRS * 2 * HEAD_DIM)),
            column_block(offer_received, n),
        ]
        for n in range(2)
    ]
    far_b, near_b, cross_p_b = attend(info, CROSS_B, cross_b, half)
    up_mine = jnp.concatenate(up_mine)
    up_theirs = other_core(up_mine)
    cross_theirs = other_core(cross_mine)
    *back_a, far_b, near_b, up_mine, up_theirs, cross_theirs, down_mine[0], down_piece = fence(
        *back_a, far_b, near_b, up_mine, up_theirs, cross_theirs, down_mine[0], down_piece
    )

    back_b = to_reader(far_b, near_b)
    down_mine = jnp.concatenate([down_mine[0], over_head(down_piece[576:])])
    up_pieces = jnp.stack([core_piece(w_up, core, 1), up_mine, core_piece(w_up, 1 - core, 1), up_theirs])
    *back_b, down_mine, up_pieces = fence(*back_b, down_mine, up_pieces)

    back_b = from_server(*back_b)
    down_theirs = other_core(down_mine)
    down_pieces = jnp.stack([core_piece(w_down, core, 0), down_mine, core_piece(w_down, 1 - core, 0), down_theirs])
    (
        result, grad_second, gm_far, gm_near, gm_left, gm_right, gm_send,
        activated, grad_up, mlp_rows, grad_out, cross_keep, cross_send, norms_3,
    ) = mlp(
        info, hidden, norms, (*back_a, *back_b), w_cross_out, cross_mine, cross_theirs, cotangent, cotangent_received,
        up_pieces, down_pieces,
    )
    result, gm_far, gm_near, gm_left, gm_right, gm_send, activated, grad_up, mlp_rows, grad_out = fence(
        result, gm_far, gm_near, gm_left, gm_right, gm_send, activated, grad_up, mlp_rows, grad_out
    )

    grad_a = to_server(gm_far, gm_near)
    layer_x = [over_head(result[:448])]
    gm_top, gm_bottom = reader_slots(gm_left, gm_right, other_core(gm_send))
    up_keep, up_send, down_keep, down_send = mlp_weights(info, mlp_rows, grad_out, activated, grad_up)
    *grad_a, gm_top, gm_bottom, layer_x[0], result, down_keep, down_send, up_keep, up_send = fence(
        *grad_a, gm_top, gm_bottom, layer_x[0], result, down_keep, down_send, up_keep, up_send
    )

    grad_b = to_server(gm_top, gm_bottom)
    layer_x.append(over_head(result[448:]))
    down_received = other_core(down_send)
    down_out = [add(down_keep[1, :576], down_received[1, :576]), add(down_keep[1, 576:], down_received[1, 576:])]
    grad_in = [column_block(grad_a[0]), column_block(grad_a[1])]
    dq_far, dq_near, dkv_a = attend_back(info, CROSS_A, cross_a + [grad_in], cross_p_a, wide)
    dq_far, dq_near, grad_b_far, grad_b_near, layer_x[1], *down_out, up_keep, up_send = fence(
        dq_far, dq_near, *grad_b, layer_x[1], *down_out, up_keep, up_send
    )

    dq_a = to_reader(dq_far, dq_near)
    down_x = [over_head(down_out[0])]
    grad_in = [column_block(grad_b_far), column_block(grad_b_near)]
    dq_b_far, dq_b_near, dkv_b, dkv_send = attend_back(info, CROSS_B, cross_b + [grad_in], cross_p_b, half)
    up_received = other_core(up_send)
    up_out = [add(up_keep[1, :192], up_received[1, :192]), add(up_keep[1, 192:], up_received[1, 192:])]
    down_out[1] = jnp.concatenate([down_out[1], up_out[0]])
    *dq_a, dq_b_far, dq_b_near, dkv_send, down_x[0], up_out[1], down_out[1] = fence(
        *dq_a, dq_b_far, dq_b_near, dkv_send, down_x[0], up_out[1], down_out[1]
    )

    dq_b = to_reader(dq_b_far, dq_b_near)
    both_x = over_head(down_out[1])
    down_own = add(down_keep[0, :576], down_received[0, :576])
    down_own = add(down_own, down_x[0])
    down_first, down_rest = down_own[:384], down_own[384:]
    down_y = [over_level(down_first, 1)]
    *dq_b, dkv_send, both_x, up_out[1], down_first, down_rest, down_y[0] = fence(
        *dq_b, dkv_send, both_x, up_out[1], down_first, down_rest, down_y[0]
    )

    dkv_received = other_core(dkv_send)
    down_x.append(both_x[:192])
    up_x = [both_x[192:], over_head(up_out[1])]
    down_second = add(add(down_keep[0, 576:], down_received[0, 576:]), down_x[1])
    down_second = jnp.concatenate([down_rest, down_second])
    down_y.append(over_level(down_second, 1))
    down_first = add(down_first, down_y[0])
    down_z = [over_level(down_first, 2)]
    grad_hidden, grad_mix, grad_send, mid_keep, mid_send, norms_2 = second_back(
        info, (*dq_a, *from_server(*dq_b)), dkv_a, dkv_b, dkv_received, joined, hidden, grad_second, norms, w_offer,
        offer_mine, offer_theirs, w_query, w_self_out, first_mine, first_theirs, mixes, cross_keep, cross_send,
    )
    up_own = add(up_keep[0], up_received[0])
    grad_hidden, grad_mix, grad_send, mid_keep, mid_send, up_x[1], up_own, down_second, down_y[1], down_first, down_z[0] = fence(
        grad_hidden, grad_mix, grad_send, mid_keep, mid_send, up_x[1], up_own, down_second, down_y[1], down_first, down_z[0]
    )

    (back_1,) = attend_back(info, SELF_A, self_1 + [halves_of(grad_mix, 1)], p_1, half)
    grad_received = other_core(grad_send)
    mid_received = other_core(mid_send)
    mid_out = [add(mid_keep[1, :3], mid_received[1, :3]), add(mid_keep[1, 3:], mid_received[1, 3:])]
    up_total = add(up_own, jnp.concatenate(up_x))
    up_y = [over_level(up_total[:384], 1)]
    down_second = add(down_second, down_y[1])
    down_z.append(over_level(down_second, 2))
    back_1, grad_mix, grad_received, mid_out[0], mid_out[1], up_total, up_y[0], down_second, down_z[1] = fence(
        back_1, grad_mix, grad_received, *mid_out, up_total, up_y[0], down_second, down_z[1]
    )

    mid_x = [over_head(mid_out[0])]
    up_y.append(over_level(up_total[384:], 1))
    up_first = add(up_total[:384], up_y[0])
    up_z = [over_level(up_first, 2)]
    grad_in = [column_block(grad_mix, 0, 2), column_block(grad_mix, 1, 2), column_block(grad_received)]
    back_s, back_send = attend_back(info, SELF_B, self_b + [grad_in], p_s, half)
    back_received = other_core(back_send)
    other_keep, other_send = first_weights(info, 1, back_1, back_s, back_received, normed)
    mid_own = add(mid_keep[0], mid_received[0])
    (
        back_s, back_received, other_keep, other_send, mid_x[0], mid_own, mid_out[1],
        up_total, up_y[1], up_first, up_z[0], grad_mix,
    ) = fence(
        back_s, back_received, other_keep, other_send, mid_x[0], mid_own, mid_out[1],
        up_total, up_y[1], up_first, up_z[0], grad_mix,
    )

    mid_x.append(over_head(mid_out[1]))
    mid_first = add(mid_own[:2], mid_x[0][:2])
    mid_y = [over_level(mid_first, 1)]
    up_second = add(up_total[384:], up_y[1])
    up_z.append(over_level(up_second, 2))
    (back_0,) = attend_back(info, SELF_A, self_0 + [halves_of(grad_mix, 0)], p_0, half)
    own_keep, own_send = first_weights(info, 0, back_0, back_s, back_received, normed)
    last_out = add(other_keep, other_core(other_send))
    down_total = jnp.concatenate([last_levels(down_first, down_z[0]), last_levels(down_second, down_z[1])])
    grad_down_weight = whole(down_total, 0)
    (
        back_0, own_keep, own_send, last_out, mid_x[1], mid_first, mid_y[0], up_second, up_z[1], mid_own,
        grad_down_weight,
    ) = fence(
        back_0, own_keep, own_send, last_out, mid_x[1], mid_first, mid_y[0], up_second, up_z[1], mid_own,
        grad_down_weight,
    )

    last_x = over_head(last_out)
    mid_second = add(mid_own[2:], jnp.concatenate([mid_x[0][2:], mid_x[1]]))
    mid_y.append(over_level(mid_second, 1))
    mid_first = add(mid_first, mid_y[0])
    mid_z = over_level(mid_first, 2)
    own_received = other_core(own_send)
    last_own = [add(own_keep[:2], own_received[:2]), add(own_keep[2:], own_received[2:])]
    grad_early, grad_late, norms_1 = first_back(
        info, back_0, back_1, back_s, back_received, rows, grad_hidden, norms, w_self, self_mine, self_theirs
    )
    up_total = jnp.concatenate([last_levels(up_first, up_z[0]), last_levels(up_second, up_z[1])])
    grad_up_weight = whole(up_total, 1)
    grad_early, grad_late, norms_1, last_own[0], last_own[1], last_x, mid_second, mid_y[1], mid_first, mid_z, grad_up_weight = fence(
        grad_early, grad_late, norms_1, *last_own, last_x, mid_second, mid_y[1], mid_first, mid_z, grad_up_weight
    )

    early_x = over_head(grad_early)
    first, second = add(last_own[0], last_x[:2]), add(last_own[1], last_x[2:])
    second = jnp.concatenate([second, add(mid_second[:1], mid_y[1][:1])])
    first_y, second_z = over_level(first, 1), over_level(second, 2)
    norm_grads = jnp.concatenate([norms_1, norms_2, norms_3], axis=0)
    norm_grads = norm_grads + other_core(norm_grads)
    norm_grads = norm_grads + over_level(norm_grads, 1)
    (
        early_x, grad_late, first, first_y, second, second_z, norm_grads, mid_first, mid_second
    ) = fence(
        early_x, grad_late, first, first_y, second, second_z, norm_grads, mid_first, mid_second
    )

    late_x = over_head(grad_late)
    first, second = add(first, first_y), add(second, second_z)
    first_z, second_y = over_level(first, 2), over_level(second[:1], 1)
    norm_grads = norm_grads + over_head(norm_grads)
    layer_x = after(jnp.concatenate(layer_x), first)
    layer_out = all_rows(result[:part_a], result[part_a:], layer_x[:part_a], layer_x[part_a:])
    mid_total = last_levels(mid_first, mid_z)
    out_total = last_levels(second[1:], None)
    rest_total = add(mid_second[1:], mid_y[1][1:])
    for bit in range(2, levels - 1):
        rest_total = add(rest_total, over_level(rest_total, bit))

    early = [layer_out, late_x, whole(out_total[0], 1), whole(mid_total, 1), whole(rest_total[0], 0)]
    early += [whole(rest_total[1], 1)]
    first, first_z, second, second_y, norm_grads, *early = fence(first, first_z, second, second_y, norm_grads, *early)
    layer_out, late_x, *grad_weights = early
    a_mine, a_theirs = (jnp.concatenate([x, y[:part_b]]) for x, y in ((grad_late, grad_early), (late_x, early_x)))
    grad_tokens = all_rows(a_mine, grad_early[part_b:], a_theirs, early_x[part_b:]).astype(F32)

    for bit in range(2, levels):
        norm_grads = norm_grads + over_level(norm_grads, bit)
    last_total = jnp.concatenate([last_levels(first, first_z), last_levels(second[:1], second_y)])
    return (layer_out, grad_tokens, norm_grads[None], whole(last_total, 1), *grad_weights, grad_up_weight, grad_down_weight)


def solution(mesh):
    return jax.shard_map(
        local,
        mesh=mesh,
        in_specs=(
            P(None, "clip", None),
            P(None, "clip", None),
            P(),
            P("clip", None, None),
            P("clip", None, None, "head"),
            P("clip", "head", None),
            P("clip", None, None, "head"),
            P("clip", None, "head"),
            P("clip", "head", None),
            P("clip", None, "head"),
            P("clip", "head", None),
        ),
        out_specs=(
            P(None, "clip", None),
            P(None, "clip", None),
            P("clip", None, None),
            P("clip", None, None, "head"),
            P("clip", "head", None),
            P("clip", None, None, "head"),
            P("clip", None, "head"),
            P("clip", "head", None),
            P("clip", None, "head"),
            P("clip", "head", None),
        ),
        check_vma=False,
    )
```
